1024 devices in a mesh: blk: 64 (over z, x), sub: 16 (over y, core).
Axes of the slice: x: 8, y: 8, z: 8, core: 2. Of those that a mesh axis runs over, the one named last changes fastest.
Arguments:
- pressure: float32 [1024, 512, 128], P('blk', 'sub'), may hold values from -6 to 6
- source: float32 [1024, 512, 128], P('blk', 'sub'), may hold values from -6 to 6
- inv_density: float32 [1024, 512, 128], P('blk', 'sub'), may hold values from 0.05 to 1
Outputs:
- corrected: float32 [1024, 512, 128], P('blk', 'sub')
The draws below stay inside these ranges and needn't reach their ends.
All inputs are finite; a program needn't handle non-finite values.
Results may differ from the reference program's by a relative error of at most 0.00002.
Values sent between devices are 32-bit elements; how exact they have to be, the bound alone decides.
A program may use at most 64 MiB of HBM per device.

```python
import math
import jax
import jax.numpy as jnp

PRE = 2
POST = 2
COARSE_SWEEPS = 6
NX = 1024
NY = 512
NZ = 128


def block_levels(rng, dims, pieces, low, high):
    def one(position, blocks):
        draws = jax.random.uniform(jax.random.fold_in(jax.random.fold_in(rng, 6), position), (blocks,), jnp.float32, low / len(pieces), high / len(pieces))
        return jnp.repeat(jnp.exp(draws), dims[position] // blocks).reshape((-1,) + (1,) * (len(dims) - position - 1))

    level = one(*pieces[0])
    for cut in pieces[1:]:
        level = level * one(*cut)
    return level


def noise(own_key, shape, spread, limit, split=(), held_as=jnp.bfloat16):
    result = jax.random.normal(own_key, shape, jnp.float32) * spread
    if len(split) > 0:
        result = block_levels(own_key, shape, split, -0.22, 0.18) * result
    return jnp.clip(result, min=-limit, max=limit).astype(held_as)


def setup_inputs(seed: int = 0) -> dict:
    keys = jax.random.split(jax.random.key(seed), 4)
    pressure = noise(keys[0], (NX, NY, NZ), 1.0, 6.0, ((0, 64), (1, 16)), jnp.float32)
    source = noise(keys[1], (NX, NY, NZ), 1.0, 6.0, ((0, 64), (1, 16)), jnp.float32)
    inv_density = jnp.clip(jnp.exp(math.log(1.0) - 2.9957323 * jax.random.uniform(keys[2], (NX, NY, NZ), jnp.float32) ** block_levels(keys[2], (NX, NY, NZ), ((0, 64), (1, 16)), -0.2, 0.2)), 0.05, 1.0)
    return {"pressure": pressure, "source": source, "inv_density": inv_density}


WEIGHT = 0.8


def shift_down(value):
    return jnp.pad(value[:, :, :-1], ((0, 0), (0, 0), (1, 0)))


def shift_up(value):
    return jnp.pad(value[:, :, 1:], ((0, 0), (0, 0), (0, 1)))


def pad_plane(value):
    return jnp.pad(value, ((1, 1), (1, 1), (0, 0)))


def face_coefs(padded):
    center = padded[1:-1, 1:-1]
    return (0.5 * (center + padded[:-2, 1:-1]), 0.5 * (center + padded[2:, 1:-1]),
            0.5 * (center + padded[1:-1, :-2]), 0.5 * (center + padded[1:-1, 2:]),
            0.5 * (center + shift_down(center)), 0.5 * (center + shift_up(center)))


def apply_operator(padded, coefs, scale):
    center = padded[1:-1, 1:-1]
    total = coefs[0] * (center - padded[:-2, 1:-1]) + coefs[1] * (center - padded[2:, 1:-1])
    total = total + coefs[2] * (center - padded[1:-1, :-2]) + coefs[3] * (center - padded[1:-1, 2:])
    total = total + coefs[4] * (center - shift_down(center)) + coefs[5] * (center - shift_up(center))
    return scale * total


def inverse_diagonal(coefs, scale):
    total = coefs[0] + coefs[1] + coefs[2] + coefs[3] + coefs[4] + coefs[5]
    return WEIGHT / (scale * total)


def mean_yz(value):
    ext_x, ext_y, ext_z = value.shape
    return value.reshape(ext_x, ext_y // 2, 2, ext_z // 2, 2).mean(axis=(2, 4))


def mean_xz(value):
    ext_x, ext_y, ext_z = value.shape
    return value.reshape(ext_x // 2, 2, ext_y, ext_z // 2, 2).mean(axis=(1, 4))


def mean_xy(value):
    ext_x, ext_y, ext_z = value.shape
    return value.reshape(ext_x // 2, 2, ext_y // 2, 2, ext_z).mean(axis=(1, 3))


def coarsen_faces(coefs):
    return (mean_yz(coefs[0][0::2]), mean_yz(coefs[1][1::2]),
            mean_xz(coefs[2][:, 0::2]), mean_xz(coefs[3][:, 1::2]),
            mean_xy(coefs[4][:, :, 0::2]), mean_xy(coefs[5][:, :, 1::2]))


def coarsen_cells(value):
    ext_x, ext_y, ext_z = value.shape
    return value.reshape(ext_x // 2, 2, ext_y // 2, 2, ext_z // 2, 2).mean(axis=(1, 3, 5))


def refine_cells(value):
    return jnp.repeat(jnp.repeat(jnp.repeat(value, 2, axis=0), 2, axis=1), 2, axis=2)


def sweep(field, rhs_level, coefs, invd, scale):
    return field + invd * (rhs_level - apply_operator(pad_plane(field), coefs, scale))


def reference(pressure, source, inv_density):
    coefs0 = face_coefs(pad_plane(inv_density))
    invd0 = inverse_diagonal(coefs0, 1.0)
    coefs1 = coarsen_faces(coefs0)
    invd1 = inverse_diagonal(coefs1, 0.25)
    coefs2 = coarsen_faces(coefs1)
    invd2 = inverse_diagonal(coefs2, 0.0625)
    field = pressure
    for sweep_index in range(PRE):
        field = sweep(field, source, coefs0, invd0, 1.0)
    res0 = source - apply_operator(pad_plane(field), coefs0, 1.0)
    rhs_one = coarsen_cells(res0)
    err_one = invd1 * rhs_one
    for sweep_index in range(PRE - 1):
        err_one = sweep(err_one, rhs_one, coefs1, invd1, 0.25)
    res1 = rhs_one - apply_operator(pad_plane(err_one), coefs1, 0.25)
    rhs_two = coarsen_cells(res1)
    err_two = invd2 * rhs_two
    for sweep_index in range(COARSE_SWEEPS):
        err_two = sweep(err_two, rhs_two, coefs2, invd2, 0.0625)
    err_one = err_one + refine_cells(err_two)
    for sweep_index in range(POST):
        err_one = sweep(err_one, rhs_one, coefs1, invd1, 0.25)
    field = field + refine_cells(err_one)
    for sweep_index in range(POST):
        field = sweep(field, source, coefs0, invd0, 1.0)
    return field
```

```python
import functools

import jax
import jax.numpy as jnp
from jax import lax
from jax.experimental import pallas as pl
from jax.experimental.pallas import tpu as pltpu
from jax.sharding import PartitionSpec as P

MESH = pl.DeviceIdType.MESH
PRE = 2
POST = 2
COARSE_SWEEPS = 6
WEIGHT = 0.8
KEEP = 1.0 - WEIGHT

DIRS = [(dx, dy) for dx in (-1, 0, 1) for dy in (-1, 0, 1) if (dx, dy) != (0, 0)]
FAR = [(dx, dy) for dx in (-2, -1, 0, 1, 2) for dy in (-1, 0, 1) if (dx, dy) != (0, 0)]


def send_range(step, first, count, width):
    if step == 0:
        return pl.ds(first, count)
    return pl.ds(first + count - width, width) if step > 0 else pl.ds(first, width)


def planes_to(step, first, count, width):
    if step == 0:
        return pl.ds(first, count)
    return pl.ds(first - width, width) if step > 0 else pl.ds(first + count, width)


def rows_to(step, count, width):
    if step == 0:
        return pl.ds(0, count)
    return pl.ds(count + width, width) if step > 0 else pl.ds(count, width)


def lanes(shape):
    return lax.broadcasted_iota(jnp.int32, shape, len(shape) - 1)


def roll_z(value, shift):
    return pltpu.roll(value, shift % 128, value.ndim - 1)


def roll_y(value, shift):
    return pltpu.roll(value, shift % value.shape[-2], value.ndim - 2)


def pack_pairs(value):
    split = value.reshape((value.shape[0] // 2, 2) + value.shape[1:])
    even, odd = split[:, 0], split[:, 1]
    mask = lanes(even.shape) % 2 == 0
    return jnp.where(mask, even + roll_z(even, -1), odd + roll_z(odd, 1))


def pack_groups(value):
    lane = lanes(value.shape[1:])
    low = jnp.where(lane % 2 == 0, value[0] + roll_z(value[0], -1), value[1] + roll_z(value[1], 1))
    high = jnp.where(lane % 2 == 0, value[2] + roll_z(value[2], -1), value[3] + roll_z(value[3], 1))
    return jnp.where(lane % 4 < 2, low + roll_z(low, -2), high + roll_z(high, 2))


def spread_pairs(value):
    mask = lanes(value.shape) % 2 == 0
    return jnp.where(mask, value, roll_z(value, 1)), jnp.where(mask, roll_z(value, -1), value)


def spread_groups(value):
    mask = lanes(value.shape) % 4 < 2
    low = jnp.where(mask, value, roll_z(value, 2))
    high = jnp.where(mask, roll_z(value, -2), value)
    return spread_pairs(low) + spread_pairs(high)


def ahead(value):
    return jnp.concatenate([value[1:], value[:1]], axis=0)


def behind(value):
    return jnp.concatenate([value[-1:], value[:-1]], axis=0)


def x_up(value, following, group):
    mask = lanes(value.shape) % group < group - 1
    return jnp.where(mask, roll_z(value, -1), roll_z(following, group - 1))


def x_down(value, previous, group):
    mask = lanes(value.shape) % group > 0
    return jnp.where(mask, roll_z(value, 1), roll_z(previous, 1 - group))


def coarse_weights(w, faces, inv, group, scale):
    half = scale * inv
    w[0] = half * faces[0]
    w[1] = half * x_up(faces[0], ahead(faces[0]), group)
    w[2] = half * faces[1]
    w[3] = half * roll_y(faces[1], -1)
    w[4] = half * faces[2]
    w[5] = half * roll_z(faces[2], -group)


def coarse_sum(w, value, group):
    total = w[0] * x_down(value, behind(value), group) + w[1] * x_up(value, ahead(value), group)
    total = total + w[2] * roll_y(value, 1) + w[3] * roll_y(value, -1)
    return total + w[4] * roll_z(value, group) + w[5] * roll_z(value, -group)


def kernel(
    sizes, p_hbm, s_hbm, d_hbm, o_hbm,
    p, d, s, v1, v2, fh, out, w0, g0, dg0,
    xs, ys, cs, l1, w1, b1, dg1, c2, w2, b2, e1, e0,
    local_sem, d_sem, p_sem, s_sem, f_sem, l1_sem, b1_sem, c2_sem, b2_sem,
):
    n_blk, n_sub = sizes
    ib, iy = lax.axis_index("blk"), lax.axis_index("sub")

    def peer(dx, dy):
        return {"blk": lax.rem(ib + (dx + n_blk), n_blk), "sub": lax.rem(iy + (dy + n_sub), n_sub)}

    def remote(src, dst, sem, k, dx, dy):
        return pltpu.make_async_remote_copy(
            src_ref=src, dst_ref=dst, send_sem=sem.at[0, k], recv_sem=sem.at[1, k],
            device_id=peer(dx, dy), device_id_type=MESH,
        )

    local = [
        pltpu.make_async_copy(src, dst.at[pl.ds(3, 16), pl.ds(0, 32)], local_sem.at[k])
        for k, (src, dst) in enumerate(((d_hbm, d), (p_hbm, p), (s_hbm, s)))
    ]
    for copy in local:
        copy.start()
    barrier = pltpu.get_barrier_semaphore()
    for dx, dy in FAR:
        pl.semaphore_signal(barrier, inc=1, device_id=peer(dx, dy), device_id_type=MESH)
    for copy in local:
        copy.wait()
    pl.semaphore_wait(barrier, len(FAR))

    def fine_copies(src, dst, sem, width):
        return [
            remote(
                src.at[send_range(dx, 3, 16, width), send_range(dy, 0, 32, 4)],
                dst.at[planes_to(dx, 3, 16, width), rows_to(dy, 32, 4)],
                sem, k, dx, dy,
            )
            for k, (dx, dy) in enumerate(DIRS)
        ]

    d_copies = fine_copies(d, d, d_sem, 3)
    p_copies = fine_copies(p, p, p_sem, 3)
    s_copies = fine_copies(s, s, s_sem, 2)
    for copy in d_copies + p_copies + s_copies:
        copy.start()

    def clear_fine(ref):
        zero = jnp.zeros((3, 40, 128), jnp.float32)
        strip = jnp.zeros((22, 4, 128), jnp.float32)

        @pl.when(ib == 0)
        def _():
            ref[0:3] = zero

        @pl.when(ib == n_blk - 1)
        def _():
            ref[19:22] = zero

        @pl.when(iy == 0)
        def _():
            ref[:, 36:40] = strip

        @pl.when(iy == n_sub - 1)
        def _():
            ref[:, 32:36] = strip

    for copy in d_copies:
        copy.wait_recv()
    clear_fine(d)

    def x_face(i, _):
        xs[i] = d[2 * i + 2, 0:32] + d[2 * i + 3, 0:32]
        return 0

    lax.fori_loop(0, 10, x_face, 0, unroll=True)

    def x_pair(i, _):
        both = d[2 * i + 3] + d[2 * i + 4]
        ys[i, 0:8] = both[32:40]
        ys[i, 8:48] = both
        return 0

    lax.fori_loop(0, 8, x_pair, 0, unroll=True)

    lane1 = lanes((4, 16, 128))
    faces_x = 0.125 * pack_pairs(xs[:, pl.ds(0, 16, stride=2), :] + xs[:, pl.ds(1, 16, stride=2), :])
    lx = faces_x[0:4]
    ux = x_up(lx, faces_x[1:5], 2)
    odd_before = ys[:, pl.ds(7, 16, stride=2), :]
    even = ys[:, pl.ds(8, 16, stride=2), :]
    odd = ys[:, pl.ds(9, 16, stride=2), :]
    even_after = ys[:, pl.ds(10, 16, stride=2), :]
    ly = 0.125 * pack_pairs(even + odd_before)
    uy = 0.125 * pack_pairs(odd + even_after)
    both = (even + odd).reshape(4, 2, 16, 128)
    b_even, b_odd = both[:, 0], both[:, 1]
    first, last = lane1 < 2, lane1 >= 126
    zero1 = jnp.zeros((4, 16, 128), jnp.float32)
    is_even = lane1 % 2 == 0
    lz = 0.125 * (
        jnp.where(is_even, b_even, roll_z(b_odd, 1))
        + jnp.where(first, zero1, jnp.where(is_even, roll_z(b_even, 1), roll_z(b_odd, 2)))
    )
    uz = 0.125 * (
        jnp.where(is_even, roll_z(b_even, -1), b_odd)
        + jnp.where(last, zero1, jnp.where(is_even, roll_z(b_even, -2), roll_z(b_odd, -1)))
    )
    diag1 = 0.25 * (lx + ux + ly + uy + lz + uz)
    dg1[...] = diag1 * (1.0 / WEIGHT)
    l1[0, 2:6, 0:16] = lx
    l1[1, 2:6, 0:16] = ly
    l1[2, 2:6, 0:16] = jnp.where(first, zero1, lz)
    l1[3, 2:6, 0:16] = WEIGHT / diag1

    l1_copies = [
        remote(
            l1.at[:, send_range(dx, 2, 4, 2), send_range(dy, 0, 16, 4)],
            l1.at[:, planes_to(dx, 2, 4, 2), rows_to(dy, 16, 4)],
            l1_sem, k, dx, dy,
        )
        for k, (dx, dy) in enumerate(DIRS)
    ]
    for copy in l1_copies:
        copy.start()

    for k, face in enumerate((lx, ux, ly, uy, lz, uz)):
        cs[k] = face

    def rows_of(k, parity):
        return cs[k, :, pl.ds(parity, 8, stride=2), :]

    lane2 = lanes((4, 8, 128))
    zero2 = jnp.zeros((4, 8, 128), jnp.float32)
    lx2 = jnp.where(lane2 % 2 == 0, rows_of(0, 0) + rows_of(0, 1), zero2)
    ux2 = jnp.where(lane2 % 2 == 1, rows_of(1, 0) + rows_of(1, 1), zero2)
    ly2 = rows_of(2, 0)
    uy2 = rows_of(3, 1)
    lz2 = jnp.where(lane2 % 4 < 2, rows_of(4, 0) + rows_of(4, 1), zero2)
    uz2 = jnp.where(lane2 % 4 >= 2, rows_of(5, 0) + rows_of(5, 1), zero2)
    diag2 = (0.0625 * 0.25) * pack_groups(lx2 + ux2 + ly2 + uy2 + lz2 + uz2)
    c2[0, 2, 8:16] = 0.25 * pack_groups(lx2)
    c2[1, 2, 8:16] = 0.25 * pack_groups(ly2)
    c2[2, 2, 8:16] = jnp.where(lanes((8, 128)) < 4, 0.0, 0.25 * pack_groups(lz2))
    c2[3, 2, 8:16] = WEIGHT / diag2

    c2_copies = [
        remote(
            c2.at[:, 2, pl.ds(8, 8)], c2.at[:, 2 - dx, pl.ds(8 - 8 * dy, 8)], c2_sem, k, dx, dy
        )
        for k, (dx, dy) in enumerate(FAR)
    ]
    for copy in c2_copies:
        copy.start()

    lane0 = lanes((40, 128))
    zero0 = jnp.zeros((40, 128), jnp.float32)

    def fine_weights(i, carry):
        below, here = carry
        above = d[i + 1]
        row_below, row_above = roll_y(here, 1), roll_y(here, -1)
        z_below = jnp.where(lane0 > 0, roll_z(here, 1), zero0)
        z_above = jnp.where(lane0 < 127, roll_z(here, -1), zero0)
        near = (below + above) + (row_below + row_above) + (z_below + z_above)
        diag = 3.0 * here + 0.5 * near
        inv = jnp.where(here > 0.0, WEIGHT / diag, zero0)
        half = 0.5 * inv
        w0[0, i] = half * (here + below)
        w0[1, i] = half * (here + above)
        w0[2, i] = half * (here + row_below)
        w0[3, i] = half * (here + row_above)
        w0[4, i] = jnp.where(lane0 > 0, half * (here + z_below), zero0)
        w0[5, i] = jnp.where(lane0 < 127, half * (here + z_above), zero0)
        g0[i] = inv
        dg0[i] = diag * (1.0 / WEIGHT)
        return here, above

    lax.fori_loop(1, 21, fine_weights, (d[0], d[1]), unroll=True)

    for copy in p_copies + s_copies:
        copy.wait_recv()
    clear_fine(p)

    def scale_source(i, _):
        g0[i] = g0[i] * s[i]
        return 0

    lax.fori_loop(1, 21, scale_source, 0, unroll=True)

    def fine_sum(i, below, here, above):
        total = g0[i] + w0[0, i] * below + w0[1, i] * above
        total = total + w0[2, i] * roll_y(here, 1) + w0[3, i] * roll_y(here, -1)
        return total + w0[4, i] * roll_z(here, 1) + w0[5, i] * roll_z(here, -1)

    def fine_sweep(src, dst, low, high):
        def plane(i, carry):
            below, here = carry
            above = src[i + 1]
            dst[i] = fine_sum(i, below, here, above) + KEEP * here
            return here, above

        lax.fori_loop(low, high, plane, (src[low - 1], src[low]), unroll=True)

    fine_sweep(p, v1, 1, 21)
    fine_sweep(v1, v2, 2, 20)

    def residual(pair, carry):
        below, here = carry
        above = v2[2 * pair + 4]
        beyond = v2[2 * pair + 5]
        first_half = (fine_sum(2 * pair + 3, below, here, above) - WEIGHT * here) * dg0[2 * pair + 3]
        second_half = (fine_sum(2 * pair + 4, here, above, beyond) - WEIGHT * above) * dg0[2 * pair + 4]
        xs[pair] = (first_half + second_half)[0:32]
        return above, beyond

    lax.fori_loop(0, 8, residual, (v2[2], v2[3]), unroll=True)
    b1[2:6, 0:16] = 0.125 * pack_pairs(
        xs[0:8, pl.ds(0, 16, stride=2), :] + xs[0:8, pl.ds(1, 16, stride=2), :]
    )
    b1_copies = [
        remote(
            b1.at[send_range(dx, 2, 4, 2), send_range(dy, 0, 16, 4)],
            b1.at[planes_to(dx, 2, 4, 2), rows_to(dy, 16, 4)],
            b1_sem, k, dx, dy,
        )
        for k, (dx, dy) in enumerate(DIRS)
    ]
    f_copies = fine_copies(v2, fh, f_sem, 2)
    for copy in b1_copies + f_copies:
        copy.start()

    for copy in l1_copies:
        copy.wait_recv()
    pairs = jnp.zeros((2, 24, 128), jnp.float32)
    strip1 = jnp.zeros((8, 4, 128), jnp.float32)

    @pl.when(ib == 0)
    def _():
        l1[3, 0:2] = pairs

    @pl.when(ib == n_blk - 1)
    def _():
        l1[3, 6:8] = pairs

    @pl.when(iy == 0)
    def _():
        l1[3, :, 20:24] = strip1

    @pl.when(iy == n_sub - 1)
    def _():
        l1[3, :, 16:20] = strip1

    inv1 = l1[3]
    coarse_weights(w1, l1, inv1, 2, 0.25)

    for copy in c2_copies:
        copy.wait_recv()
    group = jnp.zeros((24, 128), jnp.float32)
    strip2 = jnp.zeros((5, 8, 128), jnp.float32)

    for index in range(5):
        @pl.when((ib + (index - 2) < 0) | (ib + (index - 2) >= n_blk))
        def _():
            c2[3, index] = group

    @pl.when(iy == 0)
    def _():
        c2[3, :, 0:8] = strip2

    @pl.when(iy == n_sub - 1)
    def _():
        c2[3, :, 16:24] = strip2

    inv2 = c2[3]
    coarse_weights(w2, c2, inv2, 4, 0.0625)

    for copy in b1_copies:
        copy.wait_recv()
    g1 = l1[3] * b1[...]
    err1 = g1
    err1 = g1 + coarse_sum(w1, err1, 2) + KEEP * err1
    res1 = (g1 + coarse_sum(w1, err1, 2) - WEIGHT * err1)[2:6, 0:16] * dg1[...]
    xs[0:4, 0:16] = res1
    b2[2, 8:16] = 0.125 * pack_groups(
        xs[0:4, pl.ds(0, 8, stride=2), :] + xs[0:4, pl.ds(1, 8, stride=2), :]
    )
    b2_copies = [
        remote(b2.at[2, pl.ds(8, 8)], b2.at[2 - dx, pl.ds(8 - 8 * dy, 8)], b2_sem, k, dx, dy)
        for k, (dx, dy) in enumerate(FAR)
    ]
    for copy in b2_copies:
        copy.start()
    for copy in b2_copies:
        copy.wait_recv()
    g2 = c2[3] * b2[...]
    err2 = g2
    for _ in range(COARSE_SWEEPS):
        err2 = g2 + coarse_sum(w2, err2, 4) + KEEP * err2

    row = lax.broadcasted_iota(jnp.int32, (8, 128), 0)

    def put(pair, value):
        centre = value[8:16]
        sides = jnp.where(row < 2, value[16:24], roll_y(value[0:8], 4))
        for parity in range(2):
            e1[pair, pl.ds(parity, 8, stride=2), :] = centre
            e1[pair, pl.ds(16 + parity, 8, stride=2), :] = sides

    before, centre, after = spread_groups(err2[1]), spread_groups(err2[2]), spread_groups(err2[3])
    for pair, value in enumerate(before[2:4] + centre + after[0:2]):
        put(pair, value)
    g1 = l1[3] * b1[...]
    err1 = err1 + e1[:, 0:24]
    for _ in range(POST):
        err1 = g1 + coarse_sum(w1, err1, 2) + KEEP * err1

    def put_fine(index, value):
        sides = jnp.where(row < 2, value[16:24], roll_y(value[16:24], 4))
        for parity in range(2):
            e0[index, pl.ds(parity, 16, stride=2), :] = value[0:16]
            e0[index, pl.ds(32 + parity, 8, stride=2), :] = sides

    for pair in range(1, 7):
        even_cell, odd_cell = spread_pairs(err1[pair])
        if pair > 1:
            put_fine(2 * pair - 3, even_cell)
        if pair < 6:
            put_fine(2 * pair - 2, odd_cell)

    for copy in f_copies:
        copy.wait_recv()
    clear_fine(fh)

    def correct(i, _):
        halves = (2 * i + 1, 2 * i + 2)
        add = e0[i]
        for plane in halves:
            v1[plane, 0:32] = v2[plane, 0:32] + add[0:32]
            v1[plane, 32:40] = fh[plane, 32:40] + add[32:40]
        return 0

    for i in (0, 9):
        for plane in (2 * i + 1, 2 * i + 2):
            v1[plane] = fh[plane] + e0[i, 0:40]
    lax.fori_loop(1, 9, correct, 0, unroll=True)

    fine_sweep(v1, fh, 2, 20)

    def last_sweep(i, carry):
        below, here = carry
        above = fh[i + 1]
        out[i - 3] = (fine_sum(i, below, here, above) + KEEP * here)[0:32]
        return here, above

    lax.fori_loop(3, 19, last_sweep, (fh[2], fh[3]), unroll=True)
    store = pltpu.make_async_copy(out, o_hbm, local_sem.at[3])
    store.start()
    for copy in d_copies + p_copies + s_copies + l1_copies + c2_copies + f_copies + b1_copies + b2_copies:
        copy.wait_send()
    store.wait()


def solution(mesh):
    sizes = (mesh.shape["blk"], mesh.shape["sub"])

    def on_device(pressure, source, inv_density):
        def vmem(*shape):
            return pltpu.VMEM(shape, jnp.float32)

        near, far = len(DIRS), len(FAR)
        return pl.pallas_call(
            functools.partial(kernel, sizes),
            out_shape=jax.ShapeDtypeStruct((16, 32, 128), jnp.float32),
            in_specs=[pl.BlockSpec(memory_space=pl.ANY)] * 3,
            out_specs=pl.BlockSpec(memory_space=pl.ANY),
            scratch_shapes=[
                vmem(22, 40, 128), vmem(22, 40, 128), vmem(22, 40, 128),
                vmem(22, 40, 128), vmem(22, 40, 128), vmem(22, 40, 128),
                vmem(16, 32, 128), vmem(6, 22, 40, 128), vmem(22, 40, 128), vmem(22, 40, 128),
                vmem(10, 32, 128), vmem(8, 48, 128), vmem(6, 4, 16, 128),
                vmem(4, 8, 24, 128), vmem(6, 8, 24, 128), vmem(8, 24, 128), vmem(4, 16, 128),
                vmem(4, 5, 24, 128), vmem(6, 5, 24, 128), vmem(5, 24, 128),
                vmem(8, 32, 128), vmem(10, 48, 128),
                pltpu.SemaphoreType.DMA((4,)),
                pltpu.SemaphoreType.DMA((2, near)), pltpu.SemaphoreType.DMA((2, near)),
                pltpu.SemaphoreType.DMA((2, near)), pltpu.SemaphoreType.DMA((2, near)),
                pltpu.SemaphoreType.DMA((2, near)), pltpu.SemaphoreType.DMA((2, near)),
                pltpu.SemaphoreType.DMA((2, far)), pltpu.SemaphoreType.DMA((2, far)),
            ],
            compiler_params=pltpu.CompilerParams(
                collective_id=0, has_side_effects=True, vmem_limit_bytes=32 * 1024 * 1024
            ),
        )(pressure, source, inv_density)

    return jax.shard_map(
        on_device,
        mesh=mesh,
        in_specs=(P("blk", "sub", None),) * 3,
        out_specs=P("blk", "sub", None),
        check_vma=False,
    )
```

```python
import functools

import jax
import jax.numpy as jnp
from jax import lax
from jax.experimental import pallas as pl
from jax.experimental.pallas import tpu as pltpu
from jax.sharding import PartitionSpec as P

MESH = pl.DeviceIdType.MESH
PRE = 2
POST = 2
COARSE_SWEEPS = 6
WEIGHT = 0.8
KEEP = 1.0 - WEIGHT

DIRS = [(-1, -1), (1, 1), (-1, 1), (1, -1), (-1, 0), (1, 0), (0, -1), (0, 1)]
FAR = [(-2, -1), (2, 1), (-2, 1), (2, -1), (-2, 0), (2, 0)] + DIRS


def send_range(step, first, count, width):
    if step == 0:
        return pl.ds(first, count)
    return pl.ds(first + count - width, width) if step > 0 else pl.ds(first, width)


def planes_to(step, first, count, width):
    if step == 0:
        return pl.ds(first, count)
    return pl.ds(first - width, width) if step > 0 else pl.ds(first + count, width)


def rows_to(step, count, width):
    if step == 0:
        return pl.ds(0, count)
    return pl.ds(count + width, width) if step > 0 else pl.ds(count, width)


def far_rows(dx, dy, shift):
    if abs(dx) + abs(dy) == 3:
        return pl.ds(8 + shift + (4 if dy > 0 else 0), 4)
    return pl.ds(8 + shift, 8)


def lanes(shape):
    return lax.broadcasted_iota(jnp.int32, shape, len(shape) - 1)


def roll_z(value, shift):
    return pltpu.roll(value, shift % 128, value.ndim - 1)


def roll_y(value, shift):
    return pltpu.roll(value, shift % value.shape[-2], value.ndim - 2)


def pack_pairs(value):
    split = value.reshape((value.shape[0] // 2, 2) + value.shape[1:])
    even, odd = split[:, 0], split[:, 1]
    mask = lanes(even.shape) % 2 == 0
    return jnp.where(mask, even + roll_z(even, -1), odd + roll_z(odd, 1))


def pack_groups(value):
    lane = lanes(value.shape[1:])
    low = jnp.where(lane % 2 == 0, value[0] + roll_z(value[0], -1), value[1] + roll_z(value[1], 1))
    high = jnp.where(lane % 2 == 0, value[2] + roll_z(value[2], -1), value[3] + roll_z(value[3], 1))
    return jnp.where(lane % 4 < 2, low + roll_z(low, -2), high + roll_z(high, 2))


def spread_pairs(value):
    mask = lanes(value.shape) % 2 == 0
    return jnp.where(mask, value, roll_z(value, 1)), jnp.where(mask, roll_z(value, -1), value)


def spread_groups(value):
    mask = lanes(value.shape) % 4 < 2
    low = jnp.where(mask, value, roll_z(value, 2))
    high = jnp.where(mask, roll_z(value, -2), value)
    return spread_pairs(low) + spread_pairs(high)


def ahead(value):
    return jnp.concatenate([value[1:], value[:1]], axis=0)


def behind(value):
    return jnp.concatenate([value[-1:], value[:-1]], axis=0)


def x_up(value, following, group):
    mask = lanes(value.shape) % group < group - 1
    return jnp.where(mask, roll_z(value, -1), roll_z(following, group - 1))


def x_down(value, previous, group):
    mask = lanes(value.shape) % group > 0
    return jnp.where(mask, roll_z(value, 1), roll_z(previous, 1 - group))


def coarse_weights(w, faces, inv, group, scale):
    half = scale * inv
    w[0] = half * faces[0]
    w[1] = half * x_up(faces[0], ahead(faces[0]), group)
    w[2] = half * faces[1]
    w[3] = half * roll_y(faces[1], -1)
    w[4] = half * faces[2]
    w[5] = half * roll_z(faces[2], -group)


def coarse_sum(w, value, group):
    total = w[0] * x_down(value, behind(value), group) + w[1] * x_up(value, ahead(value), group)
    total = total + w[2] * roll_y(value, 1) + w[3] * roll_y(value, -1)
    return total + w[4] * roll_z(value, group) + w[5] * roll_z(value, -group)


def kernel(
    sizes, p_hbm, s_hbm, d_hbm, o_hbm,
    p, d, s, v1, v2, fh, out, w0, g0, dg0,
    xs, ys, cs, l1, w1, b1, dg1, c2, w2, b2, e1, e0,
    local_sem, d_sem, p_sem, s_sem, f_sem, l1_sem, b1_sem, c2_sem, b2_sem,
):
    n_blk, n_sub = sizes
    ib, iy = lax.axis_index("blk"), lax.axis_index("sub")

    def peer(dx, dy):
        return {"blk": lax.rem(ib + (dx + n_blk), n_blk), "sub": lax.rem(iy + (dy + n_sub), n_sub)}

    def remote(src, dst, sem, k, dx, dy):
        return pltpu.make_async_remote_copy(
            src_ref=src, dst_ref=dst, send_sem=sem.at[0, k], recv_sem=sem.at[1, k],
            device_id=peer(dx, dy), device_id_type=MESH,
        )

    local = [
        pltpu.make_async_copy(src, dst.at[pl.ds(3, 16), pl.ds(0, 32)], local_sem.at[k])
        for k, (src, dst) in enumerate(((d_hbm, d), (p_hbm, p), (s_hbm, s)))
    ]
    for copy in local:
        copy.start()
    barrier = pltpu.get_barrier_semaphore()
    for dx, dy in DIRS:
        pl.semaphore_signal(barrier, inc=1, device_id=peer(dx, dy), device_id_type=MESH)
    for copy in local:
        copy.wait()
    pl.semaphore_wait(barrier, len(DIRS))

    def fine_copies(src, dst, sem, width):
        return [
            remote(
                src.at[send_range(dx, 3, 16, width - abs(dy)), send_range(dy, 0, 32, 4)],
                dst.at[planes_to(dx, 3, 16, width - abs(dy)), rows_to(dy, 32, 4)],
                sem, k, dx, dy,
            )
            for k, (dx, dy) in enumerate(DIRS)
        ]

    d_copies = fine_copies(d, d, d_sem, 3)
    p_copies = fine_copies(p, p, p_sem, 3)
    s_copies = fine_copies(s, s, s_sem, 2)
    for copy in d_copies + p_copies + s_copies:
        copy.start()

    def clear_fine(ref):
        zero = jnp.zeros((3, 40, 128), jnp.float32)
        strip = jnp.zeros((22, 4, 128), jnp.float32)

        @pl.when(ib == 0)
        def _():
            ref[0:3] = zero

        @pl.when(ib == n_blk - 1)
        def _():
            ref[19:22] = zero

        @pl.when(iy == 0)
        def _():
            ref[:, 36:40] = strip

        @pl.when(iy == n_sub - 1)
        def _():
            ref[:, 32:36] = strip

    for copy in d_copies:
        copy.wait_recv()
    clear_fine(d)

    def x_face(i, _):
        xs[i] = d[2 * i + 2, 0:32] + d[2 * i + 3, 0:32]
        return 0

    lax.fori_loop(0, 10, x_face, 0, unroll=True)

    def x_pair(i, _):
        both = d[2 * i + 3] + d[2 * i + 4]
        ys[i, 0:8] = both[32:40]
        ys[i, 8:48] = both
        return 0

    lax.fori_loop(0, 8, x_pair, 0, unroll=True)

    lane1 = lanes((4, 16, 128))
    faces_x = 0.125 * pack_pairs(xs[:, pl.ds(0, 16, stride=2), :] + xs[:, pl.ds(1, 16, stride=2), :])
    lx = faces_x[0:4]
    ux = x_up(lx, faces_x[1:5], 2)
    odd_before = ys[:, pl.ds(7, 16, stride=2), :]
    even = ys[:, pl.ds(8, 16, stride=2), :]
    odd = ys[:, pl.ds(9, 16, stride=2), :]
    even_after = ys[:, pl.ds(10, 16, stride=2), :]
    ly = 0.125 * pack_pairs(even + odd_before)
    uy = 0.125 * pack_pairs(odd + even_after)
    both = (even + odd).reshape(4, 2, 16, 128)
    b_even, b_odd = both[:, 0], both[:, 1]
    first, last = lane1 < 2, lane1 >= 126
    zero1 = jnp.zeros((4, 16, 128), jnp.float32)
    is_even = lane1 % 2 == 0
    lz = 0.125 * (
        jnp.where(is_even, b_even, roll_z(b_odd, 1))
        + jnp.where(first, zero1, jnp.where(is_even, roll_z(b_even, 1), roll_z(b_odd, 2)))
    )
    uz = 0.125 * (
        jnp.where(is_even, roll_z(b_even, -1), b_odd)
        + jnp.where(last, zero1, jnp.where(is_even, roll_z(b_even, -2), roll_z(b_odd, -1)))
    )
    diag1 = 0.25 * (lx + ux + ly + uy + lz + uz)
    dg1[...] = diag1 * (1.0 / WEIGHT)
    l1[0, 2:6, 0:16] = lx
    l1[1, 2:6, 0:16] = ly
    l1[2, 2:6, 0:16] = jnp.where(first, zero1, lz)
    l1[3, 2:6, 0:16] = WEIGHT / diag1

    l1_copies = [
        remote(
            l1.at[:, send_range(dx, 2, 4, 2), send_range(dy, 0, 16, 4)],
            l1.at[:, planes_to(dx, 2, 4, 2), rows_to(dy, 16, 4)],
            l1_sem, k, dx, dy,
        )
        for k, (dx, dy) in enumerate(DIRS)
    ]
    for copy in l1_copies:
        copy.start()

    for k, face in enumerate((lx, ux, ly, uy, lz, uz)):
        cs[k] = face

    def rows_of(k, parity):
        return cs[k, :, pl.ds(parity, 8, stride=2), :]

    lane2 = lanes((4, 8, 128))
    zero2 = jnp.zeros((4, 8, 128), jnp.float32)
    lx2 = jnp.where(lane2 % 2 == 0, rows_of(0, 0) + rows_of(0, 1), zero2)
    ux2 = jnp.where(lane2 % 2 == 1, rows_of(1, 0) + rows_of(1, 1), zero2)
    ly2 = rows_of(2, 0)
    uy2 = rows_of(3, 1)
    lz2 = jnp.where(lane2 % 4 < 2, rows_of(4, 0) + rows_of(4, 1), zero2)
    uz2 = jnp.where(lane2 % 4 >= 2, rows_of(5, 0) + rows_of(5, 1), zero2)
    diag2 = (0.0625 * 0.25) * pack_groups(lx2 + ux2 + ly2 + uy2 + lz2 + uz2)
    c2[0, 2, 8:16] = 0.25 * pack_groups(lx2)
    c2[1, 2, 8:16] = 0.25 * pack_groups(ly2)
    c2[2, 2, 8:16] = jnp.where(lanes((8, 128)) < 4, 0.0, 0.25 * pack_groups(lz2))
    c2[3, 2, 8:16] = WEIGHT / diag2

    c2_copies = [
        remote(
            c2.at[:, 2, far_rows(dx, dy, 0)], c2.at[:, 2 - dx, far_rows(dx, dy, -8 * dy)],
            c2_sem, k, dx, dy,
        )
        for k, (dx, dy) in enumerate(FAR)
    ]
    lane0 = lanes((40, 128))
    zero0 = jnp.zeros((40, 128), jnp.float32)

    def fine_weights(i, carry):
        below, here = carry
        above = d[i + 1]
        row_below, row_above = roll_y(here, 1), roll_y(here, -1)
        z_below = jnp.where(lane0 > 0, roll_z(here, 1), zero0)
        z_above = jnp.where(lane0 < 127, roll_z(here, -1), zero0)
        near = (below + above) + (row_below + row_above) + (z_below + z_above)
        diag = 3.0 * here + 0.5 * near
        inv = jnp.where(here > 0.0, WEIGHT / diag, zero0)
        half = 0.5 * inv
        w0[0, i] = half * (here + below)
        w0[1, i] = half * (here + above)
        w0[2, i] = half * (here + row_below)
        w0[3, i] = half * (here + row_above)
        w0[4, i] = jnp.where(lane0 > 0, half * (here + z_below), zero0)
        w0[5, i] = jnp.where(lane0 < 127, half * (here + z_above), zero0)
        g0[i] = inv
        dg0[i] = diag * (1.0 / WEIGHT)
        return here, above

    lax.fori_loop(1, 21, fine_weights, (d[0], d[1]), unroll=True)

    for copy in p_copies + s_copies:
        copy.wait_recv()
    clear_fine(p)

    def scale_source(i, _):
        g0[i] = g0[i] * s[i]
        return 0

    lax.fori_loop(1, 21, scale_source, 0, unroll=True)

    def fine_sum(i, below, here, above):
        total = g0[i] + w0[0, i] * below + w0[1, i] * above
        total = total + w0[2, i] * roll_y(here, 1) + w0[3, i] * roll_y(here, -1)
        return total + w0[4, i] * roll_z(here, 1) + w0[5, i] * roll_z(here, -1)

    def fine_sweep(src, dst, low, high):
        def plane(i, carry):
            below, here = carry
            above = src[i + 1]
            dst[i] = fine_sum(i, below, here, above) + KEEP * here
            return here, above

        lax.fori_loop(low, high, plane, (src[low - 1], src[low]), unroll=True)

    fine_sweep(p, v1, 1, 21)
    fine_sweep(v1, v2, 2, 20)

    def residual(pair, carry):
        below, here = carry
        above = v2[2 * pair + 4]
        beyond = v2[2 * pair + 5]
        first_half = (fine_sum(2 * pair + 3, below, here, above) - WEIGHT * here) * dg0[2 * pair + 3]
        second_half = (fine_sum(2 * pair + 4, here, above, beyond) - WEIGHT * above) * dg0[2 * pair + 4]
        xs[pair] = (first_half + second_half)[0:32]
        return above, beyond

    lax.fori_loop(0, 8, residual, (v2[2], v2[3]), unroll=True)
    b1[2:6, 0:16] = 0.125 * pack_pairs(
        xs[0:8, pl.ds(0, 16, stride=2), :] + xs[0:8, pl.ds(1, 16, stride=2), :]
    )
    b1_copies = [
        remote(
            b1.at[send_range(dx, 2, 4, 2), send_range(dy, 0, 16, 4)],
            b1.at[planes_to(dx, 2, 4, 2), rows_to(dy, 16, 4)],
            b1_sem, k, dx, dy,
        )
        for k, (dx, dy) in enumerate(DIRS)
    ]
    f_copies = fine_copies(v2, fh, f_sem, 2)
    for copy in b1_copies + c2_copies:
        copy.start()

    for copy in l1_copies:
        copy.wait_recv()
    pairs = jnp.zeros((2, 24, 128), jnp.float32)
    strip1 = jnp.zeros((8, 4, 128), jnp.float32)

    @pl.when(ib == 0)
    def _():
        l1[3, 0:2] = pairs

    @pl.when(ib == n_blk - 1)
    def _():
        l1[3, 6:8] = pairs

    @pl.when(iy == 0)
    def _():
        l1[3, :, 20:24] = strip1

    @pl.when(iy == n_sub - 1)
    def _():
        l1[3, :, 16:20] = strip1

    inv1 = l1[3]
    coarse_weights(w1, l1, inv1, 2, 0.25)

    for copy in b1_copies:
        copy.wait_recv()
    g1 = l1[3] * b1[...]
    err1 = g1
    err1 = g1 + coarse_sum(w1, err1, 2) + KEEP * err1
    res1 = (g1 + coarse_sum(w1, err1, 2) - WEIGHT * err1)[2:6, 0:16] * dg1[...]
    xs[0:4, 0:16] = res1
    b2[2, 8:16] = 0.125 * pack_groups(
        xs[0:4, pl.ds(0, 8, stride=2), :] + xs[0:4, pl.ds(1, 8, stride=2), :]
    )
    b2_copies = [
        remote(
            b2.at[2, far_rows(dx, dy, 0)], b2.at[2 - dx, far_rows(dx, dy, -8 * dy)],
            b2_sem, k, dx, dy,
        )
        for k, (dx, dy) in enumerate(FAR)
    ]
    for copy in b2_copies + f_copies:
        copy.start()
    for copy in c2_copies:
        copy.wait_recv()
    group = jnp.zeros((24, 128), jnp.float32)
    strip2 = jnp.zeros((5, 8, 128), jnp.float32)

    for index in range(5):
        @pl.when((ib + (index - 2) < 0) | (ib + (index - 2) >= n_blk))
        def _():
            c2[3, index] = group

    @pl.when(iy == 0)
    def _():
        c2[3, :, 0:8] = strip2

    @pl.when(iy == n_sub - 1)
    def _():
        c2[3, :, 16:24] = strip2

    inv2 = c2[3]
    coarse_weights(w2, c2, inv2, 4, 0.0625)

    for copy in b2_copies:
        copy.wait_recv()
    g2 = c2[3] * b2[...]
    err2 = g2
    for _ in range(COARSE_SWEEPS):
        err2 = g2 + coarse_sum(w2, err2, 4) + KEEP * err2

    row = lax.broadcasted_iota(jnp.int32, (8, 128), 0)

    def put(pair, value):
        centre = value[8:16]
        sides = jnp.where(row < 2, value[16:24], roll_y(value[0:8], 4))
        for parity in range(2):
            e1[pair, pl.ds(parity, 8, stride=2), :] = centre
            e1[pair, pl.ds(16 + parity, 8, stride=2), :] = sides

    before, centre, after = spread_groups(err2[1]), spread_groups(err2[2]), spread_groups(err2[3])
    for pair, value in enumerate(before[2:4] + centre + after[0:2]):
        put(pair, value)
    g1 = l1[3] * b1[...]
    err1 = err1 + e1[:, 0:24]
    for _ in range(POST):
        err1 = g1 + coarse_sum(w1, err1, 2) + KEEP * err1

    def put_fine(index, value):
        sides = jnp.where(row < 2, value[16:24], roll_y(value[16:24], 4))
        for parity in range(2):
            e0[index, pl.ds(parity, 16, stride=2), :] = value[0:16]
            e0[index, pl.ds(32 + parity, 8, stride=2), :] = sides

    for pair in range(1, 7):
        even_cell, odd_cell = spread_pairs(err1[pair])
        if pair > 1:
            put_fine(2 * pair - 3, even_cell)
        if pair < 6:
            put_fine(2 * pair - 2, odd_cell)

    for copy in f_copies:
        copy.wait_recv()
    clear_fine(fh)

    def correct(i, _):
        halves = (2 * i + 1, 2 * i + 2)
        add = e0[i]
        for plane in halves:
            v1[plane, 0:32] = v2[plane, 0:32] + add[0:32]
            v1[plane, 32:40] = fh[plane, 32:40] + add[32:40]
        return 0

    for i in (0, 9):
        for plane in (2 * i + 1, 2 * i + 2):
            v1[plane] = fh[plane] + e0[i, 0:40]
    lax.fori_loop(1, 9, correct, 0, unroll=True)

    fine_sweep(v1, fh, 2, 20)

    def last_sweep(i, carry):
        below, here = carry
        above = fh[i + 1]
        out[i - 3] = (fine_sum(i, below, here, above) + KEEP * here)[0:32]
        return here, above

    carry = (fh[2], fh[3])
    stores = []
    for k in range(4):
        carry = lax.fori_loop(4 * k + 3, 4 * k + 7, last_sweep, carry, unroll=True)
        part = pl.ds(4 * k, 4)
        stores.append(pltpu.make_async_copy(out.at[part], o_hbm.at[part], local_sem.at[3 + k]))
        stores[-1].start()
    for copy in d_copies + p_copies + s_copies + l1_copies + c2_copies + f_copies + b1_copies + b2_copies:
        copy.wait_send()
    for store in stores:
        store.wait()


def solution(mesh):
    sizes = (mesh.shape["blk"], mesh.shape["sub"])

    def on_device(pressure, source, inv_density):
        def vmem(*shape):
            return pltpu.VMEM(shape, jnp.float32)

        near, far = len(DIRS), len(FAR)
        return pl.pallas_call(
            functools.partial(kernel, sizes),
            out_shape=jax.ShapeDtypeStruct((16, 32, 128), jnp.float32),
            in_specs=[pl.BlockSpec(memory_space=pltpu.HBM)] * 3,
            out_specs=pl.BlockSpec(memory_space=pl.ANY),
            scratch_shapes=[
                vmem(22, 40, 128), vmem(22, 40, 128), vmem(22, 40, 128),
                vmem(22, 40, 128), vmem(22, 40, 128), vmem(22, 40, 128),
                vmem(16, 32, 128), vmem(6, 22, 40, 128), vmem(22, 40, 128), vmem(22, 40, 128),
                vmem(10, 32, 128), vmem(8, 48, 128), vmem(6, 4, 16, 128),
                vmem(4, 8, 24, 128), vmem(6, 8, 24, 128), vmem(8, 24, 128), vmem(4, 16, 128),
                vmem(4, 5, 24, 128), vmem(6, 5, 24, 128), vmem(5, 24, 128),
                vmem(8, 32, 128), vmem(10, 48, 128),
                pltpu.SemaphoreType.DMA((7,)),
                pltpu.SemaphoreType.DMA((2, near)), pltpu.SemaphoreType.DMA((2, near)),
                pltpu.SemaphoreType.DMA((2, near)), pltpu.SemaphoreType.DMA((2, near)),
                pltpu.SemaphoreType.DMA((2, near)), pltpu.SemaphoreType.DMA((2, near)),
                pltpu.SemaphoreType.DMA((2, far)), pltpu.SemaphoreType.DMA((2, far)),
            ],
            compiler_params=pltpu.CompilerParams(
                collective_id=0, has_side_effects=True, vmem_limit_bytes=54850 * 1024
            ),
        )(pressure, source, inv_density)

    return jax.shard_map(
        on_device,
        mesh=mesh,
        in_specs=(P("blk", "sub", None),) * 3,
        out_specs=P("blk", "sub", None),
        check_vma=False,
    )
```

```python
import functools

import jax
import jax.numpy as jnp
from jax import lax
from jax.experimental import pallas as pl
from jax.experimental.pallas import tpu as pltpu
from jax.sharding import PartitionSpec as P

MESH = pl.DeviceIdType.MESH
PRE = 2
POST = 2
COARSE_SWEEPS = 6
WEIGHT = 0.8
KEEP = 1.0 - WEIGHT

DIRS = [(-1, -1), (1, 1), (-1, 1), (1, -1), (-1, 0), (1, 0), (0, -1), (0, 1)]
FAR = [(-2, -1), (2, 1), (-2, 1), (2, -1), (-2, 0), (2, 0)] + DIRS


def send_range(step, first, count, width):
    if step == 0:
        return pl.ds(first, count)
    return pl.ds(first + count - width, width) if step > 0 else pl.ds(first, width)


def planes_to(step, first, count, width):
    if step == 0:
        return pl.ds(first, count)
    return pl.ds(first - width, width) if step > 0 else pl.ds(first + count, width)


def rows_to(step, count, width):
    if step == 0:
        return pl.ds(0, count)
    return pl.ds(count + width, width) if step > 0 else pl.ds(count, width)


def far_rows(dx, dy, shift):
    if abs(dx) + abs(dy) == 3:
        return pl.ds(8 + shift + (4 if dy > 0 else 0), 4)
    return pl.ds(8 + shift, 8)


def lanes(shape):
    return lax.broadcasted_iota(jnp.int32, shape, len(shape) - 1)


def roll_z(value, shift):
    return pltpu.roll(value, shift % 128, value.ndim - 1)


def roll_y(value, shift):
    return pltpu.roll(value, shift % value.shape[-2], value.ndim - 2)


def pack_pairs(value):
    split = value.reshape((value.shape[0] // 2, 2) + value.shape[1:])
    even, odd = split[:, 0], split[:, 1]
    mask = lanes(even.shape) % 2 == 0
    return jnp.where(mask, even + roll_z(even, -1), odd + roll_z(odd, 1))


def pack_groups(value):
    lane = lanes(value.shape[1:])
    low = jnp.where(lane % 2 == 0, value[0] + roll_z(value[0], -1), value[1] + roll_z(value[1], 1))
    high = jnp.where(lane % 2 == 0, value[2] + roll_z(value[2], -1), value[3] + roll_z(value[3], 1))
    return jnp.where(lane % 4 < 2, low + roll_z(low, -2), high + roll_z(high, 2))


def spread_pairs(value):
    mask = lanes(value.shape) % 2 == 0
    return jnp.where(mask, value, roll_z(value, 1)), jnp.where(mask, roll_z(value, -1), value)


def spread_groups(value):
    mask = lanes(value.shape) % 4 < 2
    low = jnp.where(mask, value, roll_z(value, 2))
    high = jnp.where(mask, roll_z(value, -2), value)
    return spread_pairs(low) + spread_pairs(high)


def ahead(value):
    return jnp.concatenate([value[1:], value[:1]], axis=0)


def behind(value):
    return jnp.concatenate([value[-1:], value[:-1]], axis=0)


def x_up(value, following, group):
    mask = lanes(value.shape) % group < group - 1
    return jnp.where(mask, roll_z(value, -1), roll_z(following, group - 1))


def x_down(value, previous, group):
    mask = lanes(value.shape) % group > 0
    return jnp.where(mask, roll_z(value, 1), roll_z(previous, 1 - group))


def coarse_weights(w, faces, inv, group, scale):
    half = scale * inv
    w[0] = half * faces[0]
    w[1] = half * x_up(faces[0], ahead(faces[0]), group)
    w[2] = half * faces[1]
    w[3] = half * roll_y(faces[1], -1)
    w[4] = half * faces[2]
    w[5] = half * roll_z(faces[2], -group)


def coarse_sum(w, value, group):
    total = w[0] * x_down(value, behind(value), group) + w[1] * x_up(value, ahead(value), group)
    total = total + w[2] * roll_y(value, 1) + w[3] * roll_y(value, -1)
    return total + w[4] * roll_z(value, group) + w[5] * roll_z(value, -group)


class Halo:
    def __init__(self, copy, sends, receives):
        self.copy, self.sends, self.receives = copy, sends, receives

    def start(self):
        pl.when(self.sends)(self.copy.start)

    def wait_send(self):
        pl.when(self.sends)(self.copy.wait_send)

    def wait_recv(self):
        pl.when(self.receives)(self.copy.wait_recv)


def kernel(
    sizes, p_hbm, s_hbm, d_hbm, o_hbm,
    p, d, s, v1, v2, fh, out, w0, g0, dg0,
    xs, ys, cs, l1, w1, b1, dg1, c2, w2, b2, e1, e0,
    local_sem, d_sem, p_sem, s_sem, f_sem, l1_sem, b1_sem, c2_sem, b2_sem,
):
    n_blk, n_sub = sizes
    ib, iy = lax.axis_index("blk"), lax.axis_index("sub")

    def peer(dx, dy):
        return {"blk": ib + dx, "sub": iy + dy}

    def there(dx, dy):
        known = []
        if dx:
            known.append(ib >= -dx if dx < 0 else ib < n_blk - dx)
        if dy:
            known.append(iy >= -dy if dy < 0 else iy < n_sub - dy)
        return functools.reduce(jnp.logical_and, known)

    def remote(src, dst, sem, k, dx, dy):
        return Halo(
            pltpu.make_async_remote_copy(
                src_ref=src, dst_ref=dst, send_sem=sem.at[0, k], recv_sem=sem.at[1, k],
                device_id=peer(dx, dy), device_id_type=MESH,
            ),
            there(dx, dy),
            there(-dx, -dy),
        )

    def clear_outside(ref, lead, x_side, x_count, rows, low_rows, high_rows):
        planes = x_count + 2 * x_side
        slab = jnp.zeros(lead + (x_side, rows, 128), jnp.float32)
        strip = jnp.zeros(lead + (planes, low_rows[1], 128), jnp.float32)
        every = (slice(None),) * len(lead)

        @pl.when(ib == 0)
        def _():
            ref[every + (slice(0, x_side),)] = slab

        @pl.when(ib == n_blk - 1)
        def _():
            ref[every + (slice(x_side + x_count, planes),)] = slab

        @pl.when(iy == 0)
        def _():
            ref[every + (slice(None), slice(low_rows[0], low_rows[0] + low_rows[1]))] = strip

        @pl.when(iy == n_sub - 1)
        def _():
            ref[every + (slice(None), slice(high_rows[0], high_rows[0] + high_rows[1]))] = strip

    local = [
        pltpu.make_async_copy(src, dst.at[pl.ds(3, 16), pl.ds(0, 32)], local_sem.at[k])
        for k, (src, dst) in enumerate(((d_hbm, d), (p_hbm, p), (s_hbm, s)))
    ]
    for copy in local:
        copy.start()
    barrier = pltpu.get_barrier_semaphore()
    for dx, dy in DIRS:
        @pl.when(there(dx, dy))
        def _():
            pl.semaphore_signal(barrier, inc=1, device_id=peer(dx, dy), device_id_type=MESH)

    for ref in (d, p, s, fh):
        clear_outside(ref, (), 3, 16, 40, (36, 4), (32, 4))
    clear_outside(l1, (4,), 2, 4, 24, (20, 4), (16, 4))
    clear_outside(b1, (), 2, 4, 24, (20, 4), (16, 4))
    for index in (0, 1, 3, 4):
        @pl.when((ib + (index - 2) < 0) | (ib + (index - 2) >= n_blk))
        def _():
            c2[:, index] = jnp.zeros((4, 24, 128), jnp.float32)
            b2[index] = jnp.zeros((24, 128), jnp.float32)

    for edge, first in ((0, 0), (n_sub - 1, 16)):
        @pl.when(iy == edge)
        def _():
            c2[:, :, first:first + 8] = jnp.zeros((4, 5, 8, 128), jnp.float32)
            b2[:, first:first + 8] = jnp.zeros((5, 8, 128), jnp.float32)

    for copy in local:
        copy.wait()
    across = 1 + (ib > 0).astype(jnp.int32) + (ib < n_blk - 1).astype(jnp.int32)
    along = 1 + (iy > 0).astype(jnp.int32) + (iy < n_sub - 1).astype(jnp.int32)
    pl.semaphore_wait(barrier, across * along - 1)

    def fine_copies(src, dst, sem, width):
        return [
            remote(
                src.at[send_range(dx, 3, 16, width - abs(dy)), send_range(dy, 0, 32, 4)],
                dst.at[planes_to(dx, 3, 16, width - abs(dy)), rows_to(dy, 32, 4)],
                sem, k, dx, dy,
            )
            for k, (dx, dy) in enumerate(DIRS)
        ]

    d_copies = fine_copies(d, d, d_sem, 3)
    p_copies = fine_copies(p, p, p_sem, 3)
    s_copies = fine_copies(s, s, s_sem, 2)
    for copy in d_copies + p_copies + s_copies:
        copy.start()

    for copy in d_copies:
        copy.wait_recv()

    def x_face(i, _):
        xs[i] = d[2 * i + 2, 0:32] + d[2 * i + 3, 0:32]
        return 0

    lax.fori_loop(0, 10, x_face, 0, unroll=True)

    def x_pair(i, _):
        both = d[2 * i + 3] + d[2 * i + 4]
        ys[i, 0:8] = both[32:40]
        ys[i, 8:48] = both
        return 0

    lax.fori_loop(0, 8, x_pair, 0, unroll=True)

    lane1 = lanes((4, 16, 128))
    faces_x = 0.125 * pack_pairs(xs[:, pl.ds(0, 16, stride=2), :] + xs[:, pl.ds(1, 16, stride=2), :])
    lx = faces_x[0:4]
    ux = x_up(lx, faces_x[1:5], 2)
    odd_before = ys[:, pl.ds(7, 16, stride=2), :]
    even = ys[:, pl.ds(8, 16, stride=2), :]
    odd = ys[:, pl.ds(9, 16, stride=2), :]
    even_after = ys[:, pl.ds(10, 16, stride=2), :]
    ly = 0.125 * pack_pairs(even + odd_before)
    uy = 0.125 * pack_pairs(odd + even_after)
    both = (even + odd).reshape(4, 2, 16, 128)
    b_even, b_odd = both[:, 0], both[:, 1]
    first, last = lane1 < 2, lane1 >= 126
    zero1 = jnp.zeros((4, 16, 128), jnp.float32)
    is_even = lane1 % 2 == 0
    lz = 0.125 * (
        jnp.where(is_even, b_even, roll_z(b_odd, 1))
        + jnp.where(first, zero1, jnp.where(is_even, roll_z(b_even, 1), roll_z(b_odd, 2)))
    )
    uz = 0.125 * (
        jnp.where(is_even, roll_z(b_even, -1), b_odd)
        + jnp.where(last, zero1, jnp.where(is_even, roll_z(b_even, -2), roll_z(b_odd, -1)))
    )
    diag1 = 0.25 * (lx + ux + ly + uy + lz + uz)
    dg1[...] = diag1 * (1.0 / WEIGHT)
    l1[0, 2:6, 0:16] = lx
    l1[1, 2:6, 0:16] = ly
    l1[2, 2:6, 0:16] = jnp.where(first, zero1, lz)
    l1[3, 2:6, 0:16] = WEIGHT / diag1

    l1_copies = [
        remote(
            l1.at[:, send_range(dx, 2, 4, 2), send_range(dy, 0, 16, 4)],
            l1.at[:, planes_to(dx, 2, 4, 2), rows_to(dy, 16, 4)],
            l1_sem, k, dx, dy,
        )
        for k, (dx, dy) in enumerate(DIRS)
    ]
    for copy in l1_copies:
        copy.start()

    for k, face in enumerate((lx, ux, ly, uy, lz, uz)):
        cs[k] = face

    def rows_of(k, parity):
        return cs[k, :, pl.ds(parity, 8, stride=2), :]

    lane2 = lanes((4, 8, 128))
    zero2 = jnp.zeros((4, 8, 128), jnp.float32)
    lx2 = jnp.where(lane2 % 2 == 0, rows_of(0, 0) + rows_of(0, 1), zero2)
    ux2 = jnp.where(lane2 % 2 == 1, rows_of(1, 0) + rows_of(1, 1), zero2)
    ly2 = rows_of(2, 0)
    uy2 = rows_of(3, 1)
    lz2 = jnp.where(lane2 % 4 < 2, rows_of(4, 0) + rows_of(4, 1), zero2)
    uz2 = jnp.where(lane2 % 4 >= 2, rows_of(5, 0) + rows_of(5, 1), zero2)
    diag2 = (0.0625 * 0.25) * pack_groups(lx2 + ux2 + ly2 + uy2 + lz2 + uz2)
    c2[0, 2, 8:16] = 0.25 * pack_groups(lx2)
    c2[1, 2, 8:16] = 0.25 * pack_groups(ly2)
    c2[2, 2, 8:16] = jnp.where(lanes((8, 128)) < 4, 0.0, 0.25 * pack_groups(lz2))
    c2[3, 2, 8:16] = WEIGHT / diag2

    c2_copies = [
        remote(
            c2.at[:, 2, far_rows(dx, dy, 0)], c2.at[:, 2 - dx, far_rows(dx, dy, -8 * dy)],
            c2_sem, k, dx, dy,
        )
        for k, (dx, dy) in enumerate(FAR)
    ]
    lane0 = lanes((40, 128))
    zero0 = jnp.zeros((40, 128), jnp.float32)

    def fine_weights(i, carry):
        below, here = carry
        above = d[i + 1]
        row_below, row_above = roll_y(here, 1), roll_y(here, -1)
        z_below = jnp.where(lane0 > 0, roll_z(here, 1), zero0)
        z_above = jnp.where(lane0 < 127, roll_z(here, -1), zero0)
        near = (below + above) + (row_below + row_above) + (z_below + z_above)
        diag = 3.0 * here + 0.5 * near
        inv = jnp.where(here > 0.0, WEIGHT / diag, zero0)
        half = 0.5 * inv
        w0[0, i] = half * (here + below)
        w0[1, i] = half * (here + above)
        w0[2, i] = half * (here + row_below)
        w0[3, i] = half * (here + row_above)
        w0[4, i] = jnp.where(lane0 > 0, half * (here + z_below), zero0)
        w0[5, i] = jnp.where(lane0 < 127, half * (here + z_above), zero0)
        g0[i] = inv
        dg0[i] = diag * (1.0 / WEIGHT)
        return here, above

    lax.fori_loop(1, 21, fine_weights, (d[0], d[1]), unroll=True)

    for copy in p_copies + s_copies:
        copy.wait_recv()

    def scale_source(i, _):
        g0[i] = g0[i] * s[i]
        return 0

    lax.fori_loop(1, 21, scale_source, 0, unroll=True)

    def fine_sum(i, below, here, above):
        total = g0[i] + w0[0, i] * below + w0[1, i] * above
        total = total + w0[2, i] * roll_y(here, 1) + w0[3, i] * roll_y(here, -1)
        return total + w0[4, i] * roll_z(here, 1) + w0[5, i] * roll_z(here, -1)

    def fine_sweep(src, dst, low, high):
        def plane(i, carry):
            below, here = carry
            above = src[i + 1]
            dst[i] = fine_sum(i, below, here, above) + KEEP * here
            return here, above

        lax.fori_loop(low, high, plane, (src[low - 1], src[low]), unroll=True)

    fine_sweep(p, v1, 1, 21)
    fine_sweep(v1, v2, 2, 20)

    def residual(pair, carry):
        below, here = carry
        above = v2[2 * pair + 4]
        beyond = v2[2 * pair + 5]
        first_half = (fine_sum(2 * pair + 3, below, here, above) - WEIGHT * here) * dg0[2 * pair + 3]
        second_half = (fine_sum(2 * pair + 4, here, above, beyond) - WEIGHT * above) * dg0[2 * pair + 4]
        xs[pair] = (first_half + second_half)[0:32]
        return above, beyond

    lax.fori_loop(0, 8, residual, (v2[2], v2[3]), unroll=True)
    b1[2:6, 0:16] = 0.125 * pack_pairs(
        xs[0:8, pl.ds(0, 16, stride=2), :] + xs[0:8, pl.ds(1, 16, stride=2), :]
    )
    b1_copies = [
        remote(
            b1.at[send_range(dx, 2, 4, 2), send_range(dy, 0, 16, 4)],
            b1.at[planes_to(dx, 2, 4, 2), rows_to(dy, 16, 4)],
            b1_sem, k, dx, dy,
        )
        for k, (dx, dy) in enumerate(DIRS)
    ]
    f_copies = fine_copies(v2, fh, f_sem, 2)
    for copy in b1_copies + c2_copies:
        copy.start()

    for copy in l1_copies:
        copy.wait_recv()
    inv1 = l1[3]
    coarse_weights(w1, l1, inv1, 2, 0.25)

    for copy in b1_copies:
        copy.wait_recv()
    g1 = l1[3] * b1[...]
    err1 = g1
    err1 = g1 + coarse_sum(w1, err1, 2) + KEEP * err1
    res1 = (g1 + coarse_sum(w1, err1, 2) - WEIGHT * err1)[2:6, 0:16] * dg1[...]
    xs[0:4, 0:16] = res1
    b2[2, 8:16] = 0.125 * pack_groups(
        xs[0:4, pl.ds(0, 8, stride=2), :] + xs[0:4, pl.ds(1, 8, stride=2), :]
    )
    b2_copies = [
        remote(
            b2.at[2, far_rows(dx, dy, 0)], b2.at[2 - dx, far_rows(dx, dy, -8 * dy)],
            b2_sem, k, dx, dy,
        )
        for k, (dx, dy) in enumerate(FAR)
    ]
    for copy in b2_copies + f_copies:
        copy.start()
    for copy in c2_copies:
        copy.wait_recv()
    inv2 = c2[3]
    coarse_weights(w2, c2, inv2, 4, 0.0625)

    for copy in b2_copies:
        copy.wait_recv()
    g2 = c2[3] * b2[...]
    err2 = g2
    for _ in range(COARSE_SWEEPS):
        err2 = g2 + coarse_sum(w2, err2, 4) + KEEP * err2

    row = lax.broadcasted_iota(jnp.int32, (8, 128), 0)

    def put(pair, value):
        centre = value[8:16]
        sides = jnp.where(row < 2, value[16:24], roll_y(value[0:8], 4))
        for parity in range(2):
            e1[pair, pl.ds(parity, 8, stride=2), :] = centre
            e1[pair, pl.ds(16 + parity, 8, stride=2), :] = sides

    before, centre, after = spread_groups(err2[1]), spread_groups(err2[2]), spread_groups(err2[3])
    for pair, value in enumerate(before[2:4] + centre + after[0:2]):
        put(pair, value)
    g1 = l1[3] * b1[...]
    err1 = err1 + e1[:, 0:24]
    for _ in range(POST):
        err1 = g1 + coarse_sum(w1, err1, 2) + KEEP * err1

    def put_fine(index, value):
        sides = jnp.where(row < 2, value[16:24], roll_y(value[16:24], 4))
        for parity in range(2):
            e0[index, pl.ds(parity, 16, stride=2), :] = value[0:16]
            e0[index, pl.ds(32 + parity, 8, stride=2), :] = sides

    for pair in range(1, 7):
        even_cell, odd_cell = spread_pairs(err1[pair])
        if pair > 1:
            put_fine(2 * pair - 3, even_cell)
        if pair < 6:
            put_fine(2 * pair - 2, odd_cell)

    for copy in f_copies:
        copy.wait_recv()

    def correct(i, _):
        halves = (2 * i + 1, 2 * i + 2)
        add = e0[i]
        for plane in halves:
            v1[plane, 0:32] = v2[plane, 0:32] + add[0:32]
            v1[plane, 32:40] = fh[plane, 32:40] + add[32:40]
        return 0

    for i in (0, 9):
        for plane in (2 * i + 1, 2 * i + 2):
            v1[plane] = fh[plane] + e0[i, 0:40]
    lax.fori_loop(1, 9, correct, 0, unroll=True)

    fine_sweep(v1, fh, 2, 20)

    def last_sweep(i, carry):
        below, here = carry
        above = fh[i + 1]
        out[i - 3] = (fine_sum(i, below, here, above) + KEEP * here)[0:32]
        return here, above

    carry = (fh[2], fh[3])
    stores = []
    for k in range(4):
        carry = lax.fori_loop(4 * k + 3, 4 * k + 7, last_sweep, carry, unroll=True)
        part = pl.ds(4 * k, 4)
        stores.append(pltpu.make_async_copy(out.at[part], o_hbm.at[part], local_sem.at[3 + k]))
        stores[-1].start()
    for copy in d_copies + p_copies + s_copies + l1_copies + c2_copies + f_copies + b1_copies + b2_copies:
        copy.wait_send()
    for store in stores:
        store.wait()


def solution(mesh):
    sizes = (mesh.shape["blk"], mesh.shape["sub"])

    def on_device(pressure, source, inv_density):
        def vmem(*shape):
            return pltpu.VMEM(shape, jnp.float32)

        near, far = len(DIRS), len(FAR)
        return pl.pallas_call(
            functools.partial(kernel, sizes),
            out_shape=jax.ShapeDtypeStruct((16, 32, 128), jnp.float32),
            in_specs=[pl.BlockSpec(memory_space=pltpu.HBM)] * 3,
            out_specs=pl.BlockSpec(memory_space=pl.ANY),
            scratch_shapes=[
                vmem(22, 40, 128), vmem(22, 40, 128), vmem(22, 40, 128),
                vmem(22, 40, 128), vmem(22, 40, 128), vmem(22, 40, 128),
                vmem(16, 32, 128), vmem(6, 22, 40, 128), vmem(22, 40, 128), vmem(22, 40, 128),
                vmem(10, 32, 128), vmem(8, 48, 128), vmem(6, 4, 16, 128),
                vmem(4, 8, 24, 128), vmem(6, 8, 24, 128), vmem(8, 24, 128), vmem(4, 16, 128),
                vmem(4, 5, 24, 128), vmem(6, 5, 24, 128), vmem(5, 24, 128),
                vmem(8, 32, 128), vmem(10, 48, 128),
                pltpu.SemaphoreType.DMA((7,)),
                pltpu.SemaphoreType.DMA((2, near)), pltpu.SemaphoreType.DMA((2, near)),
                pltpu.SemaphoreType.DMA((2, near)), pltpu.SemaphoreType.DMA((2, near)),
                pltpu.SemaphoreType.DMA((2, near)), pltpu.SemaphoreType.DMA((2, near)),
                pltpu.SemaphoreType.DMA((2, far)), pltpu.SemaphoreType.DMA((2, far)),
            ],
            compiler_params=pltpu.CompilerParams(
                collective_id=0, has_side_effects=True, vmem_limit_bytes=54850 * 1024
            ),
        )(pressure, source, inv_density)

    return jax.shard_map(
        on_device,
        mesh=mesh,
        in_specs=(P("blk", "sub", None),) * 3,
        out_specs=P("blk", "sub", None),
        check_vma=False,
    )
```

```python
import functools

import jax
import jax.numpy as jnp
from jax import lax
from jax.experimental import pallas as pl
from jax.experimental.pallas import tpu as pltpu
from jax.sharding import PartitionSpec as P

MESH = pl.DeviceIdType.MESH
PRE = 2
POST = 2
COARSE_SWEEPS = 6
WEIGHT = 0.8
KEEP = 1.0 - WEIGHT

DIRS = [(-1, -1), (1, 1), (-1, 1), (1, -1), (-1, 0), (1, 0), (0, -1), (0, 1)]
FAR = [(-2, -1), (2, 1), (-2, 1), (2, -1), (-2, 0), (2, 0)] + DIRS


def send_range(step, first, count, width):
    if step == 0:
        return pl.ds(first, count)
    return pl.ds(first + count - width, width) if step > 0 else pl.ds(first, width)


def planes_to(step, first, count, width):
    if step == 0:
        return pl.ds(first, count)
    return pl.ds(first - width, width) if step > 0 else pl.ds(first + count, width)


def rows_to(step, count, width):
    if step == 0:
        return pl.ds(0, count)
    return pl.ds(count + width, width) if step > 0 else pl.ds(count, width)


def far_rows(dx, dy, shift):
    if abs(dx) + abs(dy) == 3:
        return pl.ds(8 + shift + (4 if dy > 0 else 0), 4)
    return pl.ds(8 + shift, 8)


def lanes(shape):
    return lax.broadcasted_iota(jnp.int32, shape, len(shape) - 1)


def roll_z(value, shift):
    return pltpu.roll(value, shift % 128, value.ndim - 1)


def roll_y(value, shift):
    return pltpu.roll(value, shift % value.shape[-2], value.ndim - 2)


def pack_pairs(value):
    split = value.reshape((value.shape[0] // 2, 2) + value.shape[1:])
    even, odd = split[:, 0], split[:, 1]
    mask = lanes(even.shape) % 2 == 0
    return jnp.where(mask, even + roll_z(even, -1), odd + roll_z(odd, 1))


def pack_groups(value):
    lane = lanes(value.shape[1:])
    low = jnp.where(lane % 2 == 0, value[0] + roll_z(value[0], -1), value[1] + roll_z(value[1], 1))
    high = jnp.where(lane % 2 == 0, value[2] + roll_z(value[2], -1), value[3] + roll_z(value[3], 1))
    return jnp.where(lane % 4 < 2, low + roll_z(low, -2), high + roll_z(high, 2))


def spread_pairs(value):
    mask = lanes(value.shape) % 2 == 0
    return jnp.where(mask, value, roll_z(value, 1)), jnp.where(mask, roll_z(value, -1), value)


def spread_groups(value):
    mask = lanes(value.shape) % 4 < 2
    low = jnp.where(mask, value, roll_z(value, 2))
    high = jnp.where(mask, roll_z(value, -2), value)
    return spread_pairs(low) + spread_pairs(high)


def ahead(value):
    return jnp.concatenate([value[1:], value[:1]], axis=0)


def behind(value):
    return jnp.concatenate([value[-1:], value[:-1]], axis=0)


def x_up(value, following, group):
    mask = lanes(value.shape) % group < group - 1
    return jnp.where(mask, roll_z(value, -1), roll_z(following, group - 1))


def x_down(value, previous, group):
    mask = lanes(value.shape) % group > 0
    return jnp.where(mask, roll_z(value, 1), roll_z(previous, 1 - group))


def coarse_weights(w, faces, inv, group, scale):
    half = scale * inv
    w[0] = half * faces[0]
    w[1] = half * x_up(faces[0], ahead(faces[0]), group)
    w[2] = half * faces[1]
    w[3] = half * roll_y(faces[1], -1)
    w[4] = half * faces[2]
    w[5] = half * roll_z(faces[2], -group)


def coarse_sum(w, value, group):
    return weighted_sum(w, value, behind(value), ahead(value), group)


def weighted_sum(w, value, previous, following, group):
    across = w[0] * x_down(value, previous, group) + w[1] * x_up(value, following, group)
    along = w[2] * roll_y(value, 1) + w[3] * roll_y(value, -1)
    return (along + (w[4] * roll_z(value, group) + w[5] * roll_z(value, -group))) + across


class Halo:
    def __init__(self, copy, sends, receives):
        self.copy, self.sends, self.receives = copy, sends, receives

    def start(self):
        pl.when(self.sends)(self.copy.start)

    def wait_send(self):
        pl.when(self.sends)(self.copy.wait_send)

    def wait_recv(self):
        pl.when(self.receives)(self.copy.wait_recv)


def kernel(
    sizes, p_hbm, s_hbm, d_hbm, o_hbm,
    p, d, s, sx, v1, v2, fh, out, w0, g0, dg0,
    xs, ys, cs, l1, w1, b1, dg1, c2, w2, b2, e1, e0,
    local_sem, d_sem, p_sem, s_sem, f_sem, l1_sem, b1_sem, c2_sem, b2_sem,
):
    n_blk, n_sub = sizes
    ib, iy = lax.axis_index("blk"), lax.axis_index("sub")

    def peer(dx, dy):
        return {"blk": ib + dx, "sub": iy + dy}

    def there(dx, dy):
        known = []
        if dx:
            known.append(ib >= -dx if dx < 0 else ib < n_blk - dx)
        if dy:
            known.append(iy >= -dy if dy < 0 else iy < n_sub - dy)
        return functools.reduce(jnp.logical_and, known)

    def remote(src, dst, sem, k, dx, dy):
        return Halo(
            pltpu.make_async_remote_copy(
                src_ref=src, dst_ref=dst, send_sem=sem.at[0, k], recv_sem=sem.at[1, k],
                device_id=peer(dx, dy), device_id_type=MESH,
            ),
            there(dx, dy),
            there(-dx, -dy),
        )

    def clear_outside(ref, lead, x_side, x_count, rows, low_rows, high_rows):
        planes = x_count + 2 * x_side
        slab = jnp.zeros(lead + (x_side, rows, 128), jnp.float32)
        strip = jnp.zeros(lead + (planes, low_rows[1], 128), jnp.float32)
        every = (slice(None),) * len(lead)

        @pl.when(ib == 0)
        def _():
            ref[every + (slice(0, x_side),)] = slab

        @pl.when(ib == n_blk - 1)
        def _():
            ref[every + (slice(x_side + x_count, planes),)] = slab

        @pl.when(iy == 0)
        def _():
            ref[every + (slice(None), slice(low_rows[0], low_rows[0] + low_rows[1]))] = strip

        @pl.when(iy == n_sub - 1)
        def _():
            ref[every + (slice(None), slice(high_rows[0], high_rows[0] + high_rows[1]))] = strip

    barrier = pltpu.get_barrier_semaphore()
    for dx, dy in DIRS:
        @pl.when(there(dx, dy))
        def _():
            pl.semaphore_signal(barrier, inc=1, device_id=peer(dx, dy), device_id_type=MESH)

    local = [
        pltpu.make_async_copy(src, dst.at[pl.ds(3, 16), pl.ds(0, 32)], local_sem.at[k])
        for k, (src, dst) in enumerate(((d_hbm, d), (p_hbm, p), (s_hbm, s)))
    ]
    for copy in local:
        copy.start()
    for ref in (d, p, s, fh):
        clear_outside(ref, (), 3, 16, 40, (36, 4), (32, 4))
    clear_outside(l1, (4,), 2, 4, 24, (20, 4), (16, 4))
    clear_outside(b1, (), 2, 4, 24, (20, 4), (16, 4))
    for index in (0, 1, 3, 4):
        @pl.when((ib + (index - 2) < 0) | (ib + (index - 2) >= n_blk))
        def _():
            c2[:, index] = jnp.zeros((4, 24, 128), jnp.float32)
            b2[index] = jnp.zeros((24, 128), jnp.float32)

    for edge, first in ((0, 0), (n_sub - 1, 16)):
        @pl.when(iy == edge)
        def _():
            c2[:, :, first:first + 8] = jnp.zeros((4, 5, 8, 128), jnp.float32)
            b2[:, first:first + 8] = jnp.zeros((5, 8, 128), jnp.float32)

    for copy in local:
        copy.wait()
    def joined(plane, beyond):
        face = 0.5 * (d[plane, 0:32] + d[beyond, 0:32])
        return s[plane, 0:32] + face * p[beyond, 0:32]

    sx[0, 0] = s[3, 0:32]
    sx[0, 1] = joined(4, 5)
    sx[1, 0] = joined(17, 16)
    sx[1, 1] = s[18, 0:32]
    p[0] = jnp.zeros((40, 128), jnp.float32)
    p[21] = jnp.zeros((40, 128), jnp.float32)

    across = 1 + (ib > 0).astype(jnp.int32) + (ib < n_blk - 1).astype(jnp.int32)
    along = 1 + (iy > 0).astype(jnp.int32) + (iy < n_sub - 1).astype(jnp.int32)
    pl.semaphore_wait(barrier, across * along - 1)

    def fine_copies(src, dst, sem, width, sides=None):
        copies = []
        for k, (dx, dy) in enumerate(DIRS):
            count = min(width - abs(dy), 2) if src is p else width - abs(dy)
            if sides is not None and dy == 0:
                block = sides.at[0 if dx < 0 else 1]
            else:
                block = src.at[send_range(dx, 3, 16, count), send_range(dy, 0, 32, 4)]
            target = dst.at[planes_to(dx, 3, 16, count), rows_to(dy, 32, 4)]
            copies.append(remote(block, target, sem, k, dx, dy))
        return copies

    d_copies = fine_copies(d, d, d_sem, 3)
    p_copies = fine_copies(p, p, p_sem, 3)
    s_copies = fine_copies(s, s, s_sem, 2, sx)
    for copy in d_copies + p_copies + s_copies:
        copy.start()

    for copy in d_copies:
        copy.wait_recv()

    def x_face(i, _):
        xs[i] = d[2 * i + 2, 0:32] + d[2 * i + 3, 0:32]
        return 0

    lax.fori_loop(0, 10, x_face, 0, unroll=True)

    def x_pair(i, _):
        both = d[2 * i + 3] + d[2 * i + 4]
        ys[i, 0:8] = both[32:40]
        ys[i, 8:48] = both
        return 0

    lax.fori_loop(0, 8, x_pair, 0, unroll=True)

    lane1 = lanes((4, 16, 128))
    faces_x = 0.125 * pack_pairs(xs[:, pl.ds(0, 16, stride=2), :] + xs[:, pl.ds(1, 16, stride=2), :])
    lx = faces_x[0:4]
    ux = x_up(lx, faces_x[1:5], 2)
    odd_before = ys[:, pl.ds(7, 16, stride=2), :]
    even = ys[:, pl.ds(8, 16, stride=2), :]
    odd = ys[:, pl.ds(9, 16, stride=2), :]
    even_after = ys[:, pl.ds(10, 16, stride=2), :]
    ly = 0.125 * pack_pairs(even + odd_before)
    uy = 0.125 * pack_pairs(odd + even_after)
    both = (even + odd).reshape(4, 2, 16, 128)
    b_even, b_odd = both[:, 0], both[:, 1]
    first, last = lane1 < 2, lane1 >= 126
    zero1 = jnp.zeros((4, 16, 128), jnp.float32)
    is_even = lane1 % 2 == 0
    lz = 0.125 * (
        jnp.where(is_even, b_even, roll_z(b_odd, 1))
        + jnp.where(first, zero1, jnp.where(is_even, roll_z(b_even, 1), roll_z(b_odd, 2)))
    )
    uz = 0.125 * (
        jnp.where(is_even, roll_z(b_even, -1), b_odd)
        + jnp.where(last, zero1, jnp.where(is_even, roll_z(b_even, -2), roll_z(b_odd, -1)))
    )
    diag1 = 0.25 * (lx + ux + ly + uy + lz + uz)
    dg1[...] = diag1 * (1.0 / WEIGHT)
    l1[0, 2:6, 0:16] = lx
    l1[1, 2:6, 0:16] = ly
    l1[2, 2:6, 0:16] = jnp.where(first, zero1, lz)
    l1[3, 2:6, 0:16] = WEIGHT / diag1

    l1_copies = [
        remote(
            l1.at[:, send_range(dx, 2, 4, 2), send_range(dy, 0, 16, 4)],
            l1.at[:, planes_to(dx, 2, 4, 2), rows_to(dy, 16, 4)],
            l1_sem, k, dx, dy,
        )
        for k, (dx, dy) in enumerate(DIRS)
    ]
    for copy in l1_copies:
        copy.start()

    for k, face in enumerate((lx, ux, ly, uy, lz, uz)):
        cs[k] = face

    def rows_of(k, parity):
        return cs[k, :, pl.ds(parity, 8, stride=2), :]

    lane2 = lanes((4, 8, 128))
    zero2 = jnp.zeros((4, 8, 128), jnp.float32)
    lx2 = jnp.where(lane2 % 2 == 0, rows_of(0, 0) + rows_of(0, 1), zero2)
    ux2 = jnp.where(lane2 % 2 == 1, rows_of(1, 0) + rows_of(1, 1), zero2)
    ly2 = rows_of(2, 0)
    uy2 = rows_of(3, 1)
    lz2 = jnp.where(lane2 % 4 < 2, rows_of(4, 0) + rows_of(4, 1), zero2)
    uz2 = jnp.where(lane2 % 4 >= 2, rows_of(5, 0) + rows_of(5, 1), zero2)
    diag2 = (0.0625 * 0.25) * pack_groups(lx2 + ux2 + ly2 + uy2 + lz2 + uz2)
    c2[0, 2, 8:16] = 0.25 * pack_groups(lx2)
    c2[1, 2, 8:16] = 0.25 * pack_groups(ly2)
    c2[2, 2, 8:16] = jnp.where(lanes((8, 128)) < 4, 0.0, 0.25 * pack_groups(lz2))
    c2[3, 2, 8:16] = WEIGHT / diag2

    c2_copies = [
        remote(
            c2.at[:, 2, far_rows(dx, dy, 0)], c2.at[:, 2 - dx, far_rows(dx, dy, -8 * dy)],
            c2_sem, k, dx, dy,
        )
        for k, (dx, dy) in enumerate(FAR)
    ]
    lane0 = lanes((40, 128))
    zero0 = jnp.zeros((40, 128), jnp.float32)

    def fine_weights(i, carry):
        below, here = carry
        above = d[i + 1]
        row_below, row_above = roll_y(here, 1), roll_y(here, -1)
        z_below = jnp.where(lane0 > 0, roll_z(here, 1), zero0)
        z_above = jnp.where(lane0 < 127, roll_z(here, -1), zero0)
        near = (below + above) + (row_below + row_above) + (z_below + z_above)
        diag = 3.0 * here + 0.5 * near
        inv = jnp.where(here > 0.0, WEIGHT / diag, zero0)
        half = 0.5 * inv
        w0[0, i] = half * (here + below)
        w0[1, i] = half * (here + above)
        w0[2, i] = half * (here + row_below)
        w0[3, i] = half * (here + row_above)
        w0[4, i] = jnp.where(lane0 > 0, half * (here + z_below), zero0)
        w0[5, i] = jnp.where(lane0 < 127, half * (here + z_above), zero0)
        g0[i] = inv
        dg0[i] = diag * (1.0 / WEIGHT)
        return here, above

    lax.fori_loop(1, 21, fine_weights, (d[0], d[1]), unroll=True)
    w0[0, 1] = zero0
    w0[1, 20] = zero0

    for copy in p_copies + s_copies:
        copy.wait_recv()

    def scale_source(i, _):
        g0[i] = g0[i] * s[i]
        return 0

    lax.fori_loop(1, 21, scale_source, 0, unroll=True)

    def fine_sum(i, below, here, above):
        total = g0[i] + w0[0, i] * below + w0[1, i] * above
        total = total + w0[2, i] * roll_y(here, 1) + w0[3, i] * roll_y(here, -1)
        return total + w0[4, i] * roll_z(here, 1) + w0[5, i] * roll_z(here, -1)

    def fine_sweep(src, dst, low, high):
        def plane(i, carry):
            below, here = carry
            above = src[i + 1]
            dst[i] = fine_sum(i, below, here, above) + KEEP * here
            return here, above

        lax.fori_loop(low, high, plane, (src[low - 1], src[low]), unroll=True)

    fine_sweep(p, v1, 1, 21)
    fine_sweep(v1, v2, 2, 20)

    def residual(pair, carry):
        below, here = carry
        above = v2[2 * pair + 4]
        beyond = v2[2 * pair + 5]
        first_half = (fine_sum(2 * pair + 3, below, here, above) - WEIGHT * here) * dg0[2 * pair + 3]
        second_half = (fine_sum(2 * pair + 4, here, above, beyond) - WEIGHT * above) * dg0[2 * pair + 4]
        xs[pair] = (first_half + second_half)[0:32]
        return above, beyond

    lax.fori_loop(0, 8, residual, (v2[2], v2[3]), unroll=True)
    b1[2:6, 0:16] = 0.125 * pack_pairs(
        xs[0:8, pl.ds(0, 16, stride=2), :] + xs[0:8, pl.ds(1, 16, stride=2), :]
    )
    b1_copies = [
        remote(
            b1.at[send_range(dx, 2, 4, 2), send_range(dy, 0, 16, 4)],
            b1.at[planes_to(dx, 2, 4, 2), rows_to(dy, 16, 4)],
            b1_sem, k, dx, dy,
        )
        for k, (dx, dy) in enumerate(DIRS)
    ]
    f_copies = fine_copies(v2, fh, f_sem, 2)
    for copy in b1_copies + c2_copies:
        copy.start()

    for copy in l1_copies:
        copy.wait_recv()
    inv1 = l1[3]
    coarse_weights(w1, l1, inv1, 2, 0.25)

    for copy in d_copies + p_copies + s_copies:
        copy.wait_send()
    for copy in b1_copies:
        copy.wait_recv()
    g1 = l1[3] * b1[...]
    err1 = g1
    err1 = (g1 + KEEP * err1) + coarse_sum(w1, err1, 2)
    res1 = ((g1 - WEIGHT * err1) + coarse_sum(w1, err1, 2))[2:6, 0:16] * dg1[...]
    xs[0:4, 0:16] = res1
    b2[2, 8:16] = 0.125 * pack_groups(
        xs[0:4, pl.ds(0, 8, stride=2), :] + xs[0:4, pl.ds(1, 8, stride=2), :]
    )
    b2_copies = [
        remote(
            b2.at[2, far_rows(dx, dy, 0)], b2.at[2 - dx, far_rows(dx, dy, -8 * dy)],
            b2_sem, k, dx, dy,
        )
        for k, (dx, dy) in enumerate(FAR)
    ]
    for copy in b2_copies + f_copies:
        copy.start()
    for copy in c2_copies:
        copy.wait_recv()
    inv2 = c2[3]
    coarse_weights(w2, c2, inv2, 4, 0.0625)

    for copy in l1_copies + c2_copies + b1_copies:
        copy.wait_send()
    for copy in b2_copies:
        copy.wait_recv()
    g2 = c2[3] * b2[...]
    err2 = g2
    for _ in range(COARSE_SWEEPS - 3):
        err2 = (g2 + KEEP * err2) + coarse_sum(w2, err2, 4)
    w2_middle = [w2[k, 1:4] for k in range(6)]
    g2 = g2[1:4]
    total = weighted_sum(w2_middle, err2[1:4], err2[0:3], err2[2:5], 4)
    err2 = (g2 + KEEP * err2[1:4]) + total
    for _ in range(2):
        err2 = (g2 + KEEP * err2) + coarse_sum(w2_middle, err2, 4)

    row = lax.broadcasted_iota(jnp.int32, (8, 128), 0)

    def put(pair, value):
        centre = value[8:16]
        sides = jnp.where(row < 2, value[16:24], roll_y(value[0:8], 4))
        for parity in range(2):
            e1[pair, pl.ds(parity, 8, stride=2), :] = centre
            e1[pair, pl.ds(16 + parity, 8, stride=2), :] = sides

    before, centre, after = spread_groups(err2[0]), spread_groups(err2[1]), spread_groups(err2[2])
    for pair, value in enumerate(before[2:4] + centre + after[0:2]):
        put(pair, value)
    g1 = l1[3] * b1[...]
    err1 = err1 + e1[:, 0:24]
    for _ in range(POST):
        err1 = (g1 + KEEP * err1) + coarse_sum(w1, err1, 2)

    def put_fine(index, value):
        sides = jnp.where(row < 2, value[16:24], roll_y(value[16:24], 4))
        for parity in range(2):
            e0[index, pl.ds(parity, 16, stride=2), :] = value[0:16]
            e0[index, pl.ds(32 + parity, 8, stride=2), :] = sides

    for pair in range(1, 7):
        even_cell, odd_cell = spread_pairs(err1[pair])
        if pair > 1:
            put_fine(2 * pair - 3, even_cell)
        if pair < 6:
            put_fine(2 * pair - 2, odd_cell)

    for copy in f_copies + b2_copies:
        copy.wait_send()
    for copy in f_copies:
        copy.wait_recv()

    def correct(i, _):
        halves = (2 * i + 1, 2 * i + 2)
        add = e0[i]
        for plane in halves:
            v1[plane, 0:32] = v2[plane, 0:32] + add[0:32]
            v1[plane, 32:40] = fh[plane, 32:40] + add[32:40]
        return 0

    for i in (0, 9):
        for plane in (2 * i + 1, 2 * i + 2):
            v1[plane] = fh[plane] + e0[i, 0:40]
    lax.fori_loop(1, 9, correct, 0, unroll=True)

    fine_sweep(v1, fh, 2, 20)

    def last_sweep(i, carry):
        below, here = carry
        above = fh[i + 1]
        out[i - 3] = (fine_sum(i, below, here, above) + KEEP * here)[0:32]
        return here, above

    carry = (fh[2], fh[3])
    stores = []
    for k in range(4):
        carry = lax.fori_loop(4 * k + 3, 4 * k + 7, last_sweep, carry, unroll=True)
        part = pl.ds(4 * k, 4)
        stores.append(pltpu.make_async_copy(out.at[part], o_hbm.at[part], local_sem.at[3 + k]))
        stores[-1].start()
    for store in stores:
        store.wait()


def solution(mesh):
    sizes = (mesh.shape["blk"], mesh.shape["sub"])

    def on_device(pressure, source, inv_density):
        def vmem(*shape):
            return pltpu.VMEM(shape, jnp.float32)

        near, far = len(DIRS), len(FAR)
        return pl.pallas_call(
            functools.partial(kernel, sizes),
            out_shape=jax.ShapeDtypeStruct((16, 32, 128), jnp.float32),
            in_specs=[pl.BlockSpec(memory_space=pltpu.HBM)] * 3,
            out_specs=pl.BlockSpec(memory_space=pl.ANY),
            scratch_shapes=[
                vmem(22, 40, 128), vmem(22, 40, 128), vmem(22, 40, 128), vmem(2, 2, 32, 128),
                vmem(22, 40, 128), vmem(22, 40, 128), vmem(22, 40, 128),
                vmem(16, 32, 128), vmem(6, 22, 40, 128), vmem(22, 40, 128), vmem(22, 40, 128),
                vmem(10, 32, 128), vmem(8, 48, 128), vmem(6, 4, 16, 128),
                vmem(4, 8, 24, 128), vmem(6, 8, 24, 128), vmem(8, 24, 128), vmem(4, 16, 128),
                vmem(4, 5, 24, 128), vmem(6, 5, 24, 128), vmem(5, 24, 128),
                vmem(8, 32, 128), vmem(10, 48, 128),
                pltpu.SemaphoreType.DMA((7,)),
                pltpu.SemaphoreType.DMA((2, near)), pltpu.SemaphoreType.DMA((2, near)),
                pltpu.SemaphoreType.DMA((2, near)), pltpu.SemaphoreType.DMA((2, near)),
                pltpu.SemaphoreType.DMA((2, near)), pltpu.SemaphoreType.DMA((2, near)),
                pltpu.SemaphoreType.DMA((2, far)), pltpu.SemaphoreType.DMA((2, far)),
            ],
            compiler_params=pltpu.CompilerParams(
                collective_id=0, has_side_effects=True, vmem_limit_bytes=54850 * 1024
            ),
        )(pressure, source, inv_density)

    return jax.shard_map(
        on_device,
        mesh=mesh,
        in_specs=(P("blk", "sub", None),) * 3,
        out_specs=P("blk", "sub", None),
        check_vma=False,
    )
```

```python
import functools

import jax
import jax.numpy as jnp
from jax import lax
from jax.experimental import pallas as pl
from jax.experimental.pallas import tpu as pltpu
from jax.sharding import PartitionSpec as P

MESH = pl.DeviceIdType.MESH
PRE = 2
POST = 2
COARSE_SWEEPS = 6
WEIGHT = 0.8
KEEP = 1.0 - WEIGHT

DIRS = [(-1, -1), (1, 1), (-1, 1), (1, -1), (-1, 0), (1, 0), (0, -1), (0, 1)]
FAR = [(-2, -1), (2, 1), (-2, 1), (2, -1), (-2, 0), (2, 0)] + DIRS


def send_range(step, first, count, width):
    if step == 0:
        return pl.ds(first, count)
    return pl.ds(first + count - width, width) if step > 0 else pl.ds(first, width)


def planes_to(step, first, count, width):
    if step == 0:
        return pl.ds(first, count)
    return pl.ds(first - width, width) if step > 0 else pl.ds(first + count, width)


def rows_to(step, count, width):
    if step == 0:
        return pl.ds(0, count)
    return pl.ds(count + width, width) if step > 0 else pl.ds(count, width)


def far_rows(dx, dy, shift):
    if abs(dx) + abs(dy) == 3:
        return pl.ds(8 + shift + (4 if dy > 0 else 0), 4)
    return pl.ds(8 + shift, 8)


def lanes(shape):
    return lax.broadcasted_iota(jnp.int32, shape, len(shape) - 1)


def roll_z(value, shift):
    return pltpu.roll(value, shift % 128, value.ndim - 1)


def roll_y(value, shift):
    return pltpu.roll(value, shift % value.shape[-2], value.ndim - 2)


def pack_pairs(value):
    split = value.reshape((value.shape[0] // 2, 2) + value.shape[1:])
    even, odd = split[:, 0], split[:, 1]
    mask = lanes(even.shape) % 2 == 0
    return jnp.where(mask, even + roll_z(even, -1), odd + roll_z(odd, 1))


def pack_groups(value):
    lane = lanes(value.shape[1:])
    low = jnp.where(lane % 2 == 0, value[0] + roll_z(value[0], -1), value[1] + roll_z(value[1], 1))
    high = jnp.where(lane % 2 == 0, value[2] + roll_z(value[2], -1), value[3] + roll_z(value[3], 1))
    return jnp.where(lane % 4 < 2, low + roll_z(low, -2), high + roll_z(high, 2))


def spread_pairs(value):
    mask = lanes(value.shape) % 2 == 0
    return jnp.where(mask, value, roll_z(value, 1)), jnp.where(mask, roll_z(value, -1), value)


def spread_groups(value):
    mask = lanes(value.shape) % 4 < 2
    low = jnp.where(mask, value, roll_z(value, 2))
    high = jnp.where(mask, roll_z(value, -2), value)
    return spread_pairs(low) + spread_pairs(high)


def ahead(value):
    return jnp.concatenate([value[1:], value[:1]], axis=0)


def behind(value):
    return jnp.concatenate([value[-1:], value[:-1]], axis=0)


def x_up(value, following, group):
    mask = lanes(value.shape) % group < group - 1
    return jnp.where(mask, roll_z(value, -1), roll_z(following, group - 1))


def x_down(value, previous, group):
    mask = lanes(value.shape) % group > 0
    return jnp.where(mask, roll_z(value, 1), roll_z(previous, 1 - group))


def coarse_weights(w, faces, inv, group, scale):
    half = scale * inv
    w[0] = half * faces[0]
    w[1] = half * x_up(faces[0], ahead(faces[0]), group)
    w[2] = half * faces[1]
    w[3] = half * roll_y(faces[1], -1)
    w[4] = half * faces[2]
    w[5] = half * roll_z(faces[2], -group)


def coarse_sum(w, value, group):
    return weighted_sum(w, value, behind(value), ahead(value), group)


def weighted_sum(w, value, previous, following, group):
    across = w[0] * x_down(value, previous, group) + w[1] * x_up(value, following, group)
    along = w[2] * roll_y(value, 1) + w[3] * roll_y(value, -1)
    return (along + (w[4] * roll_z(value, group) + w[5] * roll_z(value, -group))) + across


class Halo:
    def __init__(self, copy, sends, receives):
        self.copy, self.sends, self.receives = copy, sends, receives
        self.starts = sends

    def start(self):
        pl.when(self.starts)(self.copy.start)

    def wait_send(self):
        pl.when(self.sends)(self.copy.wait_send)

    def wait_recv(self):
        pl.when(self.receives)(self.copy.wait_recv)


def kernel(
    sizes, p_hbm, s_hbm, d_hbm, o_hbm,
    p, d, s, sx, p_mate, d_mate, s_mate, v1, v2, fh, out, w0, g0, dg0,
    xs, ys, cs, l1, w1, b1, dg1, c2, w2, b2, e1, e0,
    local_sem, d_mate_sem, p_mate_sem, s_mate_sem, d_sem, p_sem, s_sem, f_sem, l1_sem, b1_sem, c2_sem, b2_sem,
):
    n_blk, n_sub = sizes
    ib, iy = lax.axis_index("blk"), lax.axis_index("sub")

    def peer(dx, dy):
        return {"blk": ib + dx, "sub": iy + dy}

    def there(dx, dy):
        known = []
        if dx:
            known.append(ib >= -dx if dx < 0 else ib < n_blk - dx)
        if dy:
            known.append(iy >= -dy if dy < 0 else iy < n_sub - dy)
        return functools.reduce(jnp.logical_and, known)

    def remote(src, dst, sem, k, dx, dy):
        return Halo(
            pltpu.make_async_remote_copy(
                src_ref=src, dst_ref=dst, send_sem=sem.at[0, k], recv_sem=sem.at[1, k],
                device_id=peer(dx, dy), device_id_type=MESH,
            ),
            there(dx, dy),
            there(-dx, -dy),
        )

    def clear_outside(ref, lead, x_side, x_count, rows, low_rows, high_rows):
        planes = x_count + 2 * x_side
        slab = jnp.zeros(lead + (x_side, rows, 128), jnp.float32)
        strip = jnp.zeros(lead + (planes, low_rows[1], 128), jnp.float32)
        every = (slice(None),) * len(lead)

        @pl.when(ib == 0)
        def _():
            ref[every + (slice(0, x_side),)] = slab

        @pl.when(ib == n_blk - 1)
        def _():
            ref[every + (slice(x_side + x_count, planes),)] = slab

        @pl.when(iy == 0)
        def _():
            ref[every + (slice(None), slice(low_rows[0], low_rows[0] + low_rows[1]))] = strip

        @pl.when(iy == n_sub - 1)
        def _():
            ref[every + (slice(None), slice(high_rows[0], high_rows[0] + high_rows[1]))] = strip

    odd_one = lax.rem(iy, 2) == 1
    even_one = jnp.logical_not(odd_one)
    barrier = pltpu.get_barrier_semaphore()

    def announce(dx, dy):
        pl.semaphore_signal(barrier, inc=1, device_id=peer(dx, dy), device_id_type=MESH)

    pl.when(even_one)(functools.partial(announce, 0, 1))
    for dx, dy in [(i, j) for j in (-2, 1, 0, -1) for i in (-1, 1, 0) if (i, j) != (0, 0)]:
        pl.when(odd_one & there(dx, dy))(functools.partial(announce, dx, dy))

    local = [
        pltpu.make_async_copy(src, dst.at[pl.ds(3, 16), pl.ds(0, 32)], local_sem.at[k])
        for k, (src, dst) in enumerate(((d_hbm, d), (p_hbm, p), (s_hbm, s)))
    ]
    for copy in local:
        copy.start()
    for ref in (d, p, s, fh):
        clear_outside(ref, (), 3, 16, 40, (36, 4), (32, 4))
    clear_outside(l1, (4,), 2, 4, 24, (20, 4), (16, 4))
    clear_outside(b1, (), 2, 4, 24, (20, 4), (16, 4))
    for index in (0, 1, 3, 4):
        @pl.when((ib + (index - 2) < 0) | (ib + (index - 2) >= n_blk))
        def _():
            c2[:, index] = jnp.zeros((4, 24, 128), jnp.float32)
            b2[index] = jnp.zeros((24, 128), jnp.float32)

    for edge, first in ((0, 0), (n_sub - 1, 16)):
        @pl.when(iy == edge)
        def _():
            c2[:, :, first:first + 8] = jnp.zeros((4, 5, 8, 128), jnp.float32)
            b2[:, first:first + 8] = jnp.zeros((5, 8, 128), jnp.float32)

    for copy in local:
        copy.wait()
    def joined(plane, beyond):
        face = 0.5 * (d[plane, 0:32] + d[beyond, 0:32])
        return s[plane, 0:32] + face * p[beyond, 0:32]

    sx[0, 0] = s[3, 0:32]
    sx[0, 1] = joined(4, 5)
    sx[1, 0] = joined(17, 16)
    sx[1, 1] = s[18, 0:32]
    p[0] = jnp.zeros((40, 128), jnp.float32)
    p[21] = jnp.zeros((40, 128), jnp.float32)

    across = 1 + (ib > 0).astype(jnp.int32) + (ib < n_blk - 1).astype(jnp.int32)
    behind_me = (iy > 0).astype(jnp.int32)
    beyond_mate = (iy + 2 < n_sub).astype(jnp.int32)
    pl.semaphore_wait(barrier, across * jnp.where(odd_one, 1 + beyond_mate, 1 + behind_me))

    def slices(dx, dy, width):
        return (
            (send_range(dx, 3, 16, width), send_range(dy, 0, 32, 4)),
            (planes_to(dx, 3, 16, width), rows_to(dy, 32, 4)),
        )

    def fine_copies(src, dst, sem, width):
        copies = []
        for k, (dx, dy) in enumerate(DIRS):
            here, target = slices(dx, dy, width - abs(dy))
            copies.append(remote(src.at[here], dst.at[target], sem, k, dx, dy))
        return copies

    def first_copies(ref, mate, sem, mate_sem, width, side_width, sides=None):
        copies, through, onward = [], [], []
        for k, (dx, dy) in enumerate(DIRS):
            here, target = slices(dx, dy, min(width - abs(dy), side_width) if dx else width)
            block = ref.at[here] if sides is None or dy else sides.at[0 if dx < 0 else 1]
            copies.append(remote(block, ref.at[target], sem, k, dx, dy))
            if (dx, dy) == (0, -1):
                continue
            target_even = odd_one if dy else even_one
            copies[-1].starts = there(dx, dy) & jnp.logical_not(target_even)
            copy = pltpu.make_async_remote_copy(
                src_ref=block, dst_ref=mate.at[target], send_sem=sem.at[0, k],
                recv_sem=mate_sem.at[0, k], device_id=peer(dx, dy + 1), device_id_type=MESH,
            )
            from_x = ib >= dx if dx > 0 else ib < n_blk + dx
            from_y = iy >= 1 + dy if dy >= 0 else iy < n_sub + 1 + dy
            through.append(Halo(copy, there(dx, dy) & target_even, odd_one & from_x & from_y))
            copy = pltpu.make_async_remote_copy(
                src_ref=mate.at[target], dst_ref=ref.at[target], send_sem=mate_sem.at[1, k],
                recv_sem=sem.at[1, k], device_id=peer(0, -1), device_id_type=MESH,
            )
            onward.append(Halo(copy, through[-1].receives, None))
        return copies, through, onward

    def hand_on(through, onward):
        for arriving, leaving in zip(through, onward):
            @pl.when(arriving.receives)
            def _():
                arriving.copy.wait_recv()
                leaving.copy.start()

    d_copies, d_through, d_onward = first_copies(d, d_mate, d_sem, d_mate_sem, 3, 3)
    p_copies, p_through, p_onward = first_copies(p, p_mate, p_sem, p_mate_sem, 3, 2)
    s_copies, s_through, s_onward = first_copies(s, s_mate, s_sem, s_mate_sem, 2, 2, sx)
    for copies, through in ((d_copies, d_through), (p_copies, p_through), (s_copies, s_through)):
        for k, copy in enumerate(copies):
            copy.start()
            if k < 6:
                through[k].start()
            elif k == 7:
                through[6].start()
    hand_on(d_through, d_onward)

    for copy in d_copies:
        copy.wait_recv()

    def x_face(i, _):
        xs[i] = d[2 * i + 2, 0:32] + d[2 * i + 3, 0:32]
        return 0

    lax.fori_loop(0, 10, x_face, 0, unroll=True)

    def x_pair(i, _):
        both = d[2 * i + 3] + d[2 * i + 4]
        ys[i, 0:8] = both[32:40]
        ys[i, 8:48] = both
        return 0

    lax.fori_loop(0, 8, x_pair, 0, unroll=True)

    lane1 = lanes((4, 16, 128))
    faces_x = 0.125 * pack_pairs(xs[:, pl.ds(0, 16, stride=2), :] + xs[:, pl.ds(1, 16, stride=2), :])
    lx = faces_x[0:4]
    ux = x_up(lx, faces_x[1:5], 2)
    odd_before = ys[:, pl.ds(7, 16, stride=2), :]
    even = ys[:, pl.ds(8, 16, stride=2), :]
    odd = ys[:, pl.ds(9, 16, stride=2), :]
    even_after = ys[:, pl.ds(10, 16, stride=2), :]
    ly = 0.125 * pack_pairs(even + odd_before)
    uy = 0.125 * pack_pairs(odd + even_after)
    both = (even + odd).reshape(4, 2, 16, 128)
    b_even, b_odd = both[:, 0], both[:, 1]
    first, last = lane1 < 2, lane1 >= 126
    zero1 = jnp.zeros((4, 16, 128), jnp.float32)
    is_even = lane1 % 2 == 0
    lz = 0.125 * (
        jnp.where(is_even, b_even, roll_z(b_odd, 1))
        + jnp.where(first, zero1, jnp.where(is_even, roll_z(b_even, 1), roll_z(b_odd, 2)))
    )
    uz = 0.125 * (
        jnp.where(is_even, roll_z(b_even, -1), b_odd)
        + jnp.where(last, zero1, jnp.where(is_even, roll_z(b_even, -2), roll_z(b_odd, -1)))
    )
    diag1 = 0.25 * (lx + ux + ly + uy + lz + uz)
    dg1[...] = diag1 * (1.0 / WEIGHT)
    l1[0, 2:6, 0:16] = lx
    l1[1, 2:6, 0:16] = ly
    l1[2, 2:6, 0:16] = jnp.where(first, zero1, lz)
    l1[3, 2:6, 0:16] = WEIGHT / diag1

    l1_copies = [
        remote(
            l1.at[:, send_range(dx, 2, 4, 2), send_range(dy, 0, 16, 4)],
            l1.at[:, planes_to(dx, 2, 4, 2), rows_to(dy, 16, 4)],
            l1_sem, k, dx, dy,
        )
        for k, (dx, dy) in enumerate(DIRS)
    ]
    for copy in l1_copies:
        copy.start()
    hand_on(p_through, p_onward)
    hand_on(s_through, s_onward)

    for k, face in enumerate((lx, ux, ly, uy, lz, uz)):
        cs[k] = face

    def rows_of(k, parity):
        return cs[k, :, pl.ds(parity, 8, stride=2), :]

    lane2 = lanes((4, 8, 128))
    zero2 = jnp.zeros((4, 8, 128), jnp.float32)
    lx2 = jnp.where(lane2 % 2 == 0, rows_of(0, 0) + rows_of(0, 1), zero2)
    ux2 = jnp.where(lane2 % 2 == 1, rows_of(1, 0) + rows_of(1, 1), zero2)
    ly2 = rows_of(2, 0)
    uy2 = rows_of(3, 1)
    lz2 = jnp.where(lane2 % 4 < 2, rows_of(4, 0) + rows_of(4, 1), zero2)
    uz2 = jnp.where(lane2 % 4 >= 2, rows_of(5, 0) + rows_of(5, 1), zero2)
    diag2 = (0.0625 * 0.25) * pack_groups(lx2 + ux2 + ly2 + uy2 + lz2 + uz2)
    c2[0, 2, 8:16] = 0.25 * pack_groups(lx2)
    c2[1, 2, 8:16] = 0.25 * pack_groups(ly2)
    c2[2, 2, 8:16] = jnp.where(lanes((8, 128)) < 4, 0.0, 0.25 * pack_groups(lz2))
    c2[3, 2, 8:16] = WEIGHT / diag2

    c2_copies = [
        remote(
            c2.at[:, 2, far_rows(dx, dy, 0)], c2.at[:, 2 - dx, far_rows(dx, dy, -8 * dy)],
            c2_sem, k, dx, dy,
        )
        for k, (dx, dy) in enumerate(FAR)
    ]
    lane0 = lanes((40, 128))
    zero0 = jnp.zeros((40, 128), jnp.float32)

    def fine_weights(i, carry):
        below, here = carry
        above = d[i + 1]
        row_below, row_above = roll_y(here, 1), roll_y(here, -1)
        z_below = jnp.where(lane0 > 0, roll_z(here, 1), zero0)
        z_above = jnp.where(lane0 < 127, roll_z(here, -1), zero0)
        near = (below + above) + (row_below + row_above) + (z_below + z_above)
        diag = 3.0 * here + 0.5 * near
        inv = jnp.where(here > 0.0, WEIGHT / diag, zero0)
        half = 0.5 * inv
        w0[0, i] = half * (here + below)
        w0[1, i] = half * (here + above)
        w0[2, i] = half * (here + row_below)
        w0[3, i] = half * (here + row_above)
        w0[4, i] = jnp.where(lane0 > 0, half * (here + z_below), zero0)
        w0[5, i] = jnp.where(lane0 < 127, half * (here + z_above), zero0)
        g0[i] = inv
        dg0[i] = diag * (1.0 / WEIGHT)
        return here, above

    lax.fori_loop(1, 21, fine_weights, (d[0], d[1]), unroll=True)
    w0[0, 1] = zero0
    w0[1, 20] = zero0

    for copy in p_copies + s_copies:
        copy.wait_recv()

    def scale_source(i, _):
        g0[i] = g0[i] * s[i]
        return 0

    lax.fori_loop(1, 21, scale_source, 0, unroll=True)

    def fine_sum(i, below, here, above):
        total = g0[i] + w0[0, i] * below + w0[1, i] * above
        total = total + w0[2, i] * roll_y(here, 1) + w0[3, i] * roll_y(here, -1)
        return total + w0[4, i] * roll_z(here, 1) + w0[5, i] * roll_z(here, -1)

    def fine_sweep(src, dst, low, high):
        def plane(i, carry):
            below, here = carry
            above = src[i + 1]
            dst[i] = fine_sum(i, below, here, above) + KEEP * here
            return here, above

        lax.fori_loop(low, high, plane, (src[low - 1], src[low]), unroll=True)

    fine_sweep(p, v1, 1, 21)
    fine_sweep(v1, v2, 2, 20)

    def residual(pair, carry):
        below, here = carry
        above = v2[2 * pair + 4]
        beyond = v2[2 * pair + 5]
        first_half = (fine_sum(2 * pair + 3, below, here, above) - WEIGHT * here) * dg0[2 * pair + 3]
        second_half = (fine_sum(2 * pair + 4, here, above, beyond) - WEIGHT * above) * dg0[2 * pair + 4]
        xs[pair] = (first_half + second_half)[0:32]
        return above, beyond

    lax.fori_loop(0, 8, residual, (v2[2], v2[3]), unroll=True)
    b1[2:6, 0:16] = 0.125 * pack_pairs(
        xs[0:8, pl.ds(0, 16, stride=2), :] + xs[0:8, pl.ds(1, 16, stride=2), :]
    )
    b1_copies = [
        remote(
            b1.at[send_range(dx, 2, 4, 2), send_range(dy, 0, 16, 4)],
            b1.at[planes_to(dx, 2, 4, 2), rows_to(dy, 16, 4)],
            b1_sem, k, dx, dy,
        )
        for k, (dx, dy) in enumerate(DIRS)
    ]
    f_copies = fine_copies(v2, fh, f_sem, 2)
    for copy in b1_copies:
        copy.start()

    for copy in l1_copies:
        copy.wait_recv()
    for copy in c2_copies:
        copy.start()
    inv1 = l1[3]
    coarse_weights(w1, l1, inv1, 2, 0.25)

    for copy in d_copies + p_copies + s_copies + d_onward + p_onward + s_onward:
        copy.wait_send()
    for copy in b1_copies:
        copy.wait_recv()
    g1 = l1[3] * b1[...]
    err1 = g1
    err1 = (g1 + KEEP * err1) + coarse_sum(w1, err1, 2)
    res1 = ((g1 - WEIGHT * err1) + coarse_sum(w1, err1, 2))[2:6, 0:16] * dg1[...]
    xs[0:4, 0:16] = res1
    b2[2, 8:16] = 0.125 * pack_groups(
        xs[0:4, pl.ds(0, 8, stride=2), :] + xs[0:4, pl.ds(1, 8, stride=2), :]
    )
    b2_copies = [
        remote(
            b2.at[2, far_rows(dx, dy, 0)], b2.at[2 - dx, far_rows(dx, dy, -8 * dy)],
            b2_sem, k, dx, dy,
        )
        for k, (dx, dy) in enumerate(FAR)
    ]
    for copy in b2_copies + f_copies:
        copy.start()
    for copy in c2_copies:
        copy.wait_recv()
    inv2 = c2[3]
    coarse_weights(w2, c2, inv2, 4, 0.0625)

    for copy in l1_copies + c2_copies + b1_copies:
        copy.wait_send()
    for copy in b2_copies:
        copy.wait_recv()
    g2 = c2[3] * b2[...]
    err2 = g2
    for _ in range(COARSE_SWEEPS - 3):
        err2 = (g2 + KEEP * err2) + coarse_sum(w2, err2, 4)
    w2_middle = [w2[k, 1:4] for k in range(6)]
    g2 = g2[1:4]
    total = weighted_sum(w2_middle, err2[1:4], err2[0:3], err2[2:5], 4)
    err2 = (g2 + KEEP * err2[1:4]) + total
    for _ in range(2):
        err2 = (g2 + KEEP * err2) + coarse_sum(w2_middle, err2, 4)

    row = lax.broadcasted_iota(jnp.int32, (8, 128), 0)

    def put(pair, value):
        centre = value[8:16]
        sides = jnp.where(row < 2, value[16:24], roll_y(value[0:8], 4))
        for parity in range(2):
            e1[pair, pl.ds(parity, 8, stride=2), :] = centre
            e1[pair, pl.ds(16 + parity, 8, stride=2), :] = sides

    before, centre, after = spread_groups(err2[0]), spread_groups(err2[1]), spread_groups(err2[2])
    for pair, value in enumerate(before[2:4] + centre + after[0:2]):
        put(pair, value)
    g1 = l1[3] * b1[...]
    err1 = err1 + e1[:, 0:24]
    for _ in range(POST):
        err1 = (g1 + KEEP * err1) + coarse_sum(w1, err1, 2)

    def put_fine(index, value):
        sides = jnp.where(row < 2, value[16:24], roll_y(value[16:24], 4))
        for parity in range(2):
            e0[index, pl.ds(parity, 16, stride=2), :] = value[0:16]
            e0[index, pl.ds(32 + parity, 8, stride=2), :] = sides

    for pair in range(1, 7):
        even_cell, odd_cell = spread_pairs(err1[pair])
        if pair > 1:
            put_fine(2 * pair - 3, even_cell)
        if pair < 6:
            put_fine(2 * pair - 2, odd_cell)

    for copy in f_copies + b2_copies:
        copy.wait_send()
    for copy in f_copies:
        copy.wait_recv()

    def correct(i, _):
        halves = (2 * i + 1, 2 * i + 2)
        add = e0[i]
        for plane in halves:
            v1[plane, 0:32] = v2[plane, 0:32] + add[0:32]
            v1[plane, 32:40] = fh[plane, 32:40] + add[32:40]
        return 0

    for i in (0, 9):
        for plane in (2 * i + 1, 2 * i + 2):
            v1[plane] = fh[plane] + e0[i, 0:40]
    lax.fori_loop(1, 9, correct, 0, unroll=True)

    fine_sweep(v1, fh, 2, 20)

    def last_sweep(i, carry):
        below, here = carry
        above = fh[i + 1]
        out[i - 3] = (fine_sum(i, below, here, above) + KEEP * here)[0:32]
        return here, above

    carry = (fh[2], fh[3])
    stores = []
    for k in range(4):
        carry = lax.fori_loop(4 * k + 3, 4 * k + 7, last_sweep, carry, unroll=True)
        part = pl.ds(4 * k, 4)
        stores.append(pltpu.make_async_copy(out.at[part], o_hbm.at[part], local_sem.at[3 + k]))
        stores[-1].start()
    for store in stores:
        store.wait()


def solution(mesh):
    sizes = (mesh.shape["blk"], mesh.shape["sub"])

    def on_device(pressure, source, inv_density):
        def vmem(*shape):
            return pltpu.VMEM(shape, jnp.float32)

        near, far = len(DIRS), len(FAR)
        return pl.pallas_call(
            functools.partial(kernel, sizes),
            out_shape=jax.ShapeDtypeStruct((16, 32, 128), jnp.float32),
            in_specs=[pl.BlockSpec(memory_space=pltpu.HBM)] * 3,
            out_specs=pl.BlockSpec(memory_space=pl.ANY),
            scratch_shapes=[
                vmem(22, 40, 128), vmem(22, 40, 128), vmem(22, 40, 128), vmem(2, 2, 32, 128),
                vmem(22, 40, 128), vmem(22, 40, 128), vmem(22, 40, 128),
                vmem(22, 40, 128), vmem(22, 40, 128), vmem(22, 40, 128),
                vmem(16, 32, 128), vmem(6, 22, 40, 128), vmem(22, 40, 128), vmem(22, 40, 128),
                vmem(10, 32, 128), vmem(8, 48, 128), vmem(6, 4, 16, 128),
                vmem(4, 8, 24, 128), vmem(6, 8, 24, 128), vmem(8, 24, 128), vmem(4, 16, 128),
                vmem(4, 5, 24, 128), vmem(6, 5, 24, 128), vmem(5, 24, 128),
                vmem(8, 32, 128), vmem(10, 48, 128),
                pltpu.SemaphoreType.DMA((7,)),
                pltpu.SemaphoreType.DMA((2, near)), pltpu.SemaphoreType.DMA((2, near)), pltpu.SemaphoreType.DMA((2, near)),
                pltpu.SemaphoreType.DMA((2, near)), pltpu.SemaphoreType.DMA((2, near)),
                pltpu.SemaphoreType.DMA((2, near)), pltpu.SemaphoreType.DMA((2, near)),
                pltpu.SemaphoreType.DMA((2, near)), pltpu.SemaphoreType.DMA((2, near)),
                pltpu.SemaphoreType.DMA((2, far)), pltpu.SemaphoreType.DMA((2, far)),
            ],
            compiler_params=pltpu.CompilerParams(
                collective_id=0, has_side_effects=True, vmem_limit_bytes=54850 * 1024
            ),
        )(pressure, source, inv_density)

    return jax.shard_map(
        on_device,
        mesh=mesh,
        in_specs=(P("blk", "sub", None),) * 3,
        out_specs=P("blk", "sub", None),
        check_vma=False,
    )
```

```python
import functools

import jax
import jax.numpy as jnp
from jax import lax
from jax.experimental import pallas as pl
from jax.experimental.pallas import tpu as pltpu
from jax.sharding import PartitionSpec as P

MESH = pl.DeviceIdType.MESH
PRE = 2
POST = 2
COARSE_SWEEPS = 6
WEIGHT = 0.8
KEEP = 1.0 - WEIGHT

DIRS = [(-1, -1), (1, 1), (-1, 1), (1, -1), (-1, 0), (1, 0), (0, -1), (0, 1)]
FAR = [(-2, -1), (2, 1), (-2, 1), (2, -1), (-2, 0), (2, 0)] + DIRS


def send_range(step, first, count, width):
    if step == 0:
        return pl.ds(first, count)
    return pl.ds(first + count - width, width) if step > 0 else pl.ds(first, width)


def planes_to(step, first, count, width):
    if step == 0:
        return pl.ds(first, count)
    return pl.ds(first - width, width) if step > 0 else pl.ds(first + count, width)


def rows_to(step, count, width):
    if step == 0:
        return pl.ds(0, count)
    return pl.ds(count + width, width) if step > 0 else pl.ds(count, width)


def far_rows(dx, dy, shift):
    if abs(dx) + abs(dy) == 3:
        return pl.ds(8 + shift + (4 if dy > 0 else 0), 4)
    return pl.ds(8 + shift, 8)


def lanes(shape):
    return lax.broadcasted_iota(jnp.int32, shape, len(shape) - 1)


def roll_z(value, shift):
    return pltpu.roll(value, shift % 128, value.ndim - 1)


def roll_y(value, shift):
    return pltpu.roll(value, shift % value.shape[-2], value.ndim - 2)


def pack_pairs(value):
    split = value.reshape((value.shape[0] // 2, 2) + value.shape[1:])
    even, odd = split[:, 0], split[:, 1]
    mask = lanes(even.shape) % 2 == 0
    return jnp.where(mask, even + roll_z(even, -1), odd + roll_z(odd, 1))


def pack_groups(value):
    lane = lanes(value.shape[1:])
    low = jnp.where(lane % 2 == 0, value[0] + roll_z(value[0], -1), value[1] + roll_z(value[1], 1))
    high = jnp.where(lane % 2 == 0, value[2] + roll_z(value[2], -1), value[3] + roll_z(value[3], 1))
    return jnp.where(lane % 4 < 2, low + roll_z(low, -2), high + roll_z(high, 2))


def spread_pairs(value):
    mask = lanes(value.shape) % 2 == 0
    return jnp.where(mask, value, roll_z(value, 1)), jnp.where(mask, roll_z(value, -1), value)


def spread_groups(value):
    mask = lanes(value.shape) % 4 < 2
    low = jnp.where(mask, value, roll_z(value, 2))
    high = jnp.where(mask, roll_z(value, -2), value)
    return spread_pairs(low) + spread_pairs(high)


def ahead(value):
    return jnp.concatenate([value[1:], value[:1]], axis=0)


def behind(value):
    return jnp.concatenate([value[-1:], value[:-1]], axis=0)


def x_up(value, following, group):
    mask = lanes(value.shape) % group < group - 1
    return jnp.where(mask, roll_z(value, -1), roll_z(following, group - 1))


def x_down(value, previous, group):
    mask = lanes(value.shape) % group > 0
    return jnp.where(mask, roll_z(value, 1), roll_z(previous, 1 - group))


def coarse_weights(w, faces, inv, group, scale):
    half = scale * inv
    w[0] = half * faces[0]
    w[1] = half * x_up(faces[0], ahead(faces[0]), group)
    w[2] = half * faces[1]
    w[3] = half * roll_y(faces[1], -1)
    w[4] = half * faces[2]
    w[5] = half * roll_z(faces[2], -group)


def coarse_sum(w, value, group):
    return weighted_sum(w, value, behind(value), ahead(value), group)


def weighted_sum(w, value, previous, following, group):
    across = w[0] * x_down(value, previous, group) + w[1] * x_up(value, following, group)
    along = w[2] * roll_y(value, 1) + w[3] * roll_y(value, -1)
    return (along + (w[4] * roll_z(value, group) + w[5] * roll_z(value, -group))) + across


class Halo:
    def __init__(self, copy, sends, receives):
        self.copy, self.sends, self.receives = copy, sends, receives
        self.starts = sends

    def start(self):
        pl.when(self.starts)(self.copy.start)

    def wait_send(self):
        pl.when(self.sends)(self.copy.wait_send)

    def wait_recv(self):
        pl.when(self.receives)(self.copy.wait_recv)


def kernel(
    sizes, p_hbm, s_hbm, d_hbm, o_hbm,
    p, d, s, sx, p_mate, d_mate, s_mate, v1, v2, fh, out, w0, g0, dg0,
    xs, ys, cs, l1, w1, b1, dg1, c2, w2, b2, e1, e0,
    local_sem, d_mate_sem, p_mate_sem, s_mate_sem, d_sem, p_sem, s_sem, f_sem, l1_sem, b1_sem, c2_sem, b2_sem,
):
    n_blk, n_sub = sizes
    ib, iy = lax.axis_index("blk"), lax.axis_index("sub")

    def peer(dx, dy):
        return {"blk": ib + dx, "sub": iy + dy}

    def there(dx, dy):
        known = []
        if dx:
            known.append(ib >= -dx if dx < 0 else ib < n_blk - dx)
        if dy:
            known.append(iy >= -dy if dy < 0 else iy < n_sub - dy)
        return functools.reduce(jnp.logical_and, known)

    def remote(src, dst, sem, k, dx, dy):
        return Halo(
            pltpu.make_async_remote_copy(
                src_ref=src, dst_ref=dst, send_sem=sem.at[0, k], recv_sem=sem.at[1, k],
                device_id=peer(dx, dy), device_id_type=MESH,
            ),
            there(dx, dy),
            there(-dx, -dy),
        )

    def clear_outside(ref, lead, x_side, x_count, rows, low_rows, high_rows):
        planes = x_count + 2 * x_side
        slab = jnp.zeros(lead + (x_side, rows, 128), jnp.float32)
        strip = jnp.zeros(lead + (planes, low_rows[1], 128), jnp.float32)
        every = (slice(None),) * len(lead)

        @pl.when(ib == 0)
        def _():
            ref[every + (slice(0, x_side),)] = slab

        @pl.when(ib == n_blk - 1)
        def _():
            ref[every + (slice(x_side + x_count, planes),)] = slab

        @pl.when(iy == 0)
        def _():
            ref[every + (slice(None), slice(low_rows[0], low_rows[0] + low_rows[1]))] = strip

        @pl.when(iy == n_sub - 1)
        def _():
            ref[every + (slice(None), slice(high_rows[0], high_rows[0] + high_rows[1]))] = strip

    odd_one = lax.rem(iy, 2) == 1
    even_one = jnp.logical_not(odd_one)
    barrier = pltpu.get_barrier_semaphore()

    def announce(dx, dy):
        pl.semaphore_signal(barrier, inc=1, device_id=peer(dx, dy), device_id_type=MESH)

    pl.when(even_one)(functools.partial(announce, 0, 1))
    for dx, dy in [(i, j) for j in (-2, 1, 0, -1) for i in (-1, 1, 0) if (i, j) != (0, 0)]:
        pl.when(odd_one & there(dx, dy))(functools.partial(announce, dx, dy))

    local = [
        pltpu.make_async_copy(src, dst.at[pl.ds(3, 16), pl.ds(0, 32)], local_sem.at[k])
        for k, (src, dst) in enumerate(((d_hbm, d), (p_hbm, p), (s_hbm, s)))
    ]
    for copy in local:
        copy.start()
    across = 1 + (ib > 0).astype(jnp.int32) + (ib < n_blk - 1).astype(jnp.int32)
    behind_me = (iy > 0).astype(jnp.int32)
    beyond_mate = (iy + 2 < n_sub).astype(jnp.int32)
    pl.semaphore_wait(barrier, across * jnp.where(odd_one, 1 + beyond_mate, 1 + behind_me))

    def slices(dx, dy, width):
        return (
            (send_range(dx, 3, 16, width), send_range(dy, 0, 32, 4)),
            (planes_to(dx, 3, 16, width), rows_to(dy, 32, 4)),
        )

    def fine_copies(src, dst, sem, width):
        copies = []
        for k, (dx, dy) in enumerate(DIRS):
            here, target = slices(dx, dy, width - abs(dy))
            copies.append(remote(src.at[here], dst.at[target], sem, k, dx, dy))
        return copies

    def first_copies(ref, hbm, mate, sem, mate_sem, width, side_width, sides=None):
        copies, through, onward = [], [], []
        for k, (dx, dy) in enumerate(DIRS):
            here, target = slices(dx, dy, min(width - abs(dy), side_width) if dx else width)
            block = hbm.at[pl.ds(here[0].start - 3, here[0].size), here[1]]
            if sides is not None and dy == 0:
                block = sides.at[0 if dx < 0 else 1]
            copies.append(remote(block, ref.at[target], sem, k, dx, dy))
            if (dx, dy) == (0, -1):
                continue
            target_even = odd_one if dy else even_one
            copies[-1].starts = there(dx, dy) & jnp.logical_not(target_even)
            copy = pltpu.make_async_remote_copy(
                src_ref=block, dst_ref=mate.at[target], send_sem=sem.at[0, k],
                recv_sem=mate_sem.at[0, k], device_id=peer(dx, dy + 1), device_id_type=MESH,
            )
            from_x = ib >= dx if dx > 0 else ib < n_blk + dx
            from_y = iy >= 1 + dy if dy >= 0 else iy < n_sub + 1 + dy
            through.append(Halo(copy, there(dx, dy) & target_even, odd_one & from_x & from_y))
            copy = pltpu.make_async_remote_copy(
                src_ref=mate.at[target], dst_ref=ref.at[target], send_sem=mate_sem.at[1, k],
                recv_sem=sem.at[1, k], device_id=peer(0, -1), device_id_type=MESH,
            )
            onward.append(Halo(copy, through[-1].receives, None))
        return copies, through, onward

    def hand_on(through, onward):
        for arriving, leaving in zip(through, onward):
            @pl.when(arriving.receives)
            def _():
                arriving.copy.wait_recv()
                leaving.copy.start()

    d_copies, d_through, d_onward = first_copies(d, d_hbm, d_mate, d_sem, d_mate_sem, 3, 3)
    p_copies, p_through, p_onward = first_copies(p, p_hbm, p_mate, p_sem, p_mate_sem, 3, 2)
    s_copies, s_through, s_onward = first_copies(s, s_hbm, s_mate, s_sem, s_mate_sem, 2, 2, sx)
    def send_first(copies, through):
        for k, copy in enumerate(copies):
            copy.start()
            if k < 6:
                through[k].start()
            elif k == 7:
                through[6].start()

    send_first(d_copies, d_through)
    send_first(p_copies, p_through)
    for ref in (d, p, s, fh):
        clear_outside(ref, (), 3, 16, 40, (36, 4), (32, 4))
    clear_outside(l1, (4,), 2, 4, 24, (20, 4), (16, 4))
    clear_outside(b1, (), 2, 4, 24, (20, 4), (16, 4))
    for index in (0, 1, 3, 4):
        @pl.when((ib + (index - 2) < 0) | (ib + (index - 2) >= n_blk))
        def _():
            c2[:, index] = jnp.zeros((4, 24, 128), jnp.float32)
            b2[index] = jnp.zeros((24, 128), jnp.float32)

    for edge, first in ((0, 0), (n_sub - 1, 16)):
        @pl.when(iy == edge)
        def _():
            c2[:, :, first:first + 8] = jnp.zeros((4, 5, 8, 128), jnp.float32)
            b2[:, first:first + 8] = jnp.zeros((5, 8, 128), jnp.float32)

    for copy in local:
        copy.wait()
    def joined(plane, beyond):
        face = 0.5 * (d[plane, 0:32] + d[beyond, 0:32])
        return s[plane, 0:32] + face * p[beyond, 0:32]

    sx[0, 0] = s[3, 0:32]
    sx[0, 1] = joined(4, 5)
    sx[1, 0] = joined(17, 16)
    sx[1, 1] = s[18, 0:32]
    p[0] = jnp.zeros((40, 128), jnp.float32)
    p[21] = jnp.zeros((40, 128), jnp.float32)

    send_first(s_copies, s_through)
    hand_on(d_through, d_onward)

    for copy in d_copies:
        copy.wait_recv()

    def x_face(i, _):
        xs[i] = d[2 * i + 2, 0:32] + d[2 * i + 3, 0:32]
        return 0

    lax.fori_loop(0, 10, x_face, 0, unroll=True)

    def x_pair(i, _):
        both = d[2 * i + 3] + d[2 * i + 4]
        ys[i, 0:8] = both[32:40]
        ys[i, 8:48] = both
        return 0

    lax.fori_loop(0, 8, x_pair, 0, unroll=True)

    lane1 = lanes((4, 16, 128))
    faces_x = 0.125 * pack_pairs(xs[:, pl.ds(0, 16, stride=2), :] + xs[:, pl.ds(1, 16, stride=2), :])
    lx = faces_x[0:4]
    ux = x_up(lx, faces_x[1:5], 2)
    odd_before = ys[:, pl.ds(7, 16, stride=2), :]
    even = ys[:, pl.ds(8, 16, stride=2), :]
    odd = ys[:, pl.ds(9, 16, stride=2), :]
    even_after = ys[:, pl.ds(10, 16, stride=2), :]
    ly = 0.125 * pack_pairs(even + odd_before)
    uy = 0.125 * pack_pairs(odd + even_after)
    both = (even + odd).reshape(4, 2, 16, 128)
    b_even, b_odd = both[:, 0], both[:, 1]
    first, last = lane1 < 2, lane1 >= 126
    zero1 = jnp.zeros((4, 16, 128), jnp.float32)
    is_even = lane1 % 2 == 0
    lz = 0.125 * (
        jnp.where(is_even, b_even, roll_z(b_odd, 1))
        + jnp.where(first, zero1, jnp.where(is_even, roll_z(b_even, 1), roll_z(b_odd, 2)))
    )
    uz = 0.125 * (
        jnp.where(is_even, roll_z(b_even, -1), b_odd)
        + jnp.where(last, zero1, jnp.where(is_even, roll_z(b_even, -2), roll_z(b_odd, -1)))
    )
    diag1 = 0.25 * (lx + ux + ly + uy + lz + uz)
    dg1[...] = diag1 * (1.0 / WEIGHT)
    l1[0, 2:6, 0:16] = lx
    l1[1, 2:6, 0:16] = ly
    l1[2, 2:6, 0:16] = jnp.where(first, zero1, lz)
    l1[3, 2:6, 0:16] = WEIGHT / diag1

    l1_copies = [
        remote(
            l1.at[:, send_range(dx, 2, 4, 2), send_range(dy, 0, 16, 4)],
            l1.at[:, planes_to(dx, 2, 4, 2), rows_to(dy, 16, 4)],
            l1_sem, k, dx, dy,
        )
        for k, (dx, dy) in enumerate(DIRS)
    ]
    for copy in l1_copies:
        copy.start()
    hand_on(p_through, p_onward)
    hand_on(s_through, s_onward)

    for k, face in enumerate((lx, ux, ly, uy, lz, uz)):
        cs[k] = face

    def rows_of(k, parity):
        return cs[k, :, pl.ds(parity, 8, stride=2), :]

    lane2 = lanes((4, 8, 128))
    zero2 = jnp.zeros((4, 8, 128), jnp.float32)
    lx2 = jnp.where(lane2 % 2 == 0, rows_of(0, 0) + rows_of(0, 1), zero2)
    ux2 = jnp.where(lane2 % 2 == 1, rows_of(1, 0) + rows_of(1, 1), zero2)
    ly2 = rows_of(2, 0)
    uy2 = rows_of(3, 1)
    lz2 = jnp.where(lane2 % 4 < 2, rows_of(4, 0) + rows_of(4, 1), zero2)
    uz2 = jnp.where(lane2 % 4 >= 2, rows_of(5, 0) + rows_of(5, 1), zero2)
    diag2 = (0.0625 * 0.25) * pack_groups(lx2 + ux2 + ly2 + uy2 + lz2 + uz2)
    c2[0, 2, 8:16] = 0.25 * pack_groups(lx2)
    c2[1, 2, 8:16] = 0.25 * pack_groups(ly2)
    c2[2, 2, 8:16] = jnp.where(lanes((8, 128)) < 4, 0.0, 0.25 * pack_groups(lz2))
    c2[3, 2, 8:16] = WEIGHT / diag2

    c2_copies = [
        remote(
            c2.at[:, 2, far_rows(dx, dy, 0)], c2.at[:, 2 - dx, far_rows(dx, dy, -8 * dy)],
            c2_sem, k, dx, dy,
        )
        for k, (dx, dy) in enumerate(FAR)
    ]
    lane0 = lanes((40, 128))
    zero0 = jnp.zeros((40, 128), jnp.float32)

    def fine_weights(i, carry):
        below, here = carry
        above = d[i + 1]
        row_below, row_above = roll_y(here, 1), roll_y(here, -1)
        z_below = jnp.where(lane0 > 0, roll_z(here, 1), zero0)
        z_above = jnp.where(lane0 < 127, roll_z(here, -1), zero0)
        near = (below + above) + (row_below + row_above) + (z_below + z_above)
        diag = 3.0 * here + 0.5 * near
        inv = jnp.where(here > 0.0, WEIGHT / diag, zero0)
        half = 0.5 * inv
        w0[0, i] = half * (here + below)
        w0[1, i] = half * (here + above)
        w0[2, i] = half * (here + row_below)
        w0[3, i] = half * (here + row_above)
        w0[4, i] = jnp.where(lane0 > 0, half * (here + z_below), zero0)
        w0[5, i] = jnp.where(lane0 < 127, half * (here + z_above), zero0)
        g0[i] = inv
        dg0[i] = diag * (1.0 / WEIGHT)
        return here, above

    lax.fori_loop(1, 21, fine_weights, (d[0], d[1]), unroll=True)
    w0[0, 1] = zero0
    w0[1, 20] = zero0

    for copy in p_copies + s_copies:
        copy.wait_recv()

    def scale_source(i, _):
        g0[i] = g0[i] * s[i]
        return 0

    lax.fori_loop(1, 21, scale_source, 0, unroll=True)

    def fine_sum(i, below, here, above):
        total = g0[i] + w0[0, i] * below + w0[1, i] * above
        total = total + w0[2, i] * roll_y(here, 1) + w0[3, i] * roll_y(here, -1)
        return total + w0[4, i] * roll_z(here, 1) + w0[5, i] * roll_z(here, -1)

    def fine_sweep(src, dst, low, high):
        def plane(i, carry):
            below, here = carry
            above = src[i + 1]
            dst[i] = fine_sum(i, below, here, above) + KEEP * here
            return here, above

        lax.fori_loop(low, high, plane, (src[low - 1], src[low]), unroll=True)

    fine_sweep(p, v1, 1, 21)
    fine_sweep(v1, v2, 2, 20)

    def residual(pair, carry):
        below, here = carry
        above = v2[2 * pair + 4]
        beyond = v2[2 * pair + 5]
        first_half = (fine_sum(2 * pair + 3, below, here, above) - WEIGHT * here) * dg0[2 * pair + 3]
        second_half = (fine_sum(2 * pair + 4, here, above, beyond) - WEIGHT * above) * dg0[2 * pair + 4]
        xs[pair] = (first_half + second_half)[0:32]
        return above, beyond

    lax.fori_loop(0, 8, residual, (v2[2], v2[3]), unroll=True)
    b1[2:6, 0:16] = 0.125 * pack_pairs(
        xs[0:8, pl.ds(0, 16, stride=2), :] + xs[0:8, pl.ds(1, 16, stride=2), :]
    )
    b1_copies = [
        remote(
            b1.at[send_range(dx, 2, 4, 2), send_range(dy, 0, 16, 4)],
            b1.at[planes_to(dx, 2, 4, 2), rows_to(dy, 16, 4)],
            b1_sem, k, dx, dy,
        )
        for k, (dx, dy) in enumerate(DIRS)
    ]
    f_copies = fine_copies(v2, fh, f_sem, 2)
    for copy in b1_copies:
        copy.start()

    for copy in l1_copies:
        copy.wait_recv()
    for copy in c2_copies:
        copy.start()
    inv1 = l1[3]
    coarse_weights(w1, l1, inv1, 2, 0.25)

    for copy in d_copies + p_copies + s_copies + d_onward + p_onward + s_onward:
        copy.wait_send()
    for copy in b1_copies:
        copy.wait_recv()
    g1 = l1[3] * b1[...]
    err1 = g1
    err1 = (g1 + KEEP * err1) + coarse_sum(w1, err1, 2)
    res1 = ((g1 - WEIGHT * err1) + coarse_sum(w1, err1, 2))[2:6, 0:16] * dg1[...]
    xs[0:4, 0:16] = res1
    b2[2, 8:16] = 0.125 * pack_groups(
        xs[0:4, pl.ds(0, 8, stride=2), :] + xs[0:4, pl.ds(1, 8, stride=2), :]
    )
    b2_copies = [
        remote(
            b2.at[2, far_rows(dx, dy, 0)], b2.at[2 - dx, far_rows(dx, dy, -8 * dy)],
            b2_sem, k, dx, dy,
        )
        for k, (dx, dy) in enumerate(FAR)
    ]
    for copy in b2_copies + f_copies:
        copy.start()
    for copy in c2_copies:
        copy.wait_recv()
    inv2 = c2[3]
    coarse_weights(w2, c2, inv2, 4, 0.0625)

    for copy in l1_copies + c2_copies + b1_copies:
        copy.wait_send()
    for copy in b2_copies:
        copy.wait_recv()
    g2 = c2[3] * b2[...]
    err2 = g2
    for _ in range(COARSE_SWEEPS - 3):
        err2 = (g2 + KEEP * err2) + coarse_sum(w2, err2, 4)
    w2_middle = [w2[k, 1:4] for k in range(6)]
    g2 = g2[1:4]
    total = weighted_sum(w2_middle, err2[1:4], err2[0:3], err2[2:5], 4)
    err2 = (g2 + KEEP * err2[1:4]) + total
    for _ in range(2):
        err2 = (g2 + KEEP * err2) + coarse_sum(w2_middle, err2, 4)

    row = lax.broadcasted_iota(jnp.int32, (8, 128), 0)

    def put(pair, value):
        centre = value[8:16]
        sides = jnp.where(row < 2, value[16:24], roll_y(value[0:8], 4))
        for parity in range(2):
            e1[pair, pl.ds(parity, 8, stride=2), :] = centre
            e1[pair, pl.ds(16 + parity, 8, stride=2), :] = sides

    before, centre, after = spread_groups(err2[0]), spread_groups(err2[1]), spread_groups(err2[2])
    for pair, value in enumerate(before[2:4] + centre + after[0:2]):
        put(pair, value)
    g1 = l1[3] * b1[...]
    err1 = err1 + e1[:, 0:24]
    for _ in range(POST):
        err1 = (g1 + KEEP * err1) + coarse_sum(w1, err1, 2)

    def put_fine(index, value):
        sides = jnp.where(row < 2, value[16:24], roll_y(value[16:24], 4))
        for parity in range(2):
            e0[index, pl.ds(parity, 16, stride=2), :] = value[0:16]
            e0[index, pl.ds(32 + parity, 8, stride=2), :] = sides

    for pair in range(1, 7):
        even_cell, odd_cell = spread_pairs(err1[pair])
        if pair > 1:
            put_fine(2 * pair - 3, even_cell)
        if pair < 6:
            put_fine(2 * pair - 2, odd_cell)

    for copy in f_copies + b2_copies:
        copy.wait_send()
    for copy in f_copies:
        copy.wait_recv()

    def correct(i, _):
        halves = (2 * i + 1, 2 * i + 2)
        add = e0[i]
        for plane in halves:
            v1[plane, 0:32] = v2[plane, 0:32] + add[0:32]
            v1[plane, 32:40] = fh[plane, 32:40] + add[32:40]
        return 0

    for i in (0, 9):
        for plane in (2 * i + 1, 2 * i + 2):
            v1[plane] = fh[plane] + e0[i, 0:40]
    lax.fori_loop(1, 9, correct, 0, unroll=True)

    fine_sweep(v1, fh, 2, 20)

    def last_sweep(i, carry):
        below, here = carry
        above = fh[i + 1]
        out[i - 3] = (fine_sum(i, below, here, above) + KEEP * here)[0:32]
        return here, above

    carry = (fh[2], fh[3])
    stores = []
    for k in range(4):
        carry = lax.fori_loop(4 * k + 3, 4 * k + 7, last_sweep, carry, unroll=True)
        part = pl.ds(4 * k, 4)
        stores.append(pltpu.make_async_copy(out.at[part], o_hbm.at[part], local_sem.at[3 + k]))
        stores[-1].start()
    for store in stores:
        store.wait()


def solution(mesh):
    sizes = (mesh.shape["blk"], mesh.shape["sub"])

    def on_device(pressure, source, inv_density):
        def vmem(*shape):
            return pltpu.VMEM(shape, jnp.float32)

        near, far = len(DIRS), len(FAR)
        return pl.pallas_call(
            functools.partial(kernel, sizes),
            out_shape=jax.ShapeDtypeStruct((16, 32, 128), jnp.float32),
            in_specs=[pl.BlockSpec(memory_space=pltpu.HBM)] * 3,
            out_specs=pl.BlockSpec(memory_space=pl.ANY),
            scratch_shapes=[
                vmem(22, 40, 128), vmem(22, 40, 128), vmem(22, 40, 128), vmem(2, 2, 32, 128),
                vmem(22, 40, 128), vmem(22, 40, 128), vmem(22, 40, 128),
                vmem(22, 40, 128), vmem(22, 40, 128), vmem(22, 40, 128),
                vmem(16, 32, 128), vmem(6, 22, 40, 128), vmem(22, 40, 128), vmem(22, 40, 128),
                vmem(10, 32, 128), vmem(8, 48, 128), vmem(6, 4, 16, 128),
                vmem(4, 8, 24, 128), vmem(6, 8, 24, 128), vmem(8, 24, 128), vmem(4, 16, 128),
                vmem(4, 5, 24, 128), vmem(6, 5, 24, 128), vmem(5, 24, 128),
                vmem(8, 32, 128), vmem(10, 48, 128),
                pltpu.SemaphoreType.DMA((7,)),
                pltpu.SemaphoreType.DMA((2, near)), pltpu.SemaphoreType.DMA((2, near)), pltpu.SemaphoreType.DMA((2, near)),
                pltpu.SemaphoreType.DMA((2, near)), pltpu.SemaphoreType.DMA((2, near)),
                pltpu.SemaphoreType.DMA((2, near)), pltpu.SemaphoreType.DMA((2, near)),
                pltpu.SemaphoreType.DMA((2, near)), pltpu.SemaphoreType.DMA((2, near)),
                pltpu.SemaphoreType.DMA((2, far)), pltpu.SemaphoreType.DMA((2, far)),
            ],
            compiler_params=pltpu.CompilerParams(
                collective_id=0, has_side_effects=True, vmem_limit_bytes=54850 * 1024
            ),
        )(pressure, source, inv_density)

    return jax.shard_map(
        on_device,
        mesh=mesh,
        in_specs=(P("blk", "sub", None),) * 3,
        out_specs=P("blk", "sub", None),
        check_vma=False,
    )
```

```python
import functools

import jax
import jax.numpy as jnp
from jax import lax
from jax.experimental import pallas as pl
from jax.experimental.pallas import tpu as pltpu
from jax.sharding import PartitionSpec as P

MESH = pl.DeviceIdType.MESH
PRE = 2
POST = 2
COARSE_SWEEPS = 6
WEIGHT = 0.8
KEEP = 1.0 - WEIGHT

DIRS = [(-1, -1), (1, 1), (-1, 1), (1, -1), (-1, 0), (1, 0), (0, -1), (0, 1)]
FAR = [(-2, -1), (2, 1), (-2, 1), (2, -1), (-2, 0), (2, 0)] + DIRS


def send_range(step, first, count, width):
    if step == 0:
        return pl.ds(first, count)
    return pl.ds(first + count - width, width) if step > 0 else pl.ds(first, width)


def planes_to(step, first, count, width):
    if step == 0:
        return pl.ds(first, count)
    return pl.ds(first - width, width) if step > 0 else pl.ds(first + count, width)


def rows_to(step, count, width):
    if step == 0:
        return pl.ds(0, count)
    return pl.ds(count + width, width) if step > 0 else pl.ds(count, width)


def far_rows(dx, dy, shift):
    if abs(dx) + abs(dy) == 3:
        return pl.ds(8 + shift + (4 if dy > 0 else 0), 4)
    return pl.ds(8 + shift, 8)


def lanes(shape):
    return lax.broadcasted_iota(jnp.int32, shape, len(shape) - 1)


def roll_z(value, shift):
    return pltpu.roll(value, shift % 128, value.ndim - 1)


def roll_y(value, shift):
    return pltpu.roll(value, shift % value.shape[-2], value.ndim - 2)


def pack_pairs(value):
    split = value.reshape((value.shape[0] // 2, 2) + value.shape[1:])
    even, odd = split[:, 0], split[:, 1]
    mask = lanes(even.shape) % 2 == 0
    return jnp.where(mask, even + roll_z(even, -1), odd + roll_z(odd, 1))


def pack_groups(value):
    lane = lanes(value.shape[1:])
    low = jnp.where(lane % 2 == 0, value[0] + roll_z(value[0], -1), value[1] + roll_z(value[1], 1))
    high = jnp.where(lane % 2 == 0, value[2] + roll_z(value[2], -1), value[3] + roll_z(value[3], 1))
    return jnp.where(lane % 4 < 2, low + roll_z(low, -2), high + roll_z(high, 2))


def spread_pairs(value):
    mask = lanes(value.shape) % 2 == 0
    return jnp.where(mask, value, roll_z(value, 1)), jnp.where(mask, roll_z(value, -1), value)


def spread_groups(value):
    mask = lanes(value.shape) % 4 < 2
    low = jnp.where(mask, value, roll_z(value, 2))
    high = jnp.where(mask, roll_z(value, -2), value)
    return spread_pairs(low) + spread_pairs(high)


def ahead(value):
    return jnp.concatenate([value[1:], value[:1]], axis=0)


def behind(value):
    return jnp.concatenate([value[-1:], value[:-1]], axis=0)


def x_up(value, following, group):
    mask = lanes(value.shape) % group < group - 1
    return jnp.where(mask, roll_z(value, -1), roll_z(following, group - 1))


def x_down(value, previous, group):
    mask = lanes(value.shape) % group > 0
    return jnp.where(mask, roll_z(value, 1), roll_z(previous, 1 - group))


def coarse_weights(w, faces, inv, group, scale):
    half = scale * inv
    w[0] = half * faces[0]
    w[1] = half * x_up(faces[0], ahead(faces[0]), group)
    w[2] = half * faces[1]
    w[3] = half * roll_y(faces[1], -1)
    w[4] = half * faces[2]
    w[5] = half * roll_z(faces[2], -group)


def coarse_sum(w, value, group):
    return weighted_sum(w, value, behind(value), ahead(value), group)


def weighted_sum(w, value, previous, following, group):
    across = w[0] * x_down(value, previous, group) + w[1] * x_up(value, following, group)
    along = w[2] * roll_y(value, 1) + w[3] * roll_y(value, -1)
    return (along + (w[4] * roll_z(value, group) + w[5] * roll_z(value, -group))) + across


class Halo:
    def __init__(self, copy, sends, receives):
        self.copy, self.sends, self.receives = copy, sends, receives

    def start(self):
        pl.when(self.sends)(self.copy.start)

    def wait_send(self):
        pl.when(self.sends)(self.copy.wait_send)

    def wait_recv(self):
        pl.when(self.receives)(self.copy.wait_recv)


def kernel(
    sizes, p_hbm, s_hbm, d_hbm, o_hbm,
    ps, d, sx, v1, v2, fh, out, w0, g0, dg0,
    xs, ys, cs, l1, w1, b1, dg1, c2, w2, b2, e1, e0,
    local_sem, d_sem, ps_sem, f_sem, l1_sem, b1_sem, c2_sem, b2_sem,
):
    n_blk, n_sub = sizes
    p, s = ps.at[0], ps.at[1]
    ib, iy = lax.axis_index("blk"), lax.axis_index("sub")

    def peer(dx, dy):
        return {"blk": ib + dx, "sub": iy + dy}

    def there(dx, dy):
        known = []
        if dx:
            known.append(ib >= -dx if dx < 0 else ib < n_blk - dx)
        if dy:
            known.append(iy >= -dy if dy < 0 else iy < n_sub - dy)
        return functools.reduce(jnp.logical_and, known)

    def remote(src, dst, sem, k, dx, dy):
        return Halo(
            pltpu.make_async_remote_copy(
                src_ref=src, dst_ref=dst, send_sem=sem.at[0, k], recv_sem=sem.at[1, k],
                device_id=peer(dx, dy), device_id_type=MESH,
            ),
            there(dx, dy),
            there(-dx, -dy),
        )

    def clear_outside(ref, lead, x_side, x_count, rows, low_rows, high_rows):
        planes = x_count + 2 * x_side
        slab = jnp.zeros(lead + (x_side, rows, 128), jnp.float32)
        strip = jnp.zeros(lead + (planes, low_rows[1], 128), jnp.float32)
        every = (slice(None),) * len(lead)

        @pl.when(ib == 0)
        def _():
            ref[every + (slice(0, x_side),)] = slab

        @pl.when(ib == n_blk - 1)
        def _():
            ref[every + (slice(x_side + x_count, planes),)] = slab

        @pl.when(iy == 0)
        def _():
            ref[every + (slice(None), slice(low_rows[0], low_rows[0] + low_rows[1]))] = strip

        @pl.when(iy == n_sub - 1)
        def _():
            ref[every + (slice(None), slice(high_rows[0], high_rows[0] + high_rows[1]))] = strip

    barrier = pltpu.get_barrier_semaphore()
    for dx, dy in DIRS:
        @pl.when(there(dx, dy))
        def _():
            pl.semaphore_signal(barrier, inc=1, device_id=peer(dx, dy), device_id_type=MESH)

    local = [
        pltpu.make_async_copy(src, dst.at[pl.ds(3, 16), pl.ds(0, 32)], local_sem.at[k])
        for k, (src, dst) in enumerate(((d_hbm, d), (p_hbm, p), (s_hbm, s)))
    ]
    for copy in local:
        copy.start()
    for ref in (d, fh):
        clear_outside(ref, (), 3, 16, 40, (36, 4), (32, 4))
    clear_outside(ps, (2,), 3, 16, 40, (36, 4), (32, 4))
    clear_outside(l1, (4,), 2, 4, 24, (20, 4), (16, 4))
    clear_outside(b1, (), 2, 4, 24, (20, 4), (16, 4))
    for index in (0, 1, 3, 4):
        @pl.when((ib + (index - 2) < 0) | (ib + (index - 2) >= n_blk))
        def _():
            c2[:, index] = jnp.zeros((4, 24, 128), jnp.float32)
            b2[index] = jnp.zeros((24, 128), jnp.float32)

    for edge, first in ((0, 0), (n_sub - 1, 16)):
        @pl.when(iy == edge)
        def _():
            c2[:, :, first:first + 8] = jnp.zeros((4, 5, 8, 128), jnp.float32)
            b2[:, first:first + 8] = jnp.zeros((5, 8, 128), jnp.float32)

    for copy in local:
        copy.wait()
    def joined(plane, beyond):
        face = 0.5 * (d[plane, 0:32] + d[beyond, 0:32])
        return s[plane, 0:32] + face * p[beyond, 0:32]

    sx[0, 0] = p[3:5, 0:32]
    sx[0, 1, 0] = s[3, 0:32]
    sx[0, 1, 1] = joined(4, 5)
    sx[1, 0] = p[17:19, 0:32]
    sx[1, 1, 0] = joined(17, 16)
    sx[1, 1, 1] = s[18, 0:32]
    p[0] = jnp.zeros((40, 128), jnp.float32)
    p[21] = jnp.zeros((40, 128), jnp.float32)

    across = 1 + (ib > 0).astype(jnp.int32) + (ib < n_blk - 1).astype(jnp.int32)
    along = 1 + (iy > 0).astype(jnp.int32) + (iy < n_sub - 1).astype(jnp.int32)
    pl.semaphore_wait(barrier, across * along - 1)

    def fine_copies(src, dst, sem, width):
        copies = []
        for k, (dx, dy) in enumerate(DIRS):
            count = width - abs(dy)
            block = src.at[send_range(dx, 3, 16, count), send_range(dy, 0, 32, 4)]
            target = dst.at[planes_to(dx, 3, 16, count), rows_to(dy, 32, 4)]
            copies.append(remote(block, target, sem, k, dx, dy))
        return copies

    d_copies = fine_copies(d, d, d_sem, 3)
    ps_copies = []
    for k, (dx, dy) in enumerate(DIRS):
        block = ps.at[:, send_range(dx, 3, 16, 2), send_range(dy, 0, 32, 4)]
        if dy == 0:
            block = sx.at[0 if dx < 0 else 1]
        target = ps.at[:, planes_to(dx, 3, 16, 2), rows_to(dy, 32, 4)]
        ps_copies.append(remote(block, target, ps_sem, k, dx, dy))
    for copy in d_copies + ps_copies:
        copy.start()

    for copy in d_copies:
        copy.wait_recv()

    def x_face(i, _):
        xs[i] = d[2 * i + 2, 0:32] + d[2 * i + 3, 0:32]
        return 0

    lax.fori_loop(0, 10, x_face, 0, unroll=True)

    def x_pair(i, _):
        both = d[2 * i + 3] + d[2 * i + 4]
        ys[i, 0:8] = both[32:40]
        ys[i, 8:48] = both
        return 0

    lax.fori_loop(0, 8, x_pair, 0, unroll=True)

    lane1 = lanes((4, 16, 128))
    faces_x = 0.125 * pack_pairs(xs[:, pl.ds(0, 16, stride=2), :] + xs[:, pl.ds(1, 16, stride=2), :])
    lx = faces_x[0:4]
    ux = x_up(lx, faces_x[1:5], 2)
    odd_before = ys[:, pl.ds(7, 16, stride=2), :]
    even = ys[:, pl.ds(8, 16, stride=2), :]
    odd = ys[:, pl.ds(9, 16, stride=2), :]
    even_after = ys[:, pl.ds(10, 16, stride=2), :]
    ly = 0.125 * pack_pairs(even + odd_before)
    uy = 0.125 * pack_pairs(odd + even_after)
    both = (even + odd).reshape(4, 2, 16, 128)
    b_even, b_odd = both[:, 0], both[:, 1]
    first, last = lane1 < 2, lane1 >= 126
    zero1 = jnp.zeros((4, 16, 128), jnp.float32)
    is_even = lane1 % 2 == 0
    lz = 0.125 * (
        jnp.where(is_even, b_even, roll_z(b_odd, 1))
        + jnp.where(first, zero1, jnp.where(is_even, roll_z(b_even, 1), roll_z(b_odd, 2)))
    )
    uz = 0.125 * (
        jnp.where(is_even, roll_z(b_even, -1), b_odd)
        + jnp.where(last, zero1, jnp.where(is_even, roll_z(b_even, -2), roll_z(b_odd, -1)))
    )
    diag1 = 0.25 * (lx + ux + ly + uy + lz + uz)
    dg1[...] = diag1 * (1.0 / WEIGHT)
    l1[0, 2:6, 0:16] = lx
    l1[1, 2:6, 0:16] = ly
    l1[2, 2:6, 0:16] = jnp.where(first, zero1, lz)
    l1[3, 2:6, 0:16] = WEIGHT / diag1

    l1_copies = [
        remote(
            l1.at[:, send_range(dx, 2, 4, 2), send_range(dy, 0, 16, 4)],
            l1.at[:, planes_to(dx, 2, 4, 2), rows_to(dy, 16, 4)],
            l1_sem, k, dx, dy,
        )
        for k, (dx, dy) in enumerate(DIRS)
    ]
    for copy in l1_copies:
        copy.start()

    for k, face in enumerate((lx, ux, ly, uy, lz, uz)):
        cs[k] = face

    def rows_of(k, parity):
        return cs[k, :, pl.ds(parity, 8, stride=2), :]

    lane2 = lanes((4, 8, 128))
    zero2 = jnp.zeros((4, 8, 128), jnp.float32)
    lx2 = jnp.where(lane2 % 2 == 0, rows_of(0, 0) + rows_of(0, 1), zero2)
    ux2 = jnp.where(lane2 % 2 == 1, rows_of(1, 0) + rows_of(1, 1), zero2)
    ly2 = rows_of(2, 0)
    uy2 = rows_of(3, 1)
    lz2 = jnp.where(lane2 % 4 < 2, rows_of(4, 0) + rows_of(4, 1), zero2)
    uz2 = jnp.where(lane2 % 4 >= 2, rows_of(5, 0) + rows_of(5, 1), zero2)
    diag2 = (0.0625 * 0.25) * pack_groups(lx2 + ux2 + ly2 + uy2 + lz2 + uz2)
    c2[0, 2, 8:16] = 0.25 * pack_groups(lx2)
    c2[1, 2, 8:16] = 0.25 * pack_groups(ly2)
    c2[2, 2, 8:16] = jnp.where(lanes((8, 128)) < 4, 0.0, 0.25 * pack_groups(lz2))
    c2[3, 2, 8:16] = WEIGHT / diag2

    c2_copies = [
        remote(
            c2.at[:, 2, far_rows(dx, dy, 0)], c2.at[:, 2 - dx, far_rows(dx, dy, -8 * dy)],
            c2_sem, k, dx, dy,
        )
        for k, (dx, dy) in enumerate(FAR)
    ]
    lane0 = lanes((40, 128))
    zero0 = jnp.zeros((40, 128), jnp.float32)

    def fine_weights(i, carry):
        below, here = carry
        above = d[i + 1]
        row_below, row_above = roll_y(here, 1), roll_y(here, -1)
        z_below = jnp.where(lane0 > 0, roll_z(here, 1), zero0)
        z_above = jnp.where(lane0 < 127, roll_z(here, -1), zero0)
        near = (below + above) + (row_below + row_above) + (z_below + z_above)
        diag = 3.0 * here + 0.5 * near
        inv = jnp.where(here > 0.0, WEIGHT / diag, zero0)
        half = 0.5 * inv
        w0[0, i] = half * (here + below)
        w0[1, i] = half * (here + above)
        w0[2, i] = half * (here + row_below)
        w0[3, i] = half * (here + row_above)
        w0[4, i] = jnp.where(lane0 > 0, half * (here + z_below), zero0)
        w0[5, i] = jnp.where(lane0 < 127, half * (here + z_above), zero0)
        g0[i] = inv
        dg0[i] = diag * (1.0 / WEIGHT)
        return here, above

    lax.fori_loop(1, 21, fine_weights, (d[0], d[1]), unroll=True)
    w0[0, 1] = zero0
    w0[1, 20] = zero0

    for copy in ps_copies:
        copy.wait_recv()

    def scale_source(i, _):
        g0[i] = g0[i] * s[i]
        return 0

    lax.fori_loop(1, 21, scale_source, 0, unroll=True)

    def fine_sum(i, below, here, above):
        total = g0[i] + w0[0, i] * below + w0[1, i] * above
        total = total + w0[2, i] * roll_y(here, 1) + w0[3, i] * roll_y(here, -1)
        return total + w0[4, i] * roll_z(here, 1) + w0[5, i] * roll_z(here, -1)

    def fine_sweep(src, dst, low, high):
        def plane(i, carry):
            below, here = carry
            above = src[i + 1]
            dst[i] = fine_sum(i, below, here, above) + KEEP * here
            return here, above

        lax.fori_loop(low, high, plane, (src[low - 1], src[low]), unroll=True)

    fine_sweep(p, v1, 1, 21)
    fine_sweep(v1, v2, 2, 20)

    def residual(pair, carry):
        below, here = carry
        above = v2[2 * pair + 4]
        beyond = v2[2 * pair + 5]
        first_half = (fine_sum(2 * pair + 3, below, here, above) - WEIGHT * here) * dg0[2 * pair + 3]
        second_half = (fine_sum(2 * pair + 4, here, above, beyond) - WEIGHT * above) * dg0[2 * pair + 4]
        xs[pair] = (first_half + second_half)[0:32]
        return above, beyond

    lax.fori_loop(0, 8, residual, (v2[2], v2[3]), unroll=True)
    b1[2:6, 0:16] = 0.125 * pack_pairs(
        xs[0:8, pl.ds(0, 16, stride=2), :] + xs[0:8, pl.ds(1, 16, stride=2), :]
    )
    b1_copies = [
        remote(
            b1.at[send_range(dx, 2, 4, 2), send_range(dy, 0, 16, 4)],
            b1.at[planes_to(dx, 2, 4, 2), rows_to(dy, 16, 4)],
            b1_sem, k, dx, dy,
        )
        for k, (dx, dy) in enumerate(DIRS)
    ]
    f_copies = fine_copies(v2, fh, f_sem, 2)
    for copy in b1_copies + c2_copies:
        copy.start()

    for copy in l1_copies:
        copy.wait_recv()
    inv1 = l1[3]
    coarse_weights(w1, l1, inv1, 2, 0.25)

    for copy in d_copies + ps_copies:
        copy.wait_send()
    for copy in b1_copies:
        copy.wait_recv()
    g1 = l1[3] * b1[...]
    err1 = g1
    err1 = (g1 + KEEP * err1) + coarse_sum(w1, err1, 2)
    res1 = ((g1 - WEIGHT * err1) + coarse_sum(w1, err1, 2))[2:6, 0:16] * dg1[...]
    xs[0:4, 0:16] = res1
    b2[2, 8:16] = 0.125 * pack_groups(
        xs[0:4, pl.ds(0, 8, stride=2), :] + xs[0:4, pl.ds(1, 8, stride=2), :]
    )
    b2_copies = [
        remote(
            b2.at[2, far_rows(dx, dy, 0)], b2.at[2 - dx, far_rows(dx, dy, -8 * dy)],
            b2_sem, k, dx, dy,
        )
        for k, (dx, dy) in enumerate(FAR)
    ]
    for copy in b2_copies + f_copies:
        copy.start()
    for copy in c2_copies:
        copy.wait_recv()
    inv2 = c2[3]
    coarse_weights(w2, c2, inv2, 4, 0.0625)

    for copy in l1_copies + c2_copies + b1_copies:
        copy.wait_send()
    for copy in b2_copies:
        copy.wait_recv()
    g2 = c2[3] * b2[...]
    err2 = g2
    for _ in range(COARSE_SWEEPS - 3):
        err2 = (g2 + KEEP * err2) + coarse_sum(w2, err2, 4)
    w2_middle = [w2[k, 1:4] for k in range(6)]
    g2 = g2[1:4]
    total = weighted_sum(w2_middle, err2[1:4], err2[0:3], err2[2:5], 4)
    err2 = (g2 + KEEP * err2[1:4]) + total
    for _ in range(2):
        err2 = (g2 + KEEP * err2) + coarse_sum(w2_middle, err2, 4)

    row = lax.broadcasted_iota(jnp.int32, (8, 128), 0)

    def put(pair, value):
        centre = value[8:16]
        sides = jnp.where(row < 2, value[16:24], roll_y(value[0:8], 4))
        for parity in range(2):
            e1[pair, pl.ds(parity, 8, stride=2), :] = centre
            e1[pair, pl.ds(16 + parity, 8, stride=2), :] = sides

    before, centre, after = spread_groups(err2[0]), spread_groups(err2[1]), spread_groups(err2[2])
    for pair, value in enumerate(before[2:4] + centre + after[0:2]):
        put(pair, value)
    g1 = l1[3] * b1[...]
    err1 = err1 + e1[:, 0:24]
    for _ in range(POST):
        err1 = (g1 + KEEP * err1) + coarse_sum(w1, err1, 2)

    def put_fine(index, value):
        sides = jnp.where(row < 2, value[16:24], roll_y(value[16:24], 4))
        for parity in range(2):
            e0[index, pl.ds(parity, 16, stride=2), :] = value[0:16]
            e0[index, pl.ds(32 + parity, 8, stride=2), :] = sides

    for pair in range(1, 7):
        even_cell, odd_cell = spread_pairs(err1[pair])
        if pair > 1:
            put_fine(2 * pair - 3, even_cell)
        if pair < 6:
            put_fine(2 * pair - 2, odd_cell)

    for copy in f_copies + b2_copies:
        copy.wait_send()
    for copy in f_copies:
        copy.wait_recv()

    def correct(i, _):
        halves = (2 * i + 1, 2 * i + 2)
        add = e0[i]
        for plane in halves:
            v1[plane, 0:32] = v2[plane, 0:32] + add[0:32]
            v1[plane, 32:40] = fh[plane, 32:40] + add[32:40]
        return 0

    for i in (0, 9):
        for plane in (2 * i + 1, 2 * i + 2):
            v1[plane] = fh[plane] + e0[i, 0:40]
    lax.fori_loop(1, 9, correct, 0, unroll=True)

    fine_sweep(v1, fh, 2, 20)

    def last_sweep(i, carry):
        below, here = carry
        above = fh[i + 1]
        out[i - 3] = (fine_sum(i, below, here, above) + KEEP * here)[0:32]
        return here, above

    carry = (fh[2], fh[3])
    stores = []
    for k, (low, high) in enumerate(((0, 6), (6, 11), (11, 14), (14, 16))):
        carry = lax.fori_loop(low + 3, high + 3, last_sweep, carry, unroll=True)
        part = pl.ds(low, high - low)
        stores.append(pltpu.make_async_copy(out.at[part], o_hbm.at[part], local_sem.at[3 + k]))
        stores[-1].start()
    for store in stores:
        store.wait()


def solution(mesh):
    sizes = (mesh.shape["blk"], mesh.shape["sub"])

    def on_device(pressure, source, inv_density):
        def vmem(*shape):
            return pltpu.VMEM(shape, jnp.float32)

        near, far = len(DIRS), len(FAR)
        return pl.pallas_call(
            functools.partial(kernel, sizes),
            out_shape=jax.ShapeDtypeStruct((16, 32, 128), jnp.float32),
            in_specs=[pl.BlockSpec(memory_space=pltpu.HBM)] * 3,
            out_specs=pl.BlockSpec(memory_space=pl.ANY),
            scratch_shapes=[
                vmem(2, 22, 40, 128), vmem(22, 40, 128), vmem(2, 2, 2, 32, 128),
                vmem(22, 40, 128), vmem(22, 40, 128), vmem(22, 40, 128),
                vmem(16, 32, 128), vmem(6, 22, 40, 128), vmem(22, 40, 128), vmem(22, 40, 128),
                vmem(10, 32, 128), vmem(8, 48, 128), vmem(6, 4, 16, 128),
                vmem(4, 8, 24, 128), vmem(6, 8, 24, 128), vmem(8, 24, 128), vmem(4, 16, 128),
                vmem(4, 5, 24, 128), vmem(6, 5, 24, 128), vmem(5, 24, 128),
                vmem(8, 32, 128), vmem(10, 48, 128),
                pltpu.SemaphoreType.DMA((7,)),
                pltpu.SemaphoreType.DMA((2, near)), pltpu.SemaphoreType.DMA((2, near)),
                pltpu.SemaphoreType.DMA((2, near)), pltpu.SemaphoreType.DMA((2, near)),
                pltpu.SemaphoreType.DMA((2, near)),
                pltpu.SemaphoreType.DMA((2, far)), pltpu.SemaphoreType.DMA((2, far)),
            ],
            compiler_params=pltpu.CompilerParams(
                collective_id=0, has_side_effects=True, vmem_limit_bytes=54850 * 1024
            ),
        )(pressure, source, inv_density)

    return jax.shard_map(
        on_device,
        mesh=mesh,
        in_specs=(P("blk", "sub", None),) * 3,
        out_specs=P("blk", "sub", None),
        check_vma=False,
    )
```

```python
import functools

import jax
import jax.numpy as jnp
from jax import lax
from jax.experimental import pallas as pl
from jax.experimental.pallas import tpu as pltpu
from jax.sharding import PartitionSpec as P

MESH = pl.DeviceIdType.MESH
PRE = 2
POST = 2
COARSE_SWEEPS = 6
WEIGHT = 0.8
KEEP = 1.0 - WEIGHT

DIRS = [(-1, -1), (1, 1), (-1, 1), (1, -1), (-1, 0), (1, 0), (0, -1), (0, 1)]
FAR = [(-2, -1), (2, 1), (-2, 1), (2, -1), (-2, 0), (2, 0)] + DIRS


def send_range(step, first, count, width):
    if step == 0:
        return pl.ds(first, count)
    return pl.ds(first + count - width, width) if step > 0 else pl.ds(first, width)


def planes_to(step, first, count, width):
    if step == 0:
        return pl.ds(first, count)
    return pl.ds(first - width, width) if step > 0 else pl.ds(first + count, width)


def rows_to(step, count, width):
    if step == 0:
        return pl.ds(0, count)
    return pl.ds(count + width, width) if step > 0 else pl.ds(count, width)


def far_rows(dx, dy, shift):
    if abs(dx) + abs(dy) == 3:
        return pl.ds(8 + shift + (4 if dy > 0 else 0), 4)
    return pl.ds(8 + shift, 8)


def lanes(shape):
    return lax.broadcasted_iota(jnp.int32, shape, len(shape) - 1)


def roll_z(value, shift):
    return pltpu.roll(value, shift % 128, value.ndim - 1)


def roll_y(value, shift):
    return pltpu.roll(value, shift % value.shape[-2], value.ndim - 2)


def pack_pairs(value):
    split = value.reshape((value.shape[0] // 2, 2) + value.shape[1:])
    even, odd = split[:, 0], split[:, 1]
    mask = lanes(even.shape) % 2 == 0
    return jnp.where(mask, even + roll_z(even, -1), odd + roll_z(odd, 1))


def pack_groups(value):
    lane = lanes(value.shape[1:])
    low = jnp.where(lane % 2 == 0, value[0] + roll_z(value[0], -1), value[1] + roll_z(value[1], 1))
    high = jnp.where(lane % 2 == 0, value[2] + roll_z(value[2], -1), value[3] + roll_z(value[3], 1))
    return jnp.where(lane % 4 < 2, low + roll_z(low, -2), high + roll_z(high, 2))


def spread_pairs(value):
    mask = lanes(value.shape) % 2 == 0
    return jnp.where(mask, value, roll_z(value, 1)), jnp.where(mask, roll_z(value, -1), value)


def spread_groups(value):
    mask = lanes(value.shape) % 4 < 2
    low = jnp.where(mask, value, roll_z(value, 2))
    high = jnp.where(mask, roll_z(value, -2), value)
    return spread_pairs(low) + spread_pairs(high)


def ahead(value):
    return jnp.concatenate([value[1:], value[:1]], axis=0)


def behind(value):
    return jnp.concatenate([value[-1:], value[:-1]], axis=0)


def x_up(value, following, group):
    mask = lanes(value.shape) % group < group - 1
    return jnp.where(mask, roll_z(value, -1), roll_z(following, group - 1))


def x_down(value, previous, group):
    mask = lanes(value.shape) % group > 0
    return jnp.where(mask, roll_z(value, 1), roll_z(previous, 1 - group))


def coarse_weights(w, faces, inv, group, scale):
    half = scale * inv
    w[0] = half * faces[0]
    w[1] = half * x_up(faces[0], ahead(faces[0]), group)
    w[2] = half * faces[1]
    w[3] = half * roll_y(faces[1], -1)
    w[4] = half * faces[2]
    w[5] = half * roll_z(faces[2], -group)


def coarse_sum(w, value, group):
    return weighted_sum(w, value, behind(value), ahead(value), group)


def weighted_sum(w, value, previous, following, group):
    across = w[0] * x_down(value, previous, group) + w[1] * x_up(value, following, group)
    along = w[2] * roll_y(value, 1) + w[3] * roll_y(value, -1)
    return (along + (w[4] * roll_z(value, group) + w[5] * roll_z(value, -group))) + across


class Halo:
    def __init__(self, copy, sends, receives):
        self.copy, self.sends, self.receives = copy, sends, receives

    def start(self):
        pl.when(self.sends)(self.copy.start)

    def wait_send(self):
        pl.when(self.sends)(self.copy.wait_send)

    def wait_recv(self):
        pl.when(self.receives)(self.copy.wait_recv)


def kernel(
    sizes, p_hbm, s_hbm, d_hbm, o_hbm,
    ps, d, sx, v1, v2, fh, out, w0, g0, dg0,
    xs, ys, cs, l1, w1, b1, dg1, c2, w2, b2, e1, e0,
    local_sem, d_sem, ps_sem, f_sem, l1_sem, b1_sem, c2_sem, b2_sem,
):
    n_blk, n_sub = sizes
    p, s = ps.at[0], ps.at[1]
    ib, iy = lax.axis_index("blk"), lax.axis_index("sub")

    def peer(dx, dy):
        return {"blk": ib + dx, "sub": iy + dy}

    def there(dx, dy):
        known = []
        if dx:
            known.append(ib >= -dx if dx < 0 else ib < n_blk - dx)
        if dy:
            known.append(iy >= -dy if dy < 0 else iy < n_sub - dy)
        return functools.reduce(jnp.logical_and, known)

    def remote(src, dst, sem, k, dx, dy):
        return Halo(
            pltpu.make_async_remote_copy(
                src_ref=src, dst_ref=dst, send_sem=sem.at[0, k], recv_sem=sem.at[1, k],
                device_id=peer(dx, dy), device_id_type=MESH,
            ),
            there(dx, dy),
            there(-dx, -dy),
        )

    def clear_outside(ref, lead, x_side, x_count, rows, low_rows, high_rows):
        planes = x_count + 2 * x_side
        slab = jnp.zeros(lead + (x_side, rows, 128), jnp.float32)
        strip = jnp.zeros(lead + (planes, low_rows[1], 128), jnp.float32)
        every = (slice(None),) * len(lead)

        @pl.when(ib == 0)
        def _():
            ref[every + (slice(0, x_side),)] = slab

        @pl.when(ib == n_blk - 1)
        def _():
            ref[every + (slice(x_side + x_count, planes),)] = slab

        @pl.when(iy == 0)
        def _():
            ref[every + (slice(None), slice(low_rows[0], low_rows[0] + low_rows[1]))] = strip

        @pl.when(iy == n_sub - 1)
        def _():
            ref[every + (slice(None), slice(high_rows[0], high_rows[0] + high_rows[1]))] = strip

    barrier = pltpu.get_barrier_semaphore()
    for dx, dy in DIRS:
        @pl.when(there(dx, dy))
        def _():
            pl.semaphore_signal(barrier, inc=1, device_id=peer(dx, dy), device_id_type=MESH)

    local = [
        pltpu.make_async_copy(src, dst.at[pl.ds(3, 16), pl.ds(0, 32)], local_sem.at[k])
        for k, (src, dst) in enumerate(((d_hbm, d), (p_hbm, p), (s_hbm, s)))
    ]
    for copy in local:
        copy.start()
    for ref in (d, fh):
        clear_outside(ref, (), 3, 16, 40, (36, 4), (32, 4))
    clear_outside(ps, (2,), 3, 16, 40, (36, 4), (32, 4))
    clear_outside(l1, (4,), 2, 4, 24, (20, 4), (16, 4))
    clear_outside(b1, (), 2, 4, 24, (20, 4), (16, 4))
    for index in (0, 1, 3, 4):
        @pl.when((ib + (index - 2) < 0) | (ib + (index - 2) >= n_blk))
        def _():
            c2[:, index] = jnp.zeros((4, 24, 128), jnp.float32)
            b2[index] = jnp.zeros((24, 128), jnp.float32)

    for edge, first in ((0, 0), (n_sub - 1, 16)):
        @pl.when(iy == edge)
        def _():
            c2[:, :, first:first + 8] = jnp.zeros((4, 5, 8, 128), jnp.float32)
            b2[:, first:first + 8] = jnp.zeros((5, 8, 128), jnp.float32)

    local[0].wait()
    across = 1 + (ib > 0).astype(jnp.int32) + (ib < n_blk - 1).astype(jnp.int32)
    along = 1 + (iy > 0).astype(jnp.int32) + (iy < n_sub - 1).astype(jnp.int32)
    pl.semaphore_wait(barrier, across * along - 1)

    def fine_copies(src, dst, sem, width):
        copies = []
        for k, (dx, dy) in enumerate(DIRS):
            count = width - abs(dy)
            block = src.at[send_range(dx, 3, 16, count), send_range(dy, 0, 32, 4)]
            target = dst.at[planes_to(dx, 3, 16, count), rows_to(dy, 32, 4)]
            copies.append(remote(block, target, sem, k, dx, dy))
        return copies

    d_copies = fine_copies(d, d, d_sem, 3)
    for copy in d_copies:
        copy.start()
    for copy in local[1:]:
        copy.wait()

    def joined(plane, beyond):
        face = 0.5 * (d[plane, 0:32] + d[beyond, 0:32])
        return s[plane, 0:32] + face * p[beyond, 0:32]

    sx[0, 0] = p[3:5, 0:32]
    sx[0, 1, 0] = s[3, 0:32]
    sx[0, 1, 1] = joined(4, 5)
    sx[1, 0] = p[17:19, 0:32]
    sx[1, 1, 0] = joined(17, 16)
    sx[1, 1, 1] = s[18, 0:32]
    p[0] = jnp.zeros((40, 128), jnp.float32)
    p[21] = jnp.zeros((40, 128), jnp.float32)

    ps_copies = []
    for k, (dx, dy) in enumerate(DIRS):
        block = ps.at[:, send_range(dx, 3, 16, 2), send_range(dy, 0, 32, 4)]
        if dy == 0:
            block = sx.at[0 if dx < 0 else 1]
        target = ps.at[:, planes_to(dx, 3, 16, 2), rows_to(dy, 32, 4)]
        ps_copies.append(remote(block, target, ps_sem, k, dx, dy))
    for copy in ps_copies:
        copy.start()

    for copy in d_copies:
        copy.wait_recv()

    def x_face(i, _):
        xs[i] = d[2 * i + 2, 0:32] + d[2 * i + 3, 0:32]
        return 0

    lax.fori_loop(0, 10, x_face, 0, unroll=True)

    def x_pair(i, _):
        both = d[2 * i + 3] + d[2 * i + 4]
        ys[i, 0:8] = both[32:40]
        ys[i, 8:48] = both
        return 0

    lax.fori_loop(0, 8, x_pair, 0, unroll=True)

    lane1 = lanes((4, 16, 128))
    faces_x = 0.125 * pack_pairs(xs[:, pl.ds(0, 16, stride=2), :] + xs[:, pl.ds(1, 16, stride=2), :])
    lx = faces_x[0:4]
    ux = x_up(lx, faces_x[1:5], 2)
    odd_before = ys[:, pl.ds(7, 16, stride=2), :]
    even = ys[:, pl.ds(8, 16, stride=2), :]
    odd = ys[:, pl.ds(9, 16, stride=2), :]
    even_after = ys[:, pl.ds(10, 16, stride=2), :]
    ly = 0.125 * pack_pairs(even + odd_before)
    uy = 0.125 * pack_pairs(odd + even_after)
    both = (even + odd).reshape(4, 2, 16, 128)
    b_even, b_odd = both[:, 0], both[:, 1]
    first, last = lane1 < 2, lane1 >= 126
    zero1 = jnp.zeros((4, 16, 128), jnp.float32)
    is_even = lane1 % 2 == 0
    lz = 0.125 * (
        jnp.where(is_even, b_even, roll_z(b_odd, 1))
        + jnp.where(first, zero1, jnp.where(is_even, roll_z(b_even, 1), roll_z(b_odd, 2)))
    )
    uz = 0.125 * (
        jnp.where(is_even, roll_z(b_even, -1), b_odd)
        + jnp.where(last, zero1, jnp.where(is_even, roll_z(b_even, -2), roll_z(b_odd, -1)))
    )
    diag1 = 0.25 * (lx + ux + ly + uy + lz + uz)
    dg1[...] = diag1 * (1.0 / WEIGHT)
    l1[0, 2:6, 0:16] = lx
    l1[1, 2:6, 0:16] = ly
    l1[2, 2:6, 0:16] = jnp.where(first, zero1, lz)
    l1[3, 2:6, 0:16] = WEIGHT / diag1

    l1_copies = [
        remote(
            l1.at[:, send_range(dx, 2, 4, 2), send_range(dy, 0, 16, 4)],
            l1.at[:, planes_to(dx, 2, 4, 2), rows_to(dy, 16, 4)],
            l1_sem, k, dx, dy,
        )
        for k, (dx, dy) in enumerate(DIRS)
    ]
    for copy in l1_copies:
        copy.start()

    for k, face in enumerate((lx, ux, ly, uy, lz, uz)):
        cs[k] = face

    def rows_of(k, parity):
        return cs[k, :, pl.ds(parity, 8, stride=2), :]

    lane2 = lanes((4, 8, 128))
    zero2 = jnp.zeros((4, 8, 128), jnp.float32)
    lx2 = jnp.where(lane2 % 2 == 0, rows_of(0, 0) + rows_of(0, 1), zero2)
    ux2 = jnp.where(lane2 % 2 == 1, rows_of(1, 0) + rows_of(1, 1), zero2)
    ly2 = rows_of(2, 0)
    uy2 = rows_of(3, 1)
    lz2 = jnp.where(lane2 % 4 < 2, rows_of(4, 0) + rows_of(4, 1), zero2)
    uz2 = jnp.where(lane2 % 4 >= 2, rows_of(5, 0) + rows_of(5, 1), zero2)
    diag2 = (0.0625 * 0.25) * pack_groups(lx2 + ux2 + ly2 + uy2 + lz2 + uz2)
    c2[0, 2, 8:16] = 0.25 * pack_groups(lx2)
    c2[1, 2, 8:16] = 0.25 * pack_groups(ly2)
    c2[2, 2, 8:16] = jnp.where(lanes((8, 128)) < 4, 0.0, 0.25 * pack_groups(lz2))
    c2[3, 2, 8:16] = WEIGHT / diag2

    c2_copies = [
        remote(
            c2.at[:, 2, far_rows(dx, dy, 0)], c2.at[:, 2 - dx, far_rows(dx, dy, -8 * dy)],
            c2_sem, k, dx, dy,
        )
        for k, (dx, dy) in enumerate(FAR)
    ]
    lane0 = lanes((40, 128))
    zero0 = jnp.zeros((40, 128), jnp.float32)

    def fine_weights(i, carry):
        below, here = carry
        above = d[i + 1]
        row_below, row_above = roll_y(here, 1), roll_y(here, -1)
        z_below = jnp.where(lane0 > 0, roll_z(here, 1), zero0)
        z_above = jnp.where(lane0 < 127, roll_z(here, -1), zero0)
        near = (below + above) + (row_below + row_above) + (z_below + z_above)
        diag = 3.0 * here + 0.5 * near
        inv = jnp.where(here > 0.0, WEIGHT / diag, zero0)
        half = 0.5 * inv
        w0[0, i] = half * (here + below)
        w0[1, i] = half * (here + above)
        w0[2, i] = half * (here + row_below)
        w0[3, i] = half * (here + row_above)
        w0[4, i] = jnp.where(lane0 > 0, half * (here + z_below), zero0)
        w0[5, i] = jnp.where(lane0 < 127, half * (here + z_above), zero0)
        g0[i] = inv
        dg0[i] = diag * (1.0 / WEIGHT)
        return here, above

    lax.fori_loop(1, 21, fine_weights, (d[0], d[1]), unroll=True)
    w0[0, 1] = zero0
    w0[1, 20] = zero0

    for copy in ps_copies:
        copy.wait_recv()

    def scale_source(i, _):
        g0[i] = g0[i] * s[i]
        return 0

    lax.fori_loop(1, 21, scale_source, 0, unroll=True)

    def fine_sum(i, below, here, above):
        total = g0[i] + w0[0, i] * below + w0[1, i] * above
        total = total + w0[2, i] * roll_y(here, 1) + w0[3, i] * roll_y(here, -1)
        return total + w0[4, i] * roll_z(here, 1) + w0[5, i] * roll_z(here, -1)

    def fine_sweep(src, dst, low, high):
        def plane(i, carry):
            below, here = carry
            above = src[i + 1]
            dst[i] = fine_sum(i, below, here, above) + KEEP * here
            return here, above

        lax.fori_loop(low, high, plane, (src[low - 1], src[low]), unroll=True)

    fine_sweep(p, v1, 1, 21)
    fine_sweep(v1, v2, 2, 20)

    def residual(pair, carry):
        below, here = carry
        above = v2[2 * pair + 4]
        beyond = v2[2 * pair + 5]
        first_half = (fine_sum(2 * pair + 3, below, here, above) - WEIGHT * here) * dg0[2 * pair + 3]
        second_half = (fine_sum(2 * pair + 4, here, above, beyond) - WEIGHT * above) * dg0[2 * pair + 4]
        xs[pair] = (first_half + second_half)[0:32]
        return above, beyond

    lax.fori_loop(0, 8, residual, (v2[2], v2[3]), unroll=True)
    b1[2:6, 0:16] = 0.125 * pack_pairs(
        xs[0:8, pl.ds(0, 16, stride=2), :] + xs[0:8, pl.ds(1, 16, stride=2), :]
    )
    b1_copies = [
        remote(
            b1.at[send_range(dx, 2, 4, 2), send_range(dy, 0, 16, 4)],
            b1.at[planes_to(dx, 2, 4, 2), rows_to(dy, 16, 4)],
            b1_sem, k, dx, dy,
        )
        for k, (dx, dy) in enumerate(DIRS)
    ]
    f_copies = fine_copies(v2, fh, f_sem, 2)
    for copy in b1_copies + c2_copies:
        copy.start()

    for copy in l1_copies:
        copy.wait_recv()
    inv1 = l1[3]
    coarse_weights(w1, l1, inv1, 2, 0.25)

    for copy in d_copies + ps_copies:
        copy.wait_send()
    for copy in b1_copies:
        copy.wait_recv()
    g1 = l1[3] * b1[...]
    err1 = g1
    err1 = (g1 + KEEP * err1) + coarse_sum(w1, err1, 2)
    res1 = ((g1 - WEIGHT * err1) + coarse_sum(w1, err1, 2))[2:6, 0:16] * dg1[...]
    xs[0:4, 0:16] = res1
    b2[2, 8:16] = 0.125 * pack_groups(
        xs[0:4, pl.ds(0, 8, stride=2), :] + xs[0:4, pl.ds(1, 8, stride=2), :]
    )
    b2_copies = [
        remote(
            b2.at[2, far_rows(dx, dy, 0)], b2.at[2 - dx, far_rows(dx, dy, -8 * dy)],
            b2_sem, k, dx, dy,
        )
        for k, (dx, dy) in enumerate(FAR)
    ]
    for copy in b2_copies + f_copies:
        copy.start()
    for copy in c2_copies:
        copy.wait_recv()
    inv2 = c2[3]
    coarse_weights(w2, c2, inv2, 4, 0.0625)

    for copy in l1_copies + c2_copies + b1_copies:
        copy.wait_send()
    for copy in b2_copies:
        copy.wait_recv()
    g2 = c2[3] * b2[...]
    err2 = g2
    for _ in range(COARSE_SWEEPS - 3):
        err2 = (g2 + KEEP * err2) + coarse_sum(w2, err2, 4)
    w2_middle = [w2[k, 1:4] for k in range(6)]
    g2 = g2[1:4]
    total = weighted_sum(w2_middle, err2[1:4], err2[0:3], err2[2:5], 4)
    err2 = (g2 + KEEP * err2[1:4]) + total
    for _ in range(2):
        err2 = (g2 + KEEP * err2) + coarse_sum(w2_middle, err2, 4)

    row = lax.broadcasted_iota(jnp.int32, (8, 128), 0)

    def put(pair, value):
        centre = value[8:16]
        sides = jnp.where(row < 2, value[16:24], roll_y(value[0:8], 4))
        for parity in range(2):
            e1[pair, pl.ds(parity, 8, stride=2), :] = centre
            e1[pair, pl.ds(16 + parity, 8, stride=2), :] = sides

    before, centre, after = spread_groups(err2[0]), spread_groups(err2[1]), spread_groups(err2[2])
    for pair, value in enumerate(before[2:4] + centre + after[0:2]):
        put(pair, value)
    g1 = l1[3] * b1[...]
    err1 = err1 + e1[:, 0:24]
    for _ in range(POST):
        err1 = (g1 + KEEP * err1) + coarse_sum(w1, err1, 2)

    def put_fine(index, value):
        sides = jnp.where(row < 2, value[16:24], roll_y(value[16:24], 4))
        for parity in range(2):
            e0[index, pl.ds(parity, 16, stride=2), :] = value[0:16]
            e0[index, pl.ds(32 + parity, 8, stride=2), :] = sides

    for pair in range(1, 7):
        even_cell, odd_cell = spread_pairs(err1[pair])
        if pair > 1:
            put_fine(2 * pair - 3, even_cell)
        if pair < 6:
            put_fine(2 * pair - 2, odd_cell)

    for copy in f_copies + b2_copies:
        copy.wait_send()
    for copy in f_copies:
        copy.wait_recv()

    def correct(i, _):
        halves = (2 * i + 1, 2 * i + 2)
        add = e0[i]
        for plane in halves:
            v1[plane, 0:32] = v2[plane, 0:32] + add[0:32]
            v1[plane, 32:40] = fh[plane, 32:40] + add[32:40]
        return 0

    for i in (0, 9):
        for plane in (2 * i + 1, 2 * i + 2):
            v1[plane] = fh[plane] + e0[i, 0:40]
    lax.fori_loop(1, 9, correct, 0, unroll=True)

    fine_sweep(v1, fh, 2, 20)

    def last_sweep(i, carry):
        below, here = carry
        above = fh[i + 1]
        out[i - 3] = (fine_sum(i, below, here, above) + KEEP * here)[0:32]
        return here, above

    carry = (fh[2], fh[3])
    stores = []
    for k, (low, high) in enumerate(((0, 6), (6, 11), (11, 14), (14, 16))):
        carry = lax.fori_loop(low + 3, high + 3, last_sweep, carry, unroll=True)
        part = pl.ds(low, high - low)
        stores.append(pltpu.make_async_copy(out.at[part], o_hbm.at[part], local_sem.at[3 + k]))
        stores[-1].start()
    for store in stores:
        store.wait()


def solution(mesh):
    sizes = (mesh.shape["blk"], mesh.shape["sub"])

    def on_device(pressure, source, inv_density):
        def vmem(*shape):
            return pltpu.VMEM(shape, jnp.float32)

        near, far = len(DIRS), len(FAR)
        return pl.pallas_call(
            functools.partial(kernel, sizes),
            out_shape=jax.ShapeDtypeStruct((16, 32, 128), jnp.float32),
            in_specs=[pl.BlockSpec(memory_space=pltpu.HBM)] * 3,
            out_specs=pl.BlockSpec(memory_space=pl.ANY),
            scratch_shapes=[
                vmem(2, 22, 40, 128), vmem(22, 40, 128), vmem(2, 2, 2, 32, 128),
                vmem(22, 40, 128), vmem(22, 40, 128), vmem(22, 40, 128),
                vmem(16, 32, 128), vmem(6, 22, 40, 128), vmem(22, 40, 128), vmem(22, 40, 128),
                vmem(10, 32, 128), vmem(8, 48, 128), vmem(6, 4, 16, 128),
                vmem(4, 8, 24, 128), vmem(6, 8, 24, 128), vmem(8, 24, 128), vmem(4, 16, 128),
                vmem(4, 5, 24, 128), vmem(6, 5, 24, 128), vmem(5, 24, 128),
                vmem(8, 32, 128), vmem(10, 48, 128),
                pltpu.SemaphoreType.DMA((7,)),
                pltpu.SemaphoreType.DMA((2, near)), pltpu.SemaphoreType.DMA((2, near)),
                pltpu.SemaphoreType.DMA((2, near)), pltpu.SemaphoreType.DMA((2, near)),
                pltpu.SemaphoreType.DMA((2, near)),
                pltpu.SemaphoreType.DMA((2, far)), pltpu.SemaphoreType.DMA((2, far)),
            ],
            compiler_params=pltpu.CompilerParams(
                collective_id=0, has_side_effects=True, vmem_limit_bytes=54850 * 1024
            ),
        )(pressure, source, inv_density)

    return jax.shard_map(
        on_device,
        mesh=mesh,
        in_specs=(P("blk", "sub", None),) * 3,
        out_specs=P("blk", "sub", None),
        check_vma=False,
    )
```

```python
import functools

import jax
import jax.numpy as jnp
from jax import lax
from jax.experimental import pallas as pl
from jax.experimental.pallas import tpu as pltpu
from jax.sharding import PartitionSpec as P

MESH = pl.DeviceIdType.MESH
PRE = 2
POST = 2
COARSE_SWEEPS = 6
WEIGHT = 0.8
KEEP = 1.0 - WEIGHT

DIRS = [(-1, -1), (1, 1), (-1, 1), (1, -1), (-1, 0), (1, 0), (0, -1), (0, 1)]
FAR = [(-2, -1), (2, 1), (-2, 1), (2, -1), (-2, 0), (2, 0)] + DIRS


def send_range(step, first, count, width):
    if step == 0:
        return pl.ds(first, count)
    return pl.ds(first + count - width, width) if step > 0 else pl.ds(first, width)


def planes_to(step, first, count, width):
    if step == 0:
        return pl.ds(first, count)
    return pl.ds(first - width, width) if step > 0 else pl.ds(first + count, width)


def rows_to(step, count, width):
    if step == 0:
        return pl.ds(0, count)
    return pl.ds(count + width, width) if step > 0 else pl.ds(count, width)


def far_rows(dx, dy, shift):
    if abs(dx) + abs(dy) == 3:
        return pl.ds(8 + shift + (4 if dy > 0 else 0), 4)
    return pl.ds(8 + shift, 8)


def lanes(shape):
    return lax.broadcasted_iota(jnp.int32, shape, len(shape) - 1)


def roll_z(value, shift):
    return pltpu.roll(value, shift % 128, value.ndim - 1)


def roll_y(value, shift):
    return pltpu.roll(value, shift % value.shape[-2], value.ndim - 2)


def pack_pairs(value):
    split = value.reshape((value.shape[0] // 2, 2) + value.shape[1:])
    even, odd = split[:, 0], split[:, 1]
    mask = lanes(even.shape) % 2 == 0
    return jnp.where(mask, even + roll_z(even, -1), odd + roll_z(odd, 1))


def pack_groups(value):
    lane = lanes(value.shape[1:])
    low = jnp.where(lane % 2 == 0, value[0] + roll_z(value[0], -1), value[1] + roll_z(value[1], 1))
    high = jnp.where(lane % 2 == 0, value[2] + roll_z(value[2], -1), value[3] + roll_z(value[3], 1))
    return jnp.where(lane % 4 < 2, low + roll_z(low, -2), high + roll_z(high, 2))


def spread_pairs(value):
    mask = lanes(value.shape) % 2 == 0
    return jnp.where(mask, value, roll_z(value, 1)), jnp.where(mask, roll_z(value, -1), value)


def spread_groups(value):
    mask = lanes(value.shape) % 4 < 2
    low = jnp.where(mask, value, roll_z(value, 2))
    high = jnp.where(mask, roll_z(value, -2), value)
    return spread_pairs(low) + spread_pairs(high)


def ahead(value):
    return jnp.concatenate([value[1:], value[:1]], axis=0)


def behind(value):
    return jnp.concatenate([value[-1:], value[:-1]], axis=0)


def x_up(value, following, group):
    mask = lanes(value.shape) % group < group - 1
    return jnp.where(mask, roll_z(value, -1), roll_z(following, group - 1))


def x_down(value, previous, group):
    mask = lanes(value.shape) % group > 0
    return jnp.where(mask, roll_z(value, 1), roll_z(previous, 1 - group))


def coarse_weights(w, faces, inv, group, scale):
    half = scale * inv
    w[0] = half * faces[0]
    w[1] = half * x_up(faces[0], ahead(faces[0]), group)
    w[2] = half * faces[1]
    w[3] = half * roll_y(faces[1], -1)
    w[4] = half * faces[2]
    w[5] = half * roll_z(faces[2], -group)


def coarse_sum(w, value, group):
    return weighted_sum(w, value, behind(value), ahead(value), group)


def weighted_sum(w, value, previous, following, group):
    across = w[0] * x_down(value, previous, group) + w[1] * x_up(value, following, group)
    along = w[2] * roll_y(value, 1) + w[3] * roll_y(value, -1)
    return (along + (w[4] * roll_z(value, group) + w[5] * roll_z(value, -group))) + across


class Halo:
    def __init__(self, copy, sends, receives):
        self.copy, self.sends, self.receives = copy, sends, receives

    def start(self):
        pl.when(self.sends)(self.copy.start)

    def wait_send(self):
        pl.when(self.sends)(self.copy.wait_send)

    def wait_recv(self):
        pl.when(self.receives)(self.copy.wait_recv)


def kernel(
    sizes, p_hbm, s_hbm, d_hbm, o_hbm,
    p, d, s, sx, v1, v2, fh, out, w0, g0, dg0,
    xs, ys, cs, l1, w1, b1, dg1, c2, w2, b2, e1, e0,
    local_sem, d_sem, p_sem, s_sem, f_sem, l1_sem, b1_sem, c2_sem, b2_sem,
):
    n_blk, n_sub = sizes
    ib, iy = lax.axis_index("blk"), lax.axis_index("sub")

    def peer(dx, dy):
        return {"blk": ib + dx, "sub": iy + dy}

    def there(dx, dy):
        known = []
        if dx:
            known.append(ib >= -dx if dx < 0 else ib < n_blk - dx)
        if dy:
            known.append(iy >= -dy if dy < 0 else iy < n_sub - dy)
        return functools.reduce(jnp.logical_and, known)

    def remote(src, dst, sem, k, dx, dy):
        return Halo(
            pltpu.make_async_remote_copy(
                src_ref=src, dst_ref=dst, send_sem=sem.at[0, k], recv_sem=sem.at[1, k],
                device_id=peer(dx, dy), device_id_type=MESH,
            ),
            there(dx, dy),
            there(-dx, -dy),
        )

    def clear_outside(ref, lead, x_side, x_count, rows, low_rows, high_rows):
        planes = x_count + 2 * x_side
        slab = jnp.zeros(lead + (x_side, rows, 128), jnp.float32)
        strip = jnp.zeros(lead + (planes, low_rows[1], 128), jnp.float32)
        every = (slice(None),) * len(lead)

        @pl.when(ib == 0)
        def _():
            ref[every + (slice(0, x_side),)] = slab

        @pl.when(ib == n_blk - 1)
        def _():
            ref[every + (slice(x_side + x_count, planes),)] = slab

        @pl.when(iy == 0)
        def _():
            ref[every + (slice(None), slice(low_rows[0], low_rows[0] + low_rows[1]))] = strip

        @pl.when(iy == n_sub - 1)
        def _():
            ref[every + (slice(None), slice(high_rows[0], high_rows[0] + high_rows[1]))] = strip

    barrier = pltpu.get_barrier_semaphore()
    for dx, dy in DIRS:
        @pl.when(there(dx, dy))
        def _():
            pl.semaphore_signal(barrier, inc=1, device_id=peer(dx, dy), device_id_type=MESH)

    local = [
        pltpu.make_async_copy(src, dst.at[pl.ds(3, 16), pl.ds(0, 32)], local_sem.at[k])
        for k, (src, dst) in enumerate(((d_hbm, d), (p_hbm, p), (s_hbm, s)))
    ]
    for copy in local:
        copy.start()
    for ref in (d, p, s, fh):
        clear_outside(ref, (), 3, 16, 40, (36, 4), (32, 4))
    clear_outside(l1, (4,), 2, 4, 24, (20, 4), (16, 4))
    clear_outside(b1, (), 2, 4, 24, (20, 4), (16, 4))
    for index in (0, 1, 3, 4):
        @pl.when((ib + (index - 2) < 0) | (ib + (index - 2) >= n_blk))
        def _():
            c2[:, index] = jnp.zeros((4, 24, 128), jnp.float32)
            b2[index] = jnp.zeros((24, 128), jnp.float32)

    for edge, first in ((0, 0), (n_sub - 1, 16)):
        @pl.when(iy == edge)
        def _():
            c2[:, :, first:first + 8] = jnp.zeros((4, 5, 8, 128), jnp.float32)
            b2[:, first:first + 8] = jnp.zeros((5, 8, 128), jnp.float32)

    for copy in local:
        copy.wait()
    def joined(plane, beyond):
        face = 0.5 * (d[plane, 0:32] + d[beyond, 0:32])
        return s[plane, 0:32] + face * p[beyond, 0:32]

    sx[0, 0] = s[3, 0:32]
    sx[0, 1] = joined(4, 5)
    sx[1, 0] = joined(17, 16)
    sx[1, 1] = s[18, 0:32]
    p[0] = jnp.zeros((40, 128), jnp.float32)
    p[21] = jnp.zeros((40, 128), jnp.float32)

    across = 1 + (ib > 0).astype(jnp.int32) + (ib < n_blk - 1).astype(jnp.int32)
    along = 1 + (iy > 0).astype(jnp.int32) + (iy < n_sub - 1).astype(jnp.int32)
    pl.semaphore_wait(barrier, across * along - 1)

    def fine_copies(src, dst, sem, width, sides=None):
        copies = []
        for k, (dx, dy) in enumerate(DIRS):
            count = min(width - abs(dy), 2) if src is p else width - abs(dy)
            if sides is not None and dy == 0:
                block = sides.at[0 if dx < 0 else 1]
            else:
                block = src.at[send_range(dx, 3, 16, count), send_range(dy, 0, 32, 4)]
            target = dst.at[planes_to(dx, 3, 16, count), rows_to(dy, 32, 4)]
            copies.append(remote(block, target, sem, k, dx, dy))
        return copies

    d_copies = fine_copies(d, d, d_sem, 3)
    p_copies = fine_copies(p, p, p_sem, 3)
    s_copies = fine_copies(s, s, s_sem, 2, sx)
    for copy in d_copies + p_copies + s_copies:
        copy.start()

    for copy in d_copies:
        copy.wait_recv()

    def x_face(i, _):
        xs[i] = d[2 * i + 2, 0:32] + d[2 * i + 3, 0:32]
        return 0

    lax.fori_loop(0, 10, x_face, 0, unroll=True)

    def x_pair(i, _):
        both = d[2 * i + 3] + d[2 * i + 4]
        ys[i, 0:8] = both[32:40]
        ys[i, 8:48] = both
        return 0

    lax.fori_loop(0, 8, x_pair, 0, unroll=True)

    lane1 = lanes((4, 16, 128))
    faces_x = 0.125 * pack_pairs(xs[:, pl.ds(0, 16, stride=2), :] + xs[:, pl.ds(1, 16, stride=2), :])
    lx = faces_x[0:4]
    ux = x_up(lx, faces_x[1:5], 2)
    odd_before = ys[:, pl.ds(7, 16, stride=2), :]
    even = ys[:, pl.ds(8, 16, stride=2), :]
    odd = ys[:, pl.ds(9, 16, stride=2), :]
    even_after = ys[:, pl.ds(10, 16, stride=2), :]
    ly = 0.125 * pack_pairs(even + odd_before)
    uy = 0.125 * pack_pairs(odd + even_after)
    both = (even + odd).reshape(4, 2, 16, 128)
    b_even, b_odd = both[:, 0], both[:, 1]
    first, last = lane1 < 2, lane1 >= 126
    zero1 = jnp.zeros((4, 16, 128), jnp.float32)
    is_even = lane1 % 2 == 0
    lz = 0.125 * (
        jnp.where(is_even, b_even, roll_z(b_odd, 1))
        + jnp.where(first, zero1, jnp.where(is_even, roll_z(b_even, 1), roll_z(b_odd, 2)))
    )
    uz = 0.125 * (
        jnp.where(is_even, roll_z(b_even, -1), b_odd)
        + jnp.where(last, zero1, jnp.where(is_even, roll_z(b_even, -2), roll_z(b_odd, -1)))
    )
    diag1 = 0.25 * (lx + ux + ly + uy + lz + uz)
    dg1[...] = diag1 * (1.0 / WEIGHT)
    l1[0, 2:6, 0:16] = lx
    l1[1, 2:6, 0:16] = ly
    l1[2, 2:6, 0:16] = jnp.where(first, zero1, lz)
    l1[3, 2:6, 0:16] = WEIGHT / diag1

    l1_copies = [
        remote(
            l1.at[:, send_range(dx, 2, 4, 2), send_range(dy, 0, 16, 4)],
            l1.at[:, planes_to(dx, 2, 4, 2), rows_to(dy, 16, 4)],
            l1_sem, k, dx, dy,
        )
        for k, (dx, dy) in enumerate(DIRS)
    ]
    for copy in l1_copies:
        copy.start()

    for k, face in enumerate((lx, ux, ly, uy, lz, uz)):
        cs[k] = face

    def rows_of(k, parity):
        return cs[k, :, pl.ds(parity, 8, stride=2), :]

    lane2 = lanes((4, 8, 128))
    zero2 = jnp.zeros((4, 8, 128), jnp.float32)
    lx2 = jnp.where(lane2 % 2 == 0, rows_of(0, 0) + rows_of(0, 1), zero2)
    ux2 = jnp.where(lane2 % 2 == 1, rows_of(1, 0) + rows_of(1, 1), zero2)
    ly2 = rows_of(2, 0)
    uy2 = rows_of(3, 1)
    lz2 = jnp.where(lane2 % 4 < 2, rows_of(4, 0) + rows_of(4, 1), zero2)
    uz2 = jnp.where(lane2 % 4 >= 2, rows_of(5, 0) + rows_of(5, 1), zero2)
    diag2 = (0.0625 * 0.25) * pack_groups(lx2 + ux2 + ly2 + uy2 + lz2 + uz2)
    c2[0, 2, 8:16] = 0.25 * pack_groups(lx2)
    c2[1, 2, 8:16] = 0.25 * pack_groups(ly2)
    c2[2, 2, 8:16] = jnp.where(lanes((8, 128)) < 4, 0.0, 0.25 * pack_groups(lz2))
    c2[3, 2, 8:16] = WEIGHT / diag2

    c2_copies = [
        remote(
            c2.at[:, 2, far_rows(dx, dy, 0)], c2.at[:, 2 - dx, far_rows(dx, dy, -8 * dy)],
            c2_sem, k, dx, dy,
        )
        for k, (dx, dy) in enumerate(FAR)
    ]
    lane0 = lanes((40, 128))
    zero0 = jnp.zeros((40, 128), jnp.float32)

    def fine_weights(i, carry):
        below, here = carry
        above = d[i + 1]
        row_below, row_above = roll_y(here, 1), roll_y(here, -1)
        z_below = jnp.where(lane0 > 0, roll_z(here, 1), zero0)
        z_above = jnp.where(lane0 < 127, roll_z(here, -1), zero0)
        near = (below + above) + (row_below + row_above) + (z_below + z_above)
        diag = 3.0 * here + 0.5 * near
        inv = jnp.where(here > 0.0, WEIGHT / diag, zero0)
        half = 0.5 * inv
        w0[0, i] = half * (here + below)
        w0[1, i] = half * (here + above)
        w0[2, i] = half * (here + row_below)
        w0[3, i] = half * (here + row_above)
        w0[4, i] = jnp.where(lane0 > 0, half * (here + z_below), zero0)
        w0[5, i] = jnp.where(lane0 < 127, half * (here + z_above), zero0)
        g0[i] = inv
        dg0[i] = diag * (1.0 / WEIGHT)
        return here, above

    lax.fori_loop(1, 21, fine_weights, (d[0], d[1]), unroll=True)
    w0[0, 1] = zero0
    w0[1, 20] = zero0

    for copy in p_copies + s_copies:
        copy.wait_recv()

    def scale_source(i, _):
        g0[i] = g0[i] * s[i]
        return 0

    lax.fori_loop(1, 21, scale_source, 0, unroll=True)

    def fine_sum(i, below, here, above):
        total = g0[i] + w0[0, i] * below + w0[1, i] * above
        total = total + w0[2, i] * roll_y(here, 1) + w0[3, i] * roll_y(here, -1)
        return total + w0[4, i] * roll_z(here, 1) + w0[5, i] * roll_z(here, -1)

    def fine_sweep(src, dst, low, high):
        def plane(i, carry):
            below, here = carry
            above = src[i + 1]
            dst[i] = fine_sum(i, below, here, above) + KEEP * here
            return here, above

        lax.fori_loop(low, high, plane, (src[low - 1], src[low]), unroll=True)

    fine_sweep(p, v1, 1, 21)
    fine_sweep(v1, v2, 2, 20)

    def residual(pair, carry):
        below, here = carry
        above = v2[2 * pair + 4]
        beyond = v2[2 * pair + 5]
        first_half = (fine_sum(2 * pair + 3, below, here, above) - WEIGHT * here) * dg0[2 * pair + 3]
        second_half = (fine_sum(2 * pair + 4, here, above, beyond) - WEIGHT * above) * dg0[2 * pair + 4]
        xs[pair] = (first_half + second_half)[0:32]
        return above, beyond

    lax.fori_loop(0, 8, residual, (v2[2], v2[3]), unroll=True)
    b1[2:6, 0:16] = 0.125 * pack_pairs(
        xs[0:8, pl.ds(0, 16, stride=2), :] + xs[0:8, pl.ds(1, 16, stride=2), :]
    )
    b1_copies = [
        remote(
            b1.at[send_range(dx, 2, 4, 2), send_range(dy, 0, 16, 4)],
            b1.at[planes_to(dx, 2, 4, 2), rows_to(dy, 16, 4)],
            b1_sem, k, dx, dy,
        )
        for k, (dx, dy) in enumerate(DIRS)
    ]
    f_copies = fine_copies(v2, fh, f_sem, 2)
    for copy in b1_copies + c2_copies + f_copies:
        copy.start()

    for copy in l1_copies:
        copy.wait_recv()
    inv1 = l1[3]
    coarse_weights(w1, l1, inv1, 2, 0.25)

    for copy in d_copies + p_copies + s_copies:
        copy.wait_send()
    for copy in b1_copies:
        copy.wait_recv()
    g1 = l1[3] * b1[...]
    err1 = g1
    err1 = (g1 + KEEP * err1) + coarse_sum(w1, err1, 2)
    res1 = ((g1 - WEIGHT * err1) + coarse_sum(w1, err1, 2))[2:6, 0:16] * dg1[...]
    xs[0:4, 0:16] = res1
    b2[2, 8:16] = 0.125 * pack_groups(
        xs[0:4, pl.ds(0, 8, stride=2), :] + xs[0:4, pl.ds(1, 8, stride=2), :]
    )
    b2_copies = [
        remote(
            b2.at[2, far_rows(dx, dy, 0)], b2.at[2 - dx, far_rows(dx, dy, -8 * dy)],
            b2_sem, k, dx, dy,
        )
        for k, (dx, dy) in enumerate(FAR)
    ]
    for copy in b2_copies:
        copy.start()
    for copy in c2_copies:
        copy.wait_recv()
    inv2 = c2[3]
    coarse_weights(w2, c2, inv2, 4, 0.0625)

    for copy in l1_copies + c2_copies + b1_copies:
        copy.wait_send()
    for copy in b2_copies:
        copy.wait_recv()
    g2 = c2[3] * b2[...]
    err2 = g2
    for _ in range(COARSE_SWEEPS - 3):
        err2 = (g2 + KEEP * err2) + coarse_sum(w2, err2, 4)
    w2_middle = [w2[k, 1:4] for k in range(6)]
    g2 = g2[1:4]
    total = weighted_sum(w2_middle, err2[1:4], err2[0:3], err2[2:5], 4)
    err2 = (g2 + KEEP * err2[1:4]) + total
    for _ in range(2):
        err2 = (g2 + KEEP * err2) + coarse_sum(w2_middle, err2, 4)

    row = lax.broadcasted_iota(jnp.int32, (8, 128), 0)

    def put(pair, value):
        centre = value[8:16]
        sides = jnp.where(row < 2, value[16:24], roll_y(value[0:8], 4))
        for parity in range(2):
            e1[pair, pl.ds(parity, 8, stride=2), :] = centre
            e1[pair, pl.ds(16 + parity, 8, stride=2), :] = sides

    before, centre, after = spread_groups(err2[0]), spread_groups(err2[1]), spread_groups(err2[2])
    for pair, value in enumerate(before[2:4] + centre + after[0:2]):
        put(pair, value)
    g1 = l1[3] * b1[...]
    err1 = err1 + e1[:, 0:24]
    for _ in range(POST):
        err1 = (g1 + KEEP * err1) + coarse_sum(w1, err1, 2)

    def put_fine(index, value):
        sides = jnp.where(row < 2, value[16:24], roll_y(value[16:24], 4))
        for parity in range(2):
            e0[index, pl.ds(parity, 16, stride=2), :] = value[0:16]
            e0[index, pl.ds(32 + parity, 8, stride=2), :] = sides

    for pair in range(1, 7):
        even_cell, odd_cell = spread_pairs(err1[pair])
        if pair > 1:
            put_fine(2 * pair - 3, even_cell)
        if pair < 6:
            put_fine(2 * pair - 2, odd_cell)

    for copy in f_copies + b2_copies:
        copy.wait_send()
    for copy in f_copies:
        copy.wait_recv()

    def correct(i, _):
        halves = (2 * i + 1, 2 * i + 2)
        add = e0[i]
        for plane in halves:
            v1[plane, 0:32] = v2[plane, 0:32] + add[0:32]
            v1[plane, 32:40] = fh[plane, 32:40] + add[32:40]
        return 0

    for i in (0, 9):
        for plane in (2 * i + 1, 2 * i + 2):
            v1[plane] = fh[plane] + e0[i, 0:40]
    lax.fori_loop(1, 9, correct, 0, unroll=True)

    fine_sweep(v1, fh, 2, 20)

    def last_sweep(i, carry):
        below, here = carry
        above = fh[i + 1]
        out[i - 3] = (fine_sum(i, below, here, above) + KEEP * here)[0:32]
        return here, above

    carry = (fh[2], fh[3])
    stores = []
    for k in range(4):
        carry = lax.fori_loop(4 * k + 3, 4 * k + 7, last_sweep, carry, unroll=True)
        part = pl.ds(4 * k, 4)
        stores.append(pltpu.make_async_copy(out.at[part], o_hbm.at[part], local_sem.at[3 + k]))
        stores[-1].start()
    for store in stores:
        store.wait()


def solution(mesh):
    sizes = (mesh.shape["blk"], mesh.shape["sub"])

    def on_device(pressure, source, inv_density):
        def vmem(*shape):
            return pltpu.VMEM(shape, jnp.float32)

        near, far = len(DIRS), len(FAR)
        return pl.pallas_call(
            functools.partial(kernel, sizes),
            out_shape=jax.ShapeDtypeStruct((16, 32, 128), jnp.float32),
            in_specs=[pl.BlockSpec(memory_space=pltpu.HBM)] * 3,
            out_specs=pl.BlockSpec(memory_space=pl.ANY),
            scratch_shapes=[
                vmem(22, 40, 128), vmem(22, 40, 128), vmem(22, 40, 128), vmem(2, 2, 32, 128),
                vmem(22, 40, 128), vmem(22, 40, 128), vmem(22, 40, 128),
                vmem(16, 32, 128), vmem(6, 22, 40, 128), vmem(22, 40, 128), vmem(22, 40, 128),
                vmem(10, 32, 128), vmem(8, 48, 128), vmem(6, 4, 16, 128),
                vmem(4, 8, 24, 128), vmem(6, 8, 24, 128), vmem(8, 24, 128), vmem(4, 16, 128),
                vmem(4, 5, 24, 128), vmem(6, 5, 24, 128), vmem(5, 24, 128),
                vmem(8, 32, 128), vmem(10, 48, 128),
                pltpu.SemaphoreType.DMA((7,)),
                pltpu.SemaphoreType.DMA((2, near)), pltpu.SemaphoreType.DMA((2, near)),
                pltpu.SemaphoreType.DMA((2, near)), pltpu.SemaphoreType.DMA((2, near)),
                pltpu.SemaphoreType.DMA((2, near)), pltpu.SemaphoreType.DMA((2, near)),
                pltpu.SemaphoreType.DMA((2, far)), pltpu.SemaphoreType.DMA((2, far)),
            ],
            compiler_params=pltpu.CompilerParams(
                collective_id=0, has_side_effects=True, vmem_limit_bytes=54850 * 1024
            ),
        )(pressure, source, inv_density)

    return jax.shard_map(
        on_device,
        mesh=mesh,
        in_specs=(P("blk", "sub", None),) * 3,
        out_specs=P("blk", "sub", None),
        check_vma=False,
    )
```
